256 devices in a mesh: gx: 4 (over x_lo, core), gy: 8 (over z), gz: 8 (over x_hi, y).
Axes of the slice: x: 4 (x_hi: 2, x_lo: 2; x = x_hi * 2 + x_lo), y: 4, z: 8, core: 2. Of those that a mesh axis runs over, the one named last changes fastest.
Arguments:
- atom_types: int32 [32768], P(('gx', 'gy', 'gz')), may hold values from 0 to 5
- type_table: bfloat16 [6, 128], replicated, may hold values from -6 to 6
- neighbor_index: int32 [32768, 48], P(('gx', 'gy', 'gz')), may hold values from 0 to 447
- neighbor_count: int32 [32768], P(('gx', 'gy', 'gz')), may hold values from 24 to 48
- displacement: float32 [3, 32768, 48], P(None, ('gx', 'gy', 'gz')), as said below
- send_x: int32 [2, 8192], P(None, ('gx', 'gy', 'gz')), may hold values from 0 to 127
- send_y: int32 [2, 16384], P(None, ('gx', 'gy', 'gz')), may hold values from 0 to 191
- send_z: int32 [2, 16384], P(None, ('gx', 'gy', 'gz')), may hold values from 0 to 319
- message_weight: bfloat16 [3, 128, 128], replicated, may hold values from -0.5 to 0.5
- self_weight: bfloat16 [3, 128, 128], replicated, may hold values from -0.5 to 0.5
- decay: float32 [3, 128], replicated, may hold values from 0.05 to 1.5
- energy_proj: bfloat16 [128, 128], replicated, may hold values from -0.5 to 0.5
- energy_out: float32 [128], replicated, may hold values from -0.5 to 0.5
Outputs:
- atom_energy: float32 [32768], P(('gx', 'gy', 'gz'))
- forces: float32 [3, 32768], P(None, ('gx', 'gy', 'gz'))
The draws below stay inside these ranges and needn't reach their ends.
Inputs may be any that keep to these rules, and one draw needn't show every extreme that they name: `neighbor_index`: within a domain's extended rows, rows 0 to 127 are its own atoms, then 32 rows from the lower and 32 from the higher gx neighbour, then likewise 64 and 64 along gy, then 64 and 64 along gz. `send_x`: each domain's block indexes its own atoms. `send_y`: each domain's block indexes its own atoms and the gx ghost rows. `send_z`: each domain's block indexes its own atoms and the gx and gy ghost rows. Every displacement has a length between 0.9 and 3.9.
All inputs are finite; a program needn't handle non-finite values.
Results may differ from the reference program's by a relative error of at most 0.012.
Values may be sent and summed in bfloat16 or wider, within the bound.
No kernel may reach another device: no remote copies, remote signals or barrier semaphores. Data moves between devices by JAX's collectives and lax.ppermute only.
A program may use at most 64 MiB of HBM per device.

```python
import math
import jax
import jax.numpy as jnp
from jax import lax

C = 128
NNEI = 48
TYPES = 6
LAYERS = 3
ATOMS = 128
GX = 32
GY = 64
GZ = 64
EXTENDED = 448
NTOT = 32768
N_GX = 4
N_GY = 8
N_GZ = 8


def draw_displacement(key, part):
    key = jax.random.fold_in(key, 11)
    subkeys = jax.random.split(key, 3)
    extent = (NTOT, NNEI)
    radius = jax.random.uniform(subkeys[0], extent, jnp.float32, 0.9, 3.9)
    height = jax.random.uniform(subkeys[1], extent, jnp.float32, -1.0, 1.0)
    azimuth = jax.random.uniform(subkeys[2], extent, jnp.float32, -math.pi, math.pi)
    planar = jnp.sqrt(jnp.maximum(1.0 - height * height, 0.0))
    return jnp.stack([radius * planar * jnp.cos(azimuth), radius * planar * jnp.sin(azimuth), radius * height])


def with_ends(drawn, rng, low, largest):
    longest = drawn.shape.index(max(drawn.shape))
    spots = []
    for shift in (0, 1):
        where = [jax.random.randint(jax.random.fold_in(rng, axis), (), 0, length) for axis, length in enumerate(drawn.shape)]
        where[longest] = (where[longest] + shift) % drawn.shape[longest]
        spots.append(tuple(where))
    return drawn.at[spots[0]].set(low).at[spots[1]].set(largest)


def normal_values(own_key, dims, scale, reach, held_as=jnp.bfloat16):
    array = scale * jax.random.normal(own_key, dims, jnp.float32)
    return jnp.clip(array, min=-reach, max=reach).astype(held_as)


def setup_inputs(seed: int = 0) -> dict:
    key_list = jax.random.split(jax.random.key(seed), 14)
    return {
        "atom_types": with_ends(jax.random.randint(key_list[0], (NTOT,), 0, TYPES), jax.random.fold_in(key_list[0], 1), 0, TYPES - 1).astype(jnp.int32),
        "type_table": normal_values(key_list[1], (TYPES, C), 1.0, 6.0),
        "neighbor_index": with_ends(jax.random.randint(key_list[2], (NTOT, NNEI), 0, EXTENDED), jax.random.fold_in(key_list[2], 1), 0, EXTENDED - 1).astype(jnp.int32),
        "neighbor_count": with_ends(jax.random.randint(key_list[3], (NTOT,), NNEI // 2, NNEI + 1), jax.random.fold_in(key_list[3], 1), NNEI // 2, NNEI).astype(jnp.int32),
        "displacement": draw_displacement(jax.random.fold_in(key_list[13], 71), 0),
        "send_x": with_ends(jax.random.randint(key_list[5], (2, N_GX * N_GY * N_GZ * GX), 0, ATOMS), jax.random.fold_in(key_list[5], 1), 0, ATOMS - 1).astype(jnp.int32),
        "send_y": with_ends(jax.random.randint(key_list[6], (2, N_GX * N_GY * N_GZ * GY), 0, ATOMS + 2 * GX), jax.random.fold_in(key_list[6], 1), 0, (ATOMS + 2 * GX) - 1).astype(jnp.int32),
        "send_z": with_ends(jax.random.randint(key_list[7], (2, N_GX * N_GY * N_GZ * GZ), 0, ATOMS + 2 * GX + 2 * GY), jax.random.fold_in(key_list[7], 1), 0, (ATOMS + 2 * GX + 2 * GY) - 1).astype(jnp.int32),
        "message_weight": normal_values(key_list[8], (LAYERS, C, C), C ** -0.5, 0.5),
        "self_weight": normal_values(key_list[9], (LAYERS, C, C), C ** -0.5, 0.5),
        "decay": jnp.clip(jnp.exp(jax.random.uniform(key_list[10], (LAYERS, C), jnp.float32, math.log(0.05), math.log(1.5))), 0.05, 1.5),
        "energy_proj": normal_values(key_list[11], (C, C), C ** -0.5, 0.5),
        "energy_out": normal_values(key_list[12], (C,), C ** -0.5, 0.5, jnp.float32),
    }


cutoff = 4.0

def filters(delta, counts, decay_row):
    slot_index = lax.broadcasted_iota(jnp.int32, delta.shape[1:], 1)
    alive_mask = (slot_index < counts[:, None]).astype(jnp.float32)
    radius = jnp.sqrt(delta[0] * delta[0] + delta[1] * delta[1] + delta[2] * delta[2])
    angle_arg = math.pi / cutoff * radius
    switch = 0.5 * (jnp.cos(angle_arg) + 1.0)
    dswitch = -0.5 * (math.pi / cutoff) * jnp.sin(angle_arg)
    radial_base = alive_mask * switch / radius
    radial_slope = alive_mask * (dswitch / radius - switch / (radius * radius))
    decayed = jnp.exp(-decay_row * radius[:, :, None])
    weight = radial_base[:, :, None] * decayed
    weight_slope = (radial_slope[:, :, None] - decay_row * radial_base[:, :, None]) * decayed
    return (radius, weight, weight_slope)

def aggregate(table, neighbor_index, neighbor_count, displacement, decay_row, block_rows):
    atom_count, slots = neighbor_index.shape
    n_blocks = atom_count // block_rows
    norm_factor = 1.0 / math.sqrt(slots)

    def per_block(inputs):
        neighbor, delta, counts = inputs
        radius, weight, weight_slope = filters(delta, counts, decay_row)
        gathered = table[neighbor]
        return norm_factor * lax.optimization_barrier(jnp.sum(weight * gathered, axis=1))
    inputs = (neighbor_index.reshape(n_blocks, block_rows, slots), jnp.moveaxis(displacement.reshape(3, n_blocks, block_rows, slots), 1, 0), neighbor_count.reshape(n_blocks, block_rows))
    return lax.map(per_block, inputs).reshape(atom_count, table.shape[1])

def backward_block(table, upstream, neighbor_index, neighbor_count, displacement, decay_row, block_rows):
    atom_count, slots = neighbor_index.shape
    channels = table.shape[1]
    n_blocks = atom_count // block_rows
    norm_factor = 1.0 / math.sqrt(slots)

    def per_block(state_pair, inputs):
        proj_grad, pushed = state_pair
        neighbor, delta, counts, upstream_rows = inputs
        radius, weight, weight_slope = filters(delta, counts, decay_row)
        gathered = table[neighbor]
        radius_grad = norm_factor * lax.optimization_barrier(jnp.sum(upstream_rows[:, None, :] * gathered * weight_slope, axis=2))
        disp_grad = radius_grad[None] * delta / radius[None]
        flat_rows = neighbor.reshape(-1)
        proj_grad = proj_grad.at[flat_rows].add((norm_factor * weight * upstream_rows[:, None, :]).reshape(-1, channels))
        pushed = pushed.at[:, flat_rows].add(disp_grad.reshape(3, -1))
        return ((proj_grad, pushed), lax.optimization_barrier(jnp.sum(disp_grad, axis=2)))
    start = (jnp.zeros((table.shape[0], channels), jnp.float32), jnp.zeros((3, table.shape[0]), jnp.float32))
    inputs = (neighbor_index.reshape(n_blocks, block_rows, slots), jnp.moveaxis(displacement.reshape(3, n_blocks, block_rows, slots), 1, 0), neighbor_count.reshape(n_blocks, block_rows), upstream.reshape(n_blocks, block_rows, channels))
    (proj_grad, pushed), own_parts = lax.scan(per_block, start, inputs)
    return (proj_grad, pushed, jnp.moveaxis(own_parts, 0, 1).reshape(3, atom_count))

def extended_ids(send_x, send_y, send_z):
    domains = N_GX * N_GY * N_GZ
    row_ids = jnp.arange(domains * ATOMS, dtype=jnp.int32).reshape(N_GX, N_GY, N_GZ, ATOMS)
    for dim_index, send_lists in ((0, send_x), (1, send_y), (2, send_z)):
        lists_grid = send_lists.reshape(2, N_GX, N_GY, N_GZ, -1)
        upward = jnp.take_along_axis(row_ids, lists_grid[0], axis=3)
        downward = jnp.take_along_axis(row_ids, lists_grid[1], axis=3)
        row_ids = jnp.concatenate([row_ids, jnp.roll(upward, 1, axis=dim_index), jnp.roll(downward, -1, axis=dim_index)], axis=3)
    return row_ids.reshape(domains, EXTENDED)

def reference(atom_types, type_table, neighbor_index, neighbor_count, displacement, send_x, send_y, send_z, message_weight, self_weight, decay, energy_proj, energy_out):
    domains = N_GX * N_GY * N_GZ
    ext_ids = extended_ids(send_x, send_y, send_z)
    neighbor_rows = jax.vmap(lambda table_row, slot_rows: table_row[slot_rows])(ext_ids, neighbor_index.reshape(domains, ATOMS, NNEI)).reshape(domains * ATOMS, NNEI)
    onehot = (atom_types[:, None] == jnp.arange(TYPES, dtype=jnp.int32)[None, :]).astype(jnp.bfloat16)
    features = jnp.dot(onehot, type_table, preferred_element_type=jnp.float32).astype(jnp.bfloat16)
    stored = []
    for layer_index in range(LAYERS):
        projected = jnp.dot(features, message_weight[layer_index], preferred_element_type=jnp.float32).astype(jnp.bfloat16)
        self_term = jnp.dot(features, self_weight[layer_index], preferred_element_type=jnp.float32)
        preact = aggregate(projected, neighbor_rows, neighbor_count, displacement, decay[layer_index], ATOMS) + self_term
        stored.append((projected, preact))
        features = (features.astype(jnp.float32) + jnp.tanh(preact)).astype(jnp.bfloat16)
    readout = jnp.tanh(jnp.dot(features, energy_proj, preferred_element_type=jnp.float32))
    atom_energy = lax.optimization_barrier(jnp.sum(readout * energy_out, axis=1))
    gradient = jnp.dot((1.0 - readout * readout) * energy_out, energy_proj.astype(jnp.float32).T, precision=lax.Precision.HIGHEST)
    own_force = jnp.zeros((3, domains * ATOMS), jnp.float32)
    pushed_total = jnp.zeros((3, domains * ATOMS), jnp.float32)
    for layer_index in reversed(range(LAYERS)):
        projected, preact = stored[layer_index]
        activation = jnp.tanh(preact)
        preact_grad = gradient * (1.0 - activation * activation)
        proj_grad, pushed, own_part = backward_block(projected, preact_grad, neighbor_rows, neighbor_count, displacement, decay[layer_index], ATOMS)
        own_force = own_force + own_part
        pushed_total = pushed_total + pushed
        if layer_index > 0:
            gradient = gradient + jnp.dot(preact_grad, self_weight[layer_index].astype(jnp.float32).T, precision=lax.Precision.HIGHEST) + jnp.dot(proj_grad, message_weight[layer_index].astype(jnp.float32).T, precision=lax.Precision.HIGHEST)
    forces = own_force - pushed_total
    return (atom_energy, forces)
```

```python
import math

import jax
import jax.numpy as jnp
from jax import lax
from jax.experimental import pallas as pl
from jax.experimental.pallas import tpu as pltpu
from jax.sharding import PartitionSpec as P

cutoff = 4.0
ATOMS = 128
C = 128
SLOTS = 48
GX, GY, GZ = 32, 64, 64
OFF_X, OFF_Y, OFF_Z, ROWS = 128, 256, 384, 512
PAD = 64
UNPADDED = ATOMS + 2 * GX
PAIRS = ATOMS * SLOTS
CHUNK = 256
f32, bf16, i32 = jnp.float32, jnp.bfloat16, jnp.int32
NT = (((1,), (1,)), ((), ()))
VMEM_LIMIT = 56 * 1024 * 1024


def shape(dims, dtype):
    return jax.ShapeDtypeStruct(dims, dtype)


def call(body, outs, scratch=()):
    return pl.pallas_call(
        body,
        out_shape=outs,
        scratch_shapes=list(scratch),
        compiler_params=pltpu.CompilerParams(vmem_limit_bytes=VMEM_LIMIT),
    )


def along(axis, distance):
    size = lax.axis_size(axis)
    return [(i, (i + distance) % size) for i in range(size)]


def swap(to_higher, to_lower, axis):
    from_lower = lax.ppermute(to_higher, axis, along(axis, 1))
    from_higher = lax.ppermute(to_lower, axis, along(axis, -1))
    return from_lower, from_higher


def mm(a, b):
    return jnp.dot(a, b, preferred_element_type=f32)


def mm_nt(a, b):
    return lax.dot_general(a, b, NT, preferred_element_type=f32)


def split_nt(a, b):
    high = a.astype(bf16)
    low = (a - high.astype(f32)).astype(bf16)
    return mm_nt(high, b) + mm_nt(low, b)


def columns(row):
    return jnp.broadcast_to(row, (128, row.shape[1])).T


def padded(ids):
    return jnp.where(ids >= UNPADDED, ids + PAD, ids)


def picker(row, extent):
    ids = columns(row.astype(f32))
    parts = []
    for start in range(0, extent, 128):
        lane = (lax.broadcasted_iota(i32, ids.shape, 1) + start).astype(f32)
        parts.append(jnp.where(ids == lane, 1.0, 0.0).astype(bf16))
    return jnp.concatenate(parts, axis=1) if len(parts) > 1 else parts[0]


def placer(row, extent):
    sub = lax.broadcasted_iota(i32, (extent, row.shape[1]), 0)
    return jnp.where(sub == row, 1.0, 0.0).astype(bf16)


def first_kernel(types, table, weight, send_x, feat, proj, up, down, pick_x, place_x, rows):
    rows[...] = jnp.zeros_like(rows)
    rows[0:6, :] = table[...].astype(f32)
    kinds = columns(types[...].astype(f32))
    lane = lax.broadcasted_iota(i32, (ATOMS, 128), 1).astype(f32)
    onehot = jnp.where(kinds == lane, 1.0, 0.0).astype(bf16)
    features = mm(onehot, rows[...].astype(bf16)).astype(bf16)
    projected = mm(features, weight[0]).astype(bf16)
    feat[...] = features
    proj[...] = projected
    pick = picker(send_x[...], ATOMS)
    place_x[...] = placer(send_x[...], ATOMS)
    pick_x[...] = pick
    chosen = mm(pick, projected).astype(bf16)
    up[...] = chosen[0:GX]
    down[...] = chosen[GX:]


def lists_kernel(send_y, send_z, pick_y, pick_z, place_y, place_z):
    ids_y, ids_z = send_y[...], padded(send_z[...])
    pick_y[...] = picker(ids_y, OFF_Y)
    pick_z[...] = picker(ids_z, OFF_Z)
    place_y[...] = placer(ids_y, UNPADDED)
    place_z[...] = placer(ids_z, OFF_Z)


def weights_kernel(index, count, delta, decay, onehot, w0, w1, w2, slope, unit):
    ids = padded(index[...]).astype(f32).T.astype(i32)
    counts = count[...]
    d = [delta[n].T for n in range(3)]
    radius = jnp.sqrt(d[0] * d[0] + d[1] * d[1] + d[2] * d[2])
    slot = lax.broadcasted_iota(i32, (SLOTS, ATOMS), 0)
    alive = jnp.where(slot < counts, 1.0, 0.0)
    half = (math.pi / (2.0 * cutoff)) * radius
    cosine, sine = jnp.cos(half), jnp.sin(half)
    base = alive * (cosine * cosine) * (1.0 / math.sqrt(SLOTS)) / radius
    slope[...] = -(math.pi / cutoff) * sine / cosine - 1.0 / radius
    for n in range(3):
        unit[n] = d[n] / radius
    sub = lax.broadcasted_iota(i32, (ROWS, ATOMS), 0)
    rates = [columns(-decay[n : n + 1, :]) for n in range(3)]
    for k in range(SLOTS):
        here = slice(k * ATOMS, (k + 1) * ATOMS)
        onehot[:, here] = jnp.where(sub == ids[k : k + 1, :], 1.0, 0.0).astype(bf16)
        r, b = radius[k : k + 1, :], base[k : k + 1, :]
        for n, out in enumerate((w0, w1, w2)):
            out[:, here] = (b * jnp.exp(rates[n] * r)).astype(bf16)


def pick_y_kernel(proj, lower, higher, pick, up, down, table):
    table[0:ATOMS] = proj[...]
    table[OFF_X : OFF_X + GX] = lower[...]
    table[OFF_X + GX : OFF_X + 2 * GX] = higher[...]
    table[OFF_X + 2 * GX : OFF_Y] = jnp.zeros((PAD, C), bf16)
    chosen = mm(pick[...], table[...]).astype(bf16)
    up[...] = chosen[0:GY]
    down[...] = chosen[GY:]


def pick_z_kernel(proj, x_lower, x_higher, y_lower, y_higher, pick, up, down, table):
    table[0:ATOMS] = proj[...]
    table[OFF_X : OFF_X + GX] = x_lower[...]
    table[OFF_X + GX : OFF_X + 2 * GX] = x_higher[...]
    table[OFF_X + 2 * GX : OFF_Y] = jnp.zeros((PAD, C), bf16)
    table[OFF_Y : OFF_Y + GY] = y_lower[...]
    table[OFF_Y + GY : OFF_Z] = y_higher[...]
    chosen = mm(pick[...], table[...]).astype(bf16)
    up[...] = chosen[0:GZ]
    down[...] = chosen[GZ:]


def gather_rows(ghosts, proj, table):
    x_lower, x_higher, y_lower, y_higher, z_lower, z_higher = ghosts
    table[0:ATOMS] = proj[...]
    table[OFF_X : OFF_X + GX] = x_lower[...]
    table[OFF_X + GX : OFF_X + 2 * GX] = x_higher[...]
    table[OFF_X + 2 * GX : OFF_Y] = jnp.zeros((PAD, C), bf16)
    table[OFF_Y : OFF_Y + GY] = y_lower[...]
    table[OFF_Y + GY : OFF_Z] = y_higher[...]
    table[OFF_Z : OFF_Z + GZ] = z_lower[...]
    table[OFF_Z + GZ : ROWS] = z_higher[...]


def forward_part(table, onehot, w, prod):
    turned = table[...].astype(f32).T.astype(bf16)
    total = jnp.zeros((C, ATOMS), f32)
    for start in range(0, PAIRS, CHUNK):
        here = slice(start, start + CHUNK)
        m = mm(turned, onehot[:, here]) * w[:, here].astype(f32)
        prod[:, here] = m.astype(bf16)
        for inner in range(0, CHUNK, ATOMS):
            total = total + m[:, inner : inner + ATOMS]
    return total.T


def layer_kernel(
    feat, proj, xl, xh, yl, yh, zl, zh, onehot, w, self_weight, next_weight, pick_x,
    new_feat, tanh_out, prod, new_proj, up, down, table, *, layer,
):
    gather_rows((xl, xh, yl, yh, zl, zh), proj, table)
    preact = forward_part(table, onehot, w, prod) + mm(feat[...], self_weight[layer])
    t = jnp.tanh(preact)
    tanh_out[...] = t
    features = (feat[...].astype(f32) + t).astype(bf16)
    new_feat[...] = features
    projected = mm(features, next_weight[layer + 1]).astype(bf16)
    new_proj[...] = projected
    chosen = mm(pick_x[...], projected).astype(bf16)
    up[...] = chosen[0:GX]
    down[...] = chosen[GX:]


def backward_part(gradient, t, prod, w, decay_row, slope, onehot, terms, layer):
    pg = gradient * (1.0 - t * t)
    turned = pg.T
    wide = jnp.concatenate([turned] * (CHUNK // ATOMS), axis=1)
    rate = columns(decay_row)
    rates = jnp.concatenate([rate] * (CHUNK // ATOMS), axis=1)
    ones, others = [], []
    for start in range(0, PAIRS, CHUNK):
        here = slice(start, start + CHUNK)
        a = prod[:, here].astype(f32) * wide
        s1 = jnp.sum(a, axis=0, keepdims=True)
        s2 = jnp.sum(a * rates, axis=0, keepdims=True)
        for inner in range(0, CHUNK, ATOMS):
            ones.append(s1[:, inner : inner + ATOMS])
            others.append(s2[:, inner : inner + ATOMS])
        if layer > 0:
            terms[:, here] = (w[:, here].astype(f32) * wide).astype(bf16)
    radius_grad = slope[...] * jnp.concatenate(ones, axis=0) - jnp.concatenate(others, axis=0)
    rows = mm_nt(onehot[...], terms[...]) if layer > 0 else None
    return pg, radius_grad, rows


def send_back(rows, kept, z_lower, z_higher):
    kept[...] = rows[0:OFF_Z]
    z_lower[...] = rows[OFF_Z : OFF_Z + GZ].astype(bf16)
    z_higher[...] = rows[OFF_Z + GZ : ROWS].astype(bf16)


def top_kernel(
    feat, proj, xl, xh, yl, yh, zl, zh, onehot, w, self_weight, energy_proj, energy_out, decay, slope,
    energy, gradient_out, pg_out, radius_out, kept, z_lower, z_higher, table, prod, terms,
):
    gather_rows((xl, xh, yl, yh, zl, zh), proj, table)
    preact = forward_part(table, onehot, w, prod) + mm(feat[...], self_weight[2])
    t = jnp.tanh(preact)
    features = (feat[...].astype(f32) + t).astype(bf16)
    readout = jnp.tanh(mm(features, energy_proj[...]))
    out_row = energy_out[...]
    energy[...] = jnp.sum((readout * out_row).T, axis=0, keepdims=True)
    gradient = split_nt((1.0 - readout * readout) * out_row, energy_proj[...])
    pg, radius_grad, rows = backward_part(
        gradient, t, prod, w, decay[2:3, :], slope, onehot, terms, 2
    )
    gradient_out[...] = gradient
    pg_out[...] = pg
    radius_out[...] = radius_grad
    send_back(rows, kept, z_lower, z_higher)


def return_z_kernel(kept, lower, higher, place, rest, y_lower, y_higher):
    pieces = jnp.concatenate([lower[...], higher[...]], axis=0)
    total = kept[...] + mm(place[...], pieces)
    rest[...] = total[0:UNPADDED]
    y_lower[...] = total[OFF_Y : OFF_Y + GY].astype(bf16)
    y_higher[...] = total[OFF_Y + GY : OFF_Z].astype(bf16)


def return_y_kernel(kept, lower, higher, place, own, x_lower, x_higher):
    pieces = jnp.concatenate([lower[...], higher[...]], axis=0)
    total = kept[...] + mm(place[...], pieces)
    own[...] = total[0:ATOMS]
    x_lower[...] = total[OFF_X : OFF_X + GX].astype(bf16)
    x_higher[...] = total[OFF_X + GX :].astype(bf16)


def down_step(own, lower, higher, place, gradient, pg, self_weight, message_weight, layer):
    pieces = jnp.concatenate([lower[...], higher[...]], axis=0)
    row_sum = own[...] + mm(place[...], pieces)
    return (
        gradient[...]
        + split_nt(pg[...], self_weight[layer])
        + split_nt(row_sum, message_weight[layer])
    )


def middle_kernel(
    own, lower, higher, place, gradient_in, pg_in, self_weight, message_weight,
    t, prod, w, decay, slope, onehot, radius_in,
    gradient_out, pg_out, radius_out, kept, z_lower, z_higher, terms,
):
    gradient = down_step(own, lower, higher, place, gradient_in, pg_in, self_weight, message_weight, 2)
    pg, radius_grad, rows = backward_part(
        gradient, t[...], prod, w, decay[1:2, :], slope, onehot, terms, 1
    )
    gradient_out[...] = gradient
    pg_out[...] = pg
    radius_out[...] = radius_in[...] + radius_grad
    send_back(rows, kept, z_lower, z_higher)


def bottom_kernel(
    own, lower, higher, place, gradient_in, pg_in, self_weight, message_weight,
    t, prod, w, decay, slope, onehot, radius_in, unit,
    own_force, kept, z_lower, z_higher, terms,
):
    gradient = down_step(own, lower, higher, place, gradient_in, pg_in, self_weight, message_weight, 1)
    pg, radius_grad, _ = backward_part(
        gradient, t[...], prod, w, decay[0:1, :], slope, onehot, None, 0
    )
    total = radius_in[...] + radius_grad
    terms[...] = jnp.zeros_like(terms)
    for n in range(3):
        pushed = total * unit[n]
        own_force[n : n + 1, :] = jnp.sum(pushed, axis=0, keepdims=True)
        for k in range(SLOTS):
            terms[n : n + 1, k * ATOMS : (k + 1) * ATOMS] = pushed[k : k + 1, :]
    rows = mm_nt(onehot[...], terms[...].astype(bf16))
    rows = jnp.concatenate([rows, jnp.zeros((ROWS, C - rows.shape[1]), f32)], axis=1)
    send_back(rows, kept, z_lower, z_higher)


def final_kernel(own, lower, higher, place, own_force, forces):
    pieces = jnp.concatenate([lower[...], higher[...]], axis=0)
    row_sum = own[...] + mm(place[...], pieces)
    forces[...] = own_force[...] - row_sum.T[0:3, :]


def spread(proj, up, down, pick_y, pick_z):
    x = swap(up, down, "gx")
    sends = call(
        pick_y_kernel,
        [shape((GY, C), bf16)] * 2,
        [pltpu.VMEM((OFF_Y, C), bf16)],
    )(proj, *x, pick_y)
    y = swap(*sends, "gy")
    sends = call(
        pick_z_kernel,
        [shape((GZ, C), bf16)] * 2,
        [pltpu.VMEM((OFF_Z, C), bf16)],
    )(proj, *x, *y, pick_z)
    z = swap(*sends, "gz")
    return (*x, *y, *z)


def retract(kept, z_lower, z_higher, place_y, place_z):
    higher, lower = swap(z_higher, z_lower, "gz")
    rest, y_lower, y_higher = call(
        return_z_kernel,
        [shape((UNPADDED, C), f32), shape((GY, C), bf16), shape((GY, C), bf16)],
    )(kept, lower, higher, place_z)
    higher, lower = swap(y_higher, y_lower, "gy")
    own, x_lower, x_higher = call(
        return_y_kernel,
        [shape((ATOMS, C), f32), shape((GX, C), bf16), shape((GX, C), bf16)],
    )(rest, lower, higher, place_y)
    higher, lower = swap(x_higher, x_lower, "gx")
    return own, lower, higher


def local(
    atom_types,
    type_table,
    neighbor_index,
    neighbor_count,
    displacement,
    send_x,
    send_y,
    send_z,
    message_weight,
    self_weight,
    decay,
    energy_proj,
    energy_out,
):
    features, proj, up, down, pick_x, place_x = call(
        first_kernel,
        [
            shape((ATOMS, C), bf16),
            shape((ATOMS, C), bf16),
            shape((GX, C), bf16),
            shape((GX, C), bf16),
            shape((2 * GX, ATOMS), bf16),
            shape((ATOMS, 2 * GX), bf16),
        ],
        [pltpu.VMEM((128, C), f32)],
    )(atom_types.reshape(1, ATOMS), type_table, message_weight, send_x.reshape(1, 2 * GX))
    pick_y, pick_z, place_y, place_z = call(
        lists_kernel,
        [
            shape((2 * GY, OFF_Y), bf16),
            shape((2 * GZ, OFF_Z), bf16),
            shape((UNPADDED, 2 * GY), bf16),
            shape((OFF_Z, 2 * GZ), bf16),
        ],
    )(send_y.reshape(1, 2 * GY), send_z.reshape(1, 2 * GZ))
    onehot, w0, w1, w2, slope, unit = call(
        weights_kernel,
        [
            shape((ROWS, PAIRS), bf16),
            shape((C, PAIRS), bf16),
            shape((C, PAIRS), bf16),
            shape((C, PAIRS), bf16),
            shape((SLOTS, ATOMS), f32),
            shape((3, SLOTS, ATOMS), f32),
        ],
    )(neighbor_index, neighbor_count.reshape(1, ATOMS), displacement, decay)
    weights = (w0, w1, w2)
    saved = []
    for layer in range(2):
        ghosts = spread(proj, up, down, pick_y, pick_z)
        body = lambda *refs, layer=layer: layer_kernel(*refs, layer=layer)
        features, t, prod, proj, up, down = call(
            body,
            [
                shape((ATOMS, C), bf16),
                shape((ATOMS, C), f32),
                shape((C, PAIRS), bf16),
                shape((ATOMS, C), bf16),
                shape((GX, C), bf16),
                shape((GX, C), bf16),
            ],
            [pltpu.VMEM((ROWS, C), bf16)],
        )(features, proj, *ghosts, onehot, weights[layer], self_weight, message_weight, pick_x)
        saved.append((t, prod))
    ghosts = spread(proj, up, down, pick_y, pick_z)
    grad_shapes = [
        shape((ATOMS, C), f32),
        shape((ATOMS, C), f32),
        shape((SLOTS, ATOMS), f32),
    ]
    back_shapes = [shape((OFF_Z, C), f32), shape((GZ, C), bf16), shape((GZ, C), bf16)]
    energy, gradient, pg, radius_grad, *back = call(
        top_kernel,
        [shape((1, ATOMS), f32), *grad_shapes, *back_shapes],
        [
            pltpu.VMEM((ROWS, C), bf16),
            pltpu.VMEM((C, PAIRS), bf16),
            pltpu.VMEM((C, PAIRS), bf16),
        ],
    )(
        features, proj, *ghosts, onehot, w2, self_weight, energy_proj, energy_out.reshape(1, C),
        decay, slope,
    )
    returned = retract(*back, place_y, place_z)
    t, prod = saved[1]
    gradient, pg, radius_grad, *back = call(
        middle_kernel, [*grad_shapes, *back_shapes], [pltpu.VMEM((C, PAIRS), bf16)]
    )(
        *returned, place_x, gradient, pg, self_weight, message_weight, t, prod, w1, decay, slope,
        onehot, radius_grad,
    )
    returned = retract(*back, place_y, place_z)
    t, prod = saved[0]
    own_force, *back = call(
        bottom_kernel,
        [shape((3, ATOMS), f32), *back_shapes],
        [pltpu.VMEM((16, PAIRS), f32)],
    )(
        *returned, place_x, gradient, pg, self_weight, message_weight, t, prod, w0, decay, slope,
        onehot, radius_grad, unit,
    )
    returned = retract(*back, place_y, place_z)
    forces = call(final_kernel, shape((3, ATOMS), f32))(*returned, place_x, own_force)
    return (energy.reshape(ATOMS), forces)


def solution(mesh):
    split = ("gx", "gy", "gz")
    return jax.shard_map(
        local,
        mesh=mesh,
        in_specs=(
            P(split),
            P(),
            P(split, None),
            P(split),
            P(None, split, None),
            P(None, split),
            P(None, split),
            P(None, split),
            P(),
            P(),
            P(),
            P(),
            P(),
        ),
        out_specs=(P(split), P(None, split)),
        check_vma=False,
    )
```

```python
import math

import jax
import jax.numpy as jnp
from jax import lax
from jax.experimental import pallas as pl
from jax.experimental.pallas import tpu as pltpu
from jax.sharding import PartitionSpec as P

cutoff = 4.0
ATOMS = 128
C = 128
SLOTS = 48
GX, GY, GZ = 32, 64, 64
OFF_X, OFF_Y, OFF_Z, ROWS = 128, 256, 384, 512
PAD = 64
UNPADDED = ATOMS + 2 * GX
PAIRS = ATOMS * SLOTS
CHUNK = 256
f32, bf16, i32 = jnp.float32, jnp.bfloat16, jnp.int32
NT = (((1,), (1,)), ((), ()))


def shape(dims, dtype):
    return jax.ShapeDtypeStruct(dims, dtype)


def call(body, outs, scratch=(), limit=4):
    return pl.pallas_call(
        body,
        out_shape=outs,
        scratch_shapes=list(scratch),
        compiler_params=pltpu.CompilerParams(vmem_limit_bytes=limit * 1024 * 1024),
    )


def along(axis, distance):
    size = lax.axis_size(axis)
    return [(i, (i + distance) % size) for i in range(size)]


def swap(to_higher, to_lower, axis):
    from_lower = lax.ppermute(to_higher, axis, along(axis, 1))
    from_higher = lax.ppermute(to_lower, axis, along(axis, -1))
    return from_lower, from_higher


def mm(a, b):
    return jnp.dot(a, b, preferred_element_type=f32)


def mm_nt(a, b):
    return lax.dot_general(a, b, NT, preferred_element_type=f32)


def split_nt(a, b):
    high = a.astype(bf16)
    low = (a - high.astype(f32)).astype(bf16)
    return mm_nt(high, b) + mm_nt(low, b)


def columns(row):
    return jnp.broadcast_to(row, (128, row.shape[1])).T


def padded(ids):
    return jnp.where(ids >= UNPADDED, ids + PAD, ids)


def picker(lists, extent):
    ids = jnp.concatenate([columns(lists[n : n + 1, :].astype(f32)) for n in range(2)], axis=0)
    parts = []
    for start in range(0, extent, 128):
        lane = (lax.broadcasted_iota(i32, ids.shape, 1) + start).astype(f32)
        parts.append(jnp.where(ids == lane, 1.0, 0.0).astype(bf16))
    return jnp.concatenate(parts, axis=1) if len(parts) > 1 else parts[0]


def place_into(out, lists):
    n = lists.shape[1]
    sub = lax.broadcasted_iota(i32, (out.shape[0], n), 0)
    for side in range(2):
        out[:, side * n : (side + 1) * n] = jnp.where(
            sub == lists[side : side + 1, :], 1.0, 0.0
        ).astype(bf16)


def first_kernel(types, table, weight, send_x, feat, proj, up, down, pick_x, place_x, rows):
    rows[...] = jnp.zeros_like(rows)
    rows[0:6, :] = table[...].astype(f32)
    kinds = columns(types[...].astype(f32))
    lane = lax.broadcasted_iota(i32, (ATOMS, 128), 1).astype(f32)
    onehot = jnp.where(kinds == lane, 1.0, 0.0).astype(bf16)
    features = mm(onehot, rows[...].astype(bf16)).astype(bf16)
    projected = mm(features, weight[0]).astype(bf16)
    feat[...] = features
    proj[...] = projected
    pick = picker(send_x[...], ATOMS)
    place_into(place_x, send_x[...])
    pick_x[...] = pick
    chosen = mm(pick, projected).astype(bf16)
    up[...] = chosen[0:GX]
    down[...] = chosen[GX:]


def lists_kernel(send_y, send_z, pick_y, pick_z, place_y, place_z):
    ids_y, ids_z = send_y[...], padded(send_z[...])
    pick_y[...] = picker(ids_y, OFF_Y)
    pick_z[...] = picker(ids_z, OFF_Z)
    place_into(place_y, ids_y)
    place_into(place_z, ids_z)


def weights_kernel(index, count, delta, decay, onehot, w0, w1, w2, slope, unit):
    ids = padded(index[...])
    counts = count[...]
    d = [delta[n] for n in range(3)]
    radius = jnp.sqrt(d[0] * d[0] + d[1] * d[1] + d[2] * d[2])
    slot = lax.broadcasted_iota(i32, (SLOTS, ATOMS), 0)
    alive = jnp.where(slot < counts, 1.0, 0.0)
    half = (math.pi / (2.0 * cutoff)) * radius
    cosine, sine = jnp.cos(half), jnp.sin(half)
    base = alive * (cosine * cosine) * (1.0 / math.sqrt(SLOTS)) / radius
    slope[...] = -(math.pi / cutoff) * sine / cosine - 1.0 / radius
    for n in range(3):
        unit[n] = d[n] / radius
    sub = lax.broadcasted_iota(i32, (ROWS, ATOMS), 0)
    rates = [columns(-decay[n : n + 1, :]) for n in range(3)]
    for k in range(SLOTS):
        here = slice(k * ATOMS, (k + 1) * ATOMS)
        onehot[:, here] = jnp.where(sub == ids[k : k + 1, :], 1.0, 0.0).astype(bf16)
        r, b = radius[k : k + 1, :], base[k : k + 1, :]
        for n, out in enumerate((w0, w1, w2)):
            out[:, here] = (b * jnp.exp(rates[n] * r)).astype(bf16)


def pick_y_kernel(proj, lower, higher, pick, up, down, table):
    table[0:ATOMS] = proj[...]
    table[OFF_X : OFF_X + GX] = lower[...]
    table[OFF_X + GX : OFF_X + 2 * GX] = higher[...]
    table[OFF_X + 2 * GX : OFF_Y] = jnp.zeros((PAD, C), bf16)
    chosen = mm(pick[...], table[...]).astype(bf16)
    up[...] = chosen[0:GY]
    down[...] = chosen[GY:]


def pick_z_kernel(proj, x_lower, x_higher, y_lower, y_higher, pick, up, down, table):
    table[0:ATOMS] = proj[...]
    table[OFF_X : OFF_X + GX] = x_lower[...]
    table[OFF_X + GX : OFF_X + 2 * GX] = x_higher[...]
    table[OFF_X + 2 * GX : OFF_Y] = jnp.zeros((PAD, C), bf16)
    table[OFF_Y : OFF_Y + GY] = y_lower[...]
    table[OFF_Y + GY : OFF_Z] = y_higher[...]
    chosen = mm(pick[...], table[...]).astype(bf16)
    up[...] = chosen[0:GZ]
    down[...] = chosen[GZ:]


def gather_rows(ghosts, proj, table):
    x_lower, x_higher, y_lower, y_higher, z_lower, z_higher = ghosts
    table[0:ATOMS] = proj[...]
    table[OFF_X : OFF_X + GX] = x_lower[...]
    table[OFF_X + GX : OFF_X + 2 * GX] = x_higher[...]
    table[OFF_X + 2 * GX : OFF_Y] = jnp.zeros((PAD, C), bf16)
    table[OFF_Y : OFF_Y + GY] = y_lower[...]
    table[OFF_Y + GY : OFF_Z] = y_higher[...]
    table[OFF_Z : OFF_Z + GZ] = z_lower[...]
    table[OFF_Z + GZ : ROWS] = z_higher[...]


def forward_part(table, onehot, w, prod):
    turned = table[...].astype(f32).T.astype(bf16)
    total = jnp.zeros((C, ATOMS), f32)
    for start in range(0, PAIRS, CHUNK):
        here = slice(start, start + CHUNK)
        m = mm(turned, onehot[:, here]) * w[:, here].astype(f32)
        prod[:, here] = m.astype(bf16)
        for inner in range(0, CHUNK, ATOMS):
            total = total + m[:, inner : inner + ATOMS]
    return total.T


def layer_kernel(
    feat, proj, xl, xh, yl, yh, zl, zh, onehot, w, self_weight, next_weight, pick_x,
    new_feat, tanh_out, prod, new_proj, up, down, table, *, layer,
):
    gather_rows((xl, xh, yl, yh, zl, zh), proj, table)
    preact = forward_part(table, onehot, w, prod) + mm(feat[...], self_weight[layer])
    t = jnp.tanh(preact)
    tanh_out[...] = t
    features = (feat[...].astype(f32) + t).astype(bf16)
    new_feat[...] = features
    projected = mm(features, next_weight[layer + 1]).astype(bf16)
    new_proj[...] = projected
    chosen = mm(pick_x[...], projected).astype(bf16)
    up[...] = chosen[0:GX]
    down[...] = chosen[GX:]


def backward_part(gradient, t, prod, w, decay_row, slope, onehot, terms, layer):
    pg = gradient * (1.0 - t * t)
    turned = pg.T
    wide = jnp.concatenate([turned] * (CHUNK // ATOMS), axis=1)
    rate = columns(decay_row)
    rates = jnp.concatenate([rate] * (CHUNK // ATOMS), axis=1)
    ones, others = [], []
    for start in range(0, PAIRS, CHUNK):
        here = slice(start, start + CHUNK)
        a = prod[:, here].astype(f32) * wide
        s1 = jnp.sum(a, axis=0, keepdims=True)
        s2 = jnp.sum(a * rates, axis=0, keepdims=True)
        for inner in range(0, CHUNK, ATOMS):
            ones.append(s1[:, inner : inner + ATOMS])
            others.append(s2[:, inner : inner + ATOMS])
        if layer > 0:
            terms[:, here] = (w[:, here].astype(f32) * wide).astype(bf16)
    radius_grad = slope[...] * jnp.concatenate(ones, axis=0) - jnp.concatenate(others, axis=0)
    rows = mm_nt(onehot[...], terms[...]) if layer > 0 else None
    return pg, radius_grad, rows


def send_back(rows, kept, z_lower, z_higher):
    kept[...] = rows[0:OFF_Z]
    z_lower[...] = rows[OFF_Z : OFF_Z + GZ].astype(bf16)
    z_higher[...] = rows[OFF_Z + GZ : ROWS].astype(bf16)


def top_kernel(
    feat, proj, xl, xh, yl, yh, zl, zh, onehot, w, self_weight, energy_proj, energy_out, decay, slope,
    energy, gradient_out, pg_out, radius_out, kept, z_lower, z_higher, table, prod, terms,
):
    gather_rows((xl, xh, yl, yh, zl, zh), proj, table)
    preact = forward_part(table, onehot, w, prod) + mm(feat[...], self_weight[2])
    t = jnp.tanh(preact)
    features = (feat[...].astype(f32) + t).astype(bf16)
    readout = jnp.tanh(mm(features, energy_proj[...]))
    out_row = energy_out[...]
    energy[...] = jnp.sum((readout * out_row).T, axis=0, keepdims=True)
    gradient = split_nt((1.0 - readout * readout) * out_row, energy_proj[...])
    pg, radius_grad, rows = backward_part(
        gradient, t, prod, w, decay[2:3, :], slope, onehot, terms, 2
    )
    gradient_out[...] = gradient
    pg_out[...] = pg
    radius_out[...] = radius_grad
    send_back(rows, kept, z_lower, z_higher)


def return_z_kernel(kept, lower, higher, place, rest, y_lower, y_higher):
    pieces = jnp.concatenate([lower[...], higher[...]], axis=0)
    total = kept[...] + mm(place[...], pieces)
    rest[...] = total[0:UNPADDED]
    y_lower[...] = total[OFF_Y : OFF_Y + GY].astype(bf16)
    y_higher[...] = total[OFF_Y + GY : OFF_Z].astype(bf16)


def return_y_kernel(kept, lower, higher, place, own, x_lower, x_higher):
    pieces = jnp.concatenate([lower[...], higher[...]], axis=0)
    total = kept[...] + mm(place[...], pieces)
    own[...] = total[0:ATOMS]
    x_lower[...] = total[OFF_X : OFF_X + GX].astype(bf16)
    x_higher[...] = total[OFF_X + GX :].astype(bf16)


def down_step(own, lower, higher, place, gradient, pg, self_weight, message_weight, layer):
    pieces = jnp.concatenate([lower[...], higher[...]], axis=0)
    row_sum = own[...] + mm(place[...], pieces)
    return (
        gradient[...]
        + split_nt(pg[...], self_weight[layer])
        + split_nt(row_sum, message_weight[layer])
    )


def middle_kernel(
    own, lower, higher, place, gradient_in, pg_in, self_weight, message_weight,
    t, prod, w, decay, slope, onehot, radius_in,
    gradient_out, pg_out, radius_out, kept, z_lower, z_higher, terms,
):
    gradient = down_step(own, lower, higher, place, gradient_in, pg_in, self_weight, message_weight, 2)
    pg, radius_grad, rows = backward_part(
        gradient, t[...], prod, w, decay[1:2, :], slope, onehot, terms, 1
    )
    gradient_out[...] = gradient
    pg_out[...] = pg
    radius_out[...] = radius_in[...] + radius_grad
    send_back(rows, kept, z_lower, z_higher)


def bottom_kernel(
    own, lower, higher, place, gradient_in, pg_in, self_weight, message_weight,
    t, prod, w, decay, slope, onehot, radius_in, unit,
    own_force, kept, z_lower, z_higher, terms,
):
    gradient = down_step(own, lower, higher, place, gradient_in, pg_in, self_weight, message_weight, 1)
    pg, radius_grad, _ = backward_part(
        gradient, t[...], prod, w, decay[0:1, :], slope, onehot, None, 0
    )
    total = radius_in[...] + radius_grad
    terms[...] = jnp.zeros_like(terms)
    for n in range(3):
        pushed = total * unit[n]
        own_force[n : n + 1, :] = jnp.sum(pushed, axis=0, keepdims=True)
        for k in range(SLOTS):
            terms[n : n + 1, k * ATOMS : (k + 1) * ATOMS] = pushed[k : k + 1, :]
    rows = mm_nt(onehot[...], terms[...].astype(bf16))
    rows = jnp.concatenate([rows, jnp.zeros((ROWS, C - rows.shape[1]), f32)], axis=1)
    send_back(rows, kept, z_lower, z_higher)


def final_kernel(own, lower, higher, place, own_force, forces):
    pieces = jnp.concatenate([lower[...], higher[...]], axis=0)
    row_sum = own[...] + mm(place[...], pieces)
    forces[...] = own_force[...] - row_sum.T[0:3, :]


def spread(proj, up, down, pick_y, pick_z):
    x = swap(up, down, "gx")
    sends = call(
        pick_y_kernel,
        [shape((GY, C), bf16)] * 2,
        [pltpu.VMEM((OFF_Y, C), bf16)],
    )(proj, *x, pick_y)
    y = swap(*sends, "gy")
    sends = call(
        pick_z_kernel,
        [shape((GZ, C), bf16)] * 2,
        [pltpu.VMEM((OFF_Z, C), bf16)],
    )(proj, *x, *y, pick_z)
    z = swap(*sends, "gz")
    return (*x, *y, *z)


def retract(kept, z_lower, z_higher, place_y, place_z):
    higher, lower = swap(z_higher, z_lower, "gz")
    rest, y_lower, y_higher = call(
        return_z_kernel,
        [shape((UNPADDED, C), f32), shape((GY, C), bf16), shape((GY, C), bf16)],
    )(kept, lower, higher, place_z)
    higher, lower = swap(y_higher, y_lower, "gy")
    own, x_lower, x_higher = call(
        return_y_kernel,
        [shape((ATOMS, C), f32), shape((GX, C), bf16), shape((GX, C), bf16)],
    )(rest, lower, higher, place_y)
    higher, lower = swap(x_higher, x_lower, "gx")
    return own, lower, higher


def local(
    atom_types,
    type_table,
    neighbor_index,
    neighbor_count,
    displacement,
    send_x,
    send_y,
    send_z,
    message_weight,
    self_weight,
    decay,
    energy_proj,
    energy_out,
):
    features, proj, up, down, pick_x, place_x = call(
        first_kernel,
        [
            shape((ATOMS, C), bf16),
            shape((ATOMS, C), bf16),
            shape((GX, C), bf16),
            shape((GX, C), bf16),
            shape((2 * GX, ATOMS), bf16),
            shape((ATOMS, 2 * GX), bf16),
        ],
        [pltpu.VMEM((128, C), f32)],
    )(atom_types.reshape(1, ATOMS), type_table, message_weight, send_x)
    pick_y, pick_z, place_y, place_z = call(
        lists_kernel,
        [
            shape((2 * GY, OFF_Y), bf16),
            shape((2 * GZ, OFF_Z), bf16),
            shape((UNPADDED, 2 * GY), bf16),
            shape((OFF_Z, 2 * GZ), bf16),
        ],
    )(send_y, send_z)
    onehot, w0, w1, w2, slope, unit = call(
        weights_kernel,
        [
            shape((ROWS, PAIRS), bf16),
            shape((C, PAIRS), bf16),
            shape((C, PAIRS), bf16),
            shape((C, PAIRS), bf16),
            shape((SLOTS, ATOMS), f32),
            shape((3, SLOTS, ATOMS), f32),
        ],
    )(
        neighbor_index.T,
        neighbor_count.reshape(1, ATOMS),
        jnp.swapaxes(displacement, 1, 2),
        decay,
    )
    weights = (w0, w1, w2)
    saved = []
    for layer in range(2):
        ghosts = spread(proj, up, down, pick_y, pick_z)
        body = lambda *refs, layer=layer: layer_kernel(*refs, layer=layer)
        features, t, prod, proj, up, down = call(
            body,
            [
                shape((ATOMS, C), bf16),
                shape((ATOMS, C), f32),
                shape((C, PAIRS), bf16),
                shape((ATOMS, C), bf16),
                shape((GX, C), bf16),
                shape((GX, C), bf16),
            ],
            [pltpu.VMEM((ROWS, C), bf16)],
        )(features, proj, *ghosts, onehot, weights[layer], self_weight, message_weight, pick_x)
        saved.append((t, prod))
    ghosts = spread(proj, up, down, pick_y, pick_z)
    grad_shapes = [
        shape((ATOMS, C), f32),
        shape((ATOMS, C), f32),
        shape((SLOTS, ATOMS), f32),
    ]
    back_shapes = [shape((OFF_Z, C), f32), shape((GZ, C), bf16), shape((GZ, C), bf16)]
    energy, gradient, pg, radius_grad, *back = call(
        top_kernel,
        [shape((1, ATOMS), f32), *grad_shapes, *back_shapes],
        [
            pltpu.VMEM((ROWS, C), bf16),
            pltpu.VMEM((C, PAIRS), bf16),
            pltpu.VMEM((C, PAIRS), bf16),
        ],
    )(
        features, proj, *ghosts, onehot, w2, self_weight, energy_proj, energy_out.reshape(1, C),
        decay, slope,
    )
    returned = retract(*back, place_y, place_z)
    t, prod = saved[1]
    gradient, pg, radius_grad, *back = call(
        middle_kernel, [*grad_shapes, *back_shapes], [pltpu.VMEM((C, PAIRS), bf16)]
    )(
        *returned, place_x, gradient, pg, self_weight, message_weight, t, prod, w1, decay, slope,
        onehot, radius_grad,
    )
    returned = retract(*back, place_y, place_z)
    t, prod = saved[0]
    own_force, *back = call(
        bottom_kernel,
        [shape((3, ATOMS), f32), *back_shapes],
        [pltpu.VMEM((16, PAIRS), f32)],
    )(
        *returned, place_x, gradient, pg, self_weight, message_weight, t, prod, w0, decay, slope,
        onehot, radius_grad, unit,
    )
    returned = retract(*back, place_y, place_z)
    forces = call(final_kernel, shape((3, ATOMS), f32))(*returned, place_x, own_force)
    return (energy.reshape(ATOMS), forces)


def solution(mesh):
    split = ("gx", "gy", "gz")
    return jax.shard_map(
        local,
        mesh=mesh,
        in_specs=(
            P(split),
            P(),
            P(split, None),
            P(split),
            P(None, split, None),
            P(None, split),
            P(None, split),
            P(None, split),
            P(),
            P(),
            P(),
            P(),
            P(),
        ),
        out_specs=(P(split), P(None, split)),
        check_vma=False,
    )
```

```python
import math

import jax
import jax.numpy as jnp
from jax import lax
from jax.experimental import pallas as pl
from jax.experimental.pallas import tpu as pltpu
from jax.sharding import PartitionSpec as P

cutoff = 4.0
ATOMS = 128
C = 128
SLOTS = 48
GX, GY, GZ = 32, 64, 64
LOADED = 13
OFF_X, OFF_Y, OFF_Z, ROWS = 128, 256, 384, 512
PAD = 64
UNPADDED = ATOMS + 2 * GX
PAIRS = ATOMS * SLOTS
CHUNK = 256
SPAN = 1536
f32, bf16, i32 = jnp.float32, jnp.bfloat16, jnp.int32
NT = (((1,), (1,)), ((), ()))


def shape(dims, dtype):
    return jax.ShapeDtypeStruct(dims, dtype)


def call(body, outs, scratch=(), limit=4, in_specs=None):
    more = {} if in_specs is None else {"in_specs": in_specs}
    return pl.pallas_call(
        body,
        out_shape=outs,
        **more,
        scratch_shapes=list(scratch),
        compiler_params=pltpu.CompilerParams(vmem_limit_bytes=limit * 1024 * 1024),
    )


def along(axis, distance):
    size = lax.axis_size(axis)
    return [(i, (i + distance) % size) for i in range(size)]


def swap(to_higher, to_lower, axis):
    from_lower = lax.ppermute(to_higher, axis, along(axis, 1))
    from_higher = lax.ppermute(to_lower, axis, along(axis, -1))
    return from_lower, from_higher


def mm(a, b):
    return jnp.dot(a, b, preferred_element_type=f32)


def mm_nt(a, b):
    return lax.dot_general(a, b, NT, preferred_element_type=f32)


def split_nt(a, b):
    high = a.astype(bf16)
    low = (a - high.astype(f32)).astype(bf16)
    return mm_nt(high, b) + mm_nt(low, b)


def columns(row):
    return jnp.broadcast_to(row, (128, row.shape[1])).T


def padded(ids):
    return jnp.where(ids >= UNPADDED, ids + PAD, ids)


def picker(lists, extent):
    ids = jnp.concatenate([columns(lists[n : n + 1, :].astype(f32)) for n in range(2)], axis=0)
    parts = []
    for start in range(0, extent, 128):
        lane = (lax.broadcasted_iota(i32, ids.shape, 1) + start).astype(f32)
        parts.append(jnp.where(ids == lane, 1.0, 0.0).astype(bf16))
    return jnp.concatenate(parts, axis=1) if len(parts) > 1 else parts[0]


def place_into(out, lists):
    n = lists.shape[1]
    sub = lax.broadcasted_iota(i32, (out.shape[0], n), 0)
    for side in range(2):
        out[:, side * n : (side + 1) * n] = jnp.where(
            sub == lists[side : side + 1, :], 1.0, 0.0
        ).astype(bf16)


def first_kernel(*refs):
    inputs, refs = refs[:LOADED], refs[LOADED:]
    kept, refs = refs[: LOADED - 3], refs[LOADED - 3 :]
    feat, proj, up, down, pick_x, place_x, rows, types, table, send_x, sems = refs
    copies = (types, table, send_x, *kept)
    weight = kept[0]
    moves = [pltpu.make_async_copy(a, b, sems.at[i]) for i, (a, b) in enumerate(zip(inputs, copies))]
    for move in moves:
        move.start()
    rows[...] = jnp.zeros_like(rows)
    for move in moves[:4]:
        move.wait()
    rows[0:6, :] = table[...].astype(f32)
    kinds = columns(types[...].astype(f32))
    lane = lax.broadcasted_iota(i32, (ATOMS, 128), 1).astype(f32)
    onehot = jnp.where(kinds == lane, 1.0, 0.0).astype(bf16)
    features = mm(onehot, rows[...].astype(bf16)).astype(bf16)
    projected = mm(features, weight[0]).astype(bf16)
    feat[...] = features
    proj[...] = projected
    pick = picker(send_x[...], ATOMS)
    place_into(place_x, send_x[...])
    pick_x[...] = pick
    chosen = mm(pick, projected).astype(bf16)
    up[...] = chosen[0:GX]
    down[...] = chosen[GX:]
    for move in moves[4:]:
        move.wait()


def lists_kernel(send_y, send_z, pick_y, pick_z, place_y, place_z):
    ids_y, ids_z = send_y[...], padded(send_z[...])
    pick_y[...] = picker(ids_y, OFF_Y)
    pick_z[...] = picker(ids_z, OFF_Z)
    place_into(place_y, ids_y)
    place_into(place_z, ids_z)


def onehot_kernel(index, onehot):
    ids = padded(index[...])
    sub = lax.broadcasted_iota(i32, (ROWS, ATOMS), 0)
    for k in range(SLOTS):
        here = slice(k * ATOMS, (k + 1) * ATOMS)
        onehot[:, here] = jnp.where(sub == ids[k : k + 1, :], 1.0, 0.0).astype(bf16)


def weights_into(out, radius, base, decay_row):
    rate = columns(-decay_row)
    for k in range(SLOTS):
        here = slice(k * ATOMS, (k + 1) * ATOMS)
        out[:, here] = (base[k : k + 1, :] * jnp.exp(rate * radius[k : k + 1, :])).astype(bf16)


def radial_kernel(count, delta, decay, w, slope, unit, radius_out, base_out):
    d = [delta[n] for n in range(3)]
    radius = jnp.sqrt(d[0] * d[0] + d[1] * d[1] + d[2] * d[2])
    slot = lax.broadcasted_iota(i32, (SLOTS, ATOMS), 0)
    alive = jnp.where(slot < count[...], 1.0, 0.0)
    half = (math.pi / (2.0 * cutoff)) * radius
    cosine, sine = jnp.cos(half), jnp.sin(half)
    base = alive * (cosine * cosine) * (1.0 / math.sqrt(SLOTS)) / radius
    slope[...] = -(math.pi / cutoff) * sine / cosine - 1.0 / radius
    for n in range(3):
        unit[n] = d[n] / radius
    radius_out[...] = radius
    base_out[...] = base
    weights_into(w, radius, base, decay[0:1, :])


def later_weights_kernel(radius, base, decay, w, *, layer):
    weights_into(w, radius[...], base[...], decay[layer : layer + 1, :])


def pick_y_kernel(proj, lower, higher, pick, up, down, table):
    table[0:ATOMS] = proj[...]
    table[OFF_X : OFF_X + GX] = lower[...]
    table[OFF_X + GX : OFF_X + 2 * GX] = higher[...]
    table[OFF_X + 2 * GX : OFF_Y] = jnp.zeros((PAD, C), bf16)
    chosen = mm(pick[...], table[...]).astype(bf16)
    up[...] = chosen[0:GY]
    down[...] = chosen[GY:]


def pick_z_kernel(proj, x_lower, x_higher, y_lower, y_higher, pick, ready, up, down, table):
    table[0:ATOMS] = proj[...]
    table[OFF_X : OFF_X + GX] = x_lower[...]
    table[OFF_X + GX : OFF_X + 2 * GX] = x_higher[...]
    table[OFF_X + 2 * GX : OFF_Y] = jnp.zeros((PAD, C), bf16)
    table[OFF_Y : OFF_Y + GY] = y_lower[...]
    table[OFF_Y + GY : OFF_Z] = y_higher[...]
    chosen = mm(pick[...], table[...]).astype(bf16)
    up[...] = chosen[0:GZ]
    down[...] = chosen[GZ:]


def gather_rows(ghosts, proj, table):
    x_lower, x_higher, y_lower, y_higher, z_lower, z_higher = ghosts
    table[0:ATOMS] = proj[...]
    table[OFF_X : OFF_X + GX] = x_lower[...]
    table[OFF_X + GX : OFF_X + 2 * GX] = x_higher[...]
    table[OFF_X + 2 * GX : OFF_Y] = jnp.zeros((PAD, C), bf16)
    table[OFF_Y : OFF_Y + GY] = y_lower[...]
    table[OFF_Y + GY : OFF_Z] = y_higher[...]
    table[OFF_Z : OFF_Z + GZ] = z_lower[...]
    table[OFF_Z + GZ : ROWS] = z_higher[...]


def forward_part(table, onehot, w, prod):
    turned = table[...].astype(f32).T.astype(bf16)
    total = jnp.zeros((C, ATOMS), f32)
    for start in range(0, PAIRS, CHUNK):
        here = slice(start, start + CHUNK)
        m = mm(turned, onehot[:, here]) * w[:, here].astype(f32)
        prod[:, here] = m.astype(bf16)
        for inner in range(0, CHUNK, ATOMS):
            total = total + m[:, inner : inner + ATOMS]
    return total.T


def layer_kernel(
    feat, proj, xl, xh, yl, yh, zl, zh, onehot, w, self_weight, next_weight, pick_x,
    new_feat, tanh_out, prod, new_proj, up, down, table, *, layer,
):
    gather_rows((xl, xh, yl, yh, zl, zh), proj, table)
    preact = forward_part(table, onehot, w, prod) + mm(feat[...], self_weight[layer])
    t = jnp.tanh(preact)
    tanh_out[...] = t
    features = (feat[...].astype(f32) + t).astype(bf16)
    new_feat[...] = features
    projected = mm(features, next_weight[layer + 1]).astype(bf16)
    new_proj[...] = projected
    chosen = mm(pick_x[...], projected).astype(bf16)
    up[...] = chosen[0:GX]
    down[...] = chosen[GX:]


def backward_sums(prod, start, wide, rates, slope):
    a = prod[:, start : start + CHUNK].astype(f32) * wide
    s1 = jnp.sum(a, axis=0, keepdims=True)
    s2 = jnp.sum(a * rates, axis=0, keepdims=True)
    out = []
    for inner in range(0, CHUNK, ATOMS):
        k = (start + inner) // ATOMS
        here = slice(inner, inner + ATOMS)
        out.append(slope[k : k + 1, :] * s1[:, here] - s2[:, here])
    return out


def backward_part(gradient, t, prod, w, decay_row, slope, onehot, rows):
    pg = gradient * (1.0 - t * t)
    wide = jnp.concatenate([pg.T] * (CHUNK // ATOMS), axis=1)
    rates = jnp.concatenate([columns(decay_row)] * (CHUNK // ATOMS), axis=1)
    parts = []
    for start in range(0, PAIRS, SPAN):
        terms = []
        for inner in range(start, start + SPAN, CHUNK):
            parts += backward_sums(prod, inner, wide, rates, slope)
            terms.append((w[:, inner : inner + CHUNK].astype(f32) * wide).astype(bf16))
        terms = jnp.concatenate(terms, axis=1)
        added = mm_nt(onehot[:, start : start + SPAN], terms)
        rows[...] = added if start == 0 else rows[...] + added
    return pg, jnp.concatenate(parts, axis=0)


def send_back(rows, kept, z_lower, z_higher):
    kept[...] = rows[0:OFF_Z]
    z_lower[...] = rows[OFF_Z : OFF_Z + GZ].astype(bf16)
    z_higher[...] = rows[OFF_Z + GZ : ROWS].astype(bf16)


def top_kernel(
    feat, proj, xl, xh, yl, yh, zl, zh, onehot, w, self_weight, energy_proj, energy_out, decay, slope,
    energy, gradient_out, pg_out, radius_out, kept, z_lower, z_higher, table, prod, rows,
):
    gather_rows((xl, xh, yl, yh, zl, zh), proj, table)
    preact = forward_part(table, onehot, w, prod) + mm(feat[...], self_weight[2])
    t = jnp.tanh(preact)
    features = (feat[...].astype(f32) + t).astype(bf16)
    readout = jnp.tanh(mm(features, energy_proj[...]))
    out_row = energy_out[...]
    energy[...] = jnp.sum((readout * out_row).T, axis=0, keepdims=True)
    gradient = split_nt((1.0 - readout * readout) * out_row, energy_proj[...])
    pg, radius_grad = backward_part(gradient, t, prod, w, decay[2:3, :], slope, onehot, rows)
    gradient_out[...] = gradient
    pg_out[...] = pg
    radius_out[...] = radius_grad
    send_back(rows, kept, z_lower, z_higher)


def return_z_kernel(kept, lower, higher, place, rest, y_lower, y_higher):
    pieces = jnp.concatenate([lower[...], higher[...]], axis=0)
    total = kept[...] + mm(place[...], pieces)
    rest[...] = total[0:UNPADDED]
    y_lower[...] = total[OFF_Y : OFF_Y + GY].astype(bf16)
    y_higher[...] = total[OFF_Y + GY : OFF_Z].astype(bf16)


def return_y_kernel(kept, lower, higher, place, own, x_lower, x_higher):
    pieces = jnp.concatenate([lower[...], higher[...]], axis=0)
    total = kept[...] + mm(place[...], pieces)
    own[...] = total[0:ATOMS]
    x_lower[...] = total[OFF_X : OFF_X + GX].astype(bf16)
    x_higher[...] = total[OFF_X + GX :].astype(bf16)


def down_step(own, lower, higher, place, gradient, pg, self_weight, message_weight, layer):
    pieces = jnp.concatenate([lower[...], higher[...]], axis=0)
    row_sum = own[...] + mm(place[...], pieces)
    return (
        gradient[...]
        + split_nt(pg[...], self_weight[layer])
        + split_nt(row_sum, message_weight[layer])
    )


def middle_kernel(
    own, lower, higher, place, gradient_in, pg_in, self_weight, message_weight,
    t, prod, w, decay, slope, onehot, radius_in,
    gradient_out, pg_out, radius_out, kept, z_lower, z_higher, rows,
):
    gradient = down_step(own, lower, higher, place, gradient_in, pg_in, self_weight, message_weight, 2)
    pg, radius_grad = backward_part(
        gradient, t[...], prod, w, decay[1:2, :], slope, onehot, rows
    )
    gradient_out[...] = gradient
    pg_out[...] = pg
    radius_out[...] = radius_in[...] + radius_grad
    send_back(rows, kept, z_lower, z_higher)


def bottom_kernel(
    own, lower, higher, place, gradient_in, pg_in, self_weight, message_weight,
    t, prod, decay, slope, onehot, radius_in, unit,
    own_force, kept, z_lower, z_higher, terms, rows,
):
    gradient = down_step(own, lower, higher, place, gradient_in, pg_in, self_weight, message_weight, 1)
    activation = t[...]
    pg = gradient * (1.0 - activation * activation)
    wide = jnp.concatenate([pg.T] * (CHUNK // ATOMS), axis=1)
    rates = jnp.concatenate([columns(decay[0:1, :])] * (CHUNK // ATOMS), axis=1)
    terms[...] = jnp.zeros_like(terms)
    sums = [jnp.zeros((1, ATOMS), f32)] * 3
    for start in range(0, PAIRS, SPAN):
        for inner in range(start, start + SPAN, CHUNK):
            for i, part in enumerate(backward_sums(prod, inner, wide, rates, slope)):
                k = inner // ATOMS + i
                total = radius_in[k : k + 1, :] + part
                for n in range(3):
                    pushed = total * unit[n, k : k + 1, :]
                    sums[n] = sums[n] + pushed
                    terms[n : n + 1, k * ATOMS : (k + 1) * ATOMS] = pushed
        span = slice(start, start + SPAN)
        added = mm_nt(onehot[:, span], terms[:, span].astype(bf16))
        rows[...] = added if start == 0 else rows[...] + added
    for n in range(3):
        own_force[n : n + 1, :] = sums[n]
    padding = jnp.zeros((ROWS, C - rows.shape[1]), f32)
    send_back(jnp.concatenate([rows[...], padding], axis=1), kept, z_lower, z_higher)


def final_kernel(own, lower, higher, place, own_force, forces):
    pieces = jnp.concatenate([lower[...], higher[...]], axis=0)
    row_sum = own[...] + mm(place[...], pieces)
    forces[...] = own_force[...] - row_sum.T[0:3, :]


def spread(proj, up, down, pick_y, pick_z, ready):
    x = swap(up, down, "gx")
    sends = call(
        pick_y_kernel,
        [shape((GY, C), bf16)] * 2,
        [pltpu.VMEM((OFF_Y, C), bf16)],
    )(proj, *x, pick_y)
    y = swap(*sends, "gy")
    sends = call(
        pick_z_kernel,
        [shape((GZ, C), bf16)] * 2,
        [pltpu.VMEM((OFF_Z, C), bf16)],
    )(proj, *x, *y, pick_z, ready)
    z = swap(*sends, "gz")
    return (*x, *y, *z)


def retract(kept, z_lower, z_higher, place_y, place_z):
    higher, lower = swap(z_higher, z_lower, "gz")
    rest, y_lower, y_higher = call(
        return_z_kernel,
        [shape((UNPADDED, C), f32), shape((GY, C), bf16), shape((GY, C), bf16)],
    )(kept, lower, higher, place_z)
    higher, lower = swap(y_higher, y_lower, "gy")
    own, x_lower, x_higher = call(
        return_y_kernel,
        [shape((ATOMS, C), f32), shape((GX, C), bf16), shape((GX, C), bf16)],
    )(rest, lower, higher, place_y)
    higher, lower = swap(x_higher, x_lower, "gx")
    return own, lower, higher


def local(
    atom_types,
    type_table,
    neighbor_index,
    neighbor_count,
    displacement,
    send_x,
    send_y,
    send_z,
    message_weight,
    self_weight,
    decay,
    energy_proj,
    energy_out,
):
    inputs = (
        atom_types.reshape(1, ATOMS),
        type_table,
        send_x,
        message_weight,
        send_y,
        send_z,
        neighbor_index.T,
        neighbor_count.reshape(1, ATOMS),
        jnp.swapaxes(displacement, 1, 2),
        decay,
        self_weight,
        energy_proj,
        energy_out.reshape(1, C),
    )
    inputs = [pltpu.with_memory_space_constraint(a, pltpu.HBM) for a in inputs]
    *loaded, features, proj, up, down, pick_x, place_x = call(
        first_kernel,
        [
            *[shape(a.shape, a.dtype) for a in inputs[3:]],
            shape((ATOMS, C), bf16),
            shape((ATOMS, C), bf16),
            shape((GX, C), bf16),
            shape((GX, C), bf16),
            shape((2 * GX, ATOMS), bf16),
            shape((ATOMS, 2 * GX), bf16),
        ],
        [
            pltpu.VMEM((128, C), f32),
            *[pltpu.VMEM(a.shape, a.dtype) for a in inputs[:3]],
            pltpu.SemaphoreType.DMA((LOADED,)),
        ],
        in_specs=[pl.BlockSpec(memory_space=pltpu.HBM)] * LOADED,
    )(*inputs)
    message_weight, send_y, send_z, index, count, delta = loaded[:6]
    decay, self_weight, energy_proj, energy_row = loaded[6:]
    pick_y, pick_z, place_y, place_z = call(
        lists_kernel,
        [
            shape((2 * GY, OFF_Y), bf16),
            shape((2 * GZ, OFF_Z), bf16),
            shape((UNPADDED, 2 * GY), bf16),
            shape((OFF_Z, 2 * GZ), bf16),
        ],
    )(send_y, send_z)
    onehot = call(onehot_kernel, shape((ROWS, PAIRS), bf16))(index)
    w0, slope, unit, radius, base = call(
        radial_kernel,
        [
            shape((C, PAIRS), bf16),
            shape((SLOTS, ATOMS), f32),
            shape((3, SLOTS, ATOMS), f32),
            shape((SLOTS, ATOMS), f32),
            shape((SLOTS, ATOMS), f32),
        ],
    )(count, delta, decay)
    weights = [w0]
    for layer in (1, 2):
        body = lambda *refs, layer=layer: later_weights_kernel(*refs, layer=layer)
        weights.append(call(body, shape((C, PAIRS), bf16))(radius, base, decay))
    w0, w1, w2 = weights
    saved = []
    for layer in range(2):
        ghosts = spread(proj, up, down, pick_y, pick_z, (onehot, w1)[layer])
        body = lambda *refs, layer=layer: layer_kernel(*refs, layer=layer)
        features, t, prod, proj, up, down = call(
            body,
            [
                shape((ATOMS, C), bf16),
                shape((ATOMS, C), f32),
                shape((C, PAIRS), bf16),
                shape((ATOMS, C), bf16),
                shape((GX, C), bf16),
                shape((GX, C), bf16),
            ],
            [pltpu.VMEM((ROWS, C), bf16)],
        )(features, proj, *ghosts, onehot, weights[layer], self_weight, message_weight, pick_x)
        saved.append((t, prod))
    ghosts = spread(proj, up, down, pick_y, pick_z, w2)
    grad_shapes = [
        shape((ATOMS, C), f32),
        shape((ATOMS, C), f32),
        shape((SLOTS, ATOMS), f32),
    ]
    back_shapes = [shape((OFF_Z, C), f32), shape((GZ, C), bf16), shape((GZ, C), bf16)]
    energy, gradient, pg, radius_grad, *back = call(
        top_kernel,
        [shape((1, ATOMS), f32), *grad_shapes, *back_shapes],
        [
            pltpu.VMEM((ROWS, C), bf16),
            pltpu.VMEM((C, PAIRS), bf16),
            pltpu.VMEM((ROWS, C), f32),
        ],
    )(
        features, proj, *ghosts, onehot, w2, self_weight, energy_proj, energy_row, decay, slope,
    )
    returned = retract(*back, place_y, place_z)
    t, prod = saved[1]
    gradient, pg, radius_grad, *back = call(
        middle_kernel, [*grad_shapes, *back_shapes], [pltpu.VMEM((ROWS, C), f32)]
    )(
        *returned, place_x, gradient, pg, self_weight, message_weight, t, prod, w1, decay, slope,
        onehot, radius_grad,
    )
    returned = retract(*back, place_y, place_z)
    t, prod = saved[0]
    own_force, *back = call(
        bottom_kernel,
        [shape((3, ATOMS), f32), *back_shapes],
        [pltpu.VMEM((16, PAIRS), f32), pltpu.VMEM((ROWS, 16), f32)],
    )(
        *returned, place_x, gradient, pg, self_weight, message_weight, t, prod, decay, slope,
        onehot, radius_grad, unit,
    )
    returned = retract(*back, place_y, place_z)
    forces = call(final_kernel, shape((3, ATOMS), f32))(*returned, place_x, own_force)
    return (energy.reshape(ATOMS), forces)


def solution(mesh):
    split = ("gx", "gy", "gz")
    return jax.shard_map(
        local,
        mesh=mesh,
        in_specs=(
            P(split),
            P(),
            P(split, None),
            P(split),
            P(None, split, None),
            P(None, split),
            P(None, split),
            P(None, split),
            P(),
            P(),
            P(),
            P(),
            P(),
        ),
        out_specs=(P(split), P(None, split)),
        check_vma=False,
    )
```

```python
import math

import jax
import jax.numpy as jnp
from jax import lax
from jax.experimental import pallas as pl
from jax.experimental.pallas import tpu as pltpu
from jax.sharding import PartitionSpec as P

cutoff = 4.0
ATOMS = 128
C = 128
SLOTS = 48
GX, GY, GZ = 32, 64, 64
LOADED = 13
OFF_X, OFF_Y, OFF_Z, ROWS = 128, 256, 384, 512
PAD = 64
UNPADDED = ATOMS + 2 * GX
PAIRS = ATOMS * SLOTS
CHUNK = 256
f32, bf16, i32 = jnp.float32, jnp.bfloat16, jnp.int32
NT = (((1,), (1,)), ((), ()))


def shape(dims, dtype):
    return jax.ShapeDtypeStruct(dims, dtype)


def call(body, outs, scratch=(), limit=4, in_specs=None):
    more = {} if in_specs is None else {"in_specs": in_specs}
    return pl.pallas_call(
        body,
        out_shape=outs,
        **more,
        scratch_shapes=list(scratch),
        compiler_params=pltpu.CompilerParams(vmem_limit_bytes=limit * 1024 * 1024),
    )


def along(axis, distance):
    size = lax.axis_size(axis)
    return [(i, (i + distance) % size) for i in range(size)]


def swap(to_higher, to_lower, axis):
    from_lower = lax.ppermute(to_higher, axis, along(axis, 1))
    from_higher = lax.ppermute(to_lower, axis, along(axis, -1))
    return from_lower, from_higher


def mm(a, b):
    return jnp.dot(a, b, preferred_element_type=f32)


def mm_nt(a, b):
    return lax.dot_general(a, b, NT, preferred_element_type=f32)


def split_nt(a, b):
    high = a.astype(bf16)
    low = (a - high.astype(f32)).astype(bf16)
    return mm_nt(high, b) + mm_nt(low, b)


def columns(row):
    return jnp.broadcast_to(row, (128, row.shape[1])).T


def padded(ids):
    return jnp.where(ids >= UNPADDED, ids + PAD, ids)


def picker(lists, extent):
    ids = jnp.concatenate([columns(lists[n : n + 1, :].astype(f32)) for n in range(2)], axis=0)
    parts = []
    for start in range(0, extent, 128):
        lane = (lax.broadcasted_iota(i32, ids.shape, 1) + start).astype(f32)
        parts.append(jnp.where(ids == lane, 1.0, 0.0).astype(bf16))
    return jnp.concatenate(parts, axis=1) if len(parts) > 1 else parts[0]


def place_into(out, lists):
    n = lists.shape[1]
    sub = lax.broadcasted_iota(i32, (out.shape[0], n), 0)
    for side in range(2):
        out[:, side * n : (side + 1) * n] = jnp.where(
            sub == lists[side : side + 1, :], 1.0, 0.0
        ).astype(bf16)


def first_kernel(*refs):
    inputs, refs = refs[:LOADED], refs[LOADED:]
    kept, refs = refs[: LOADED - 3], refs[LOADED - 3 :]
    feat, proj, up, down, pick_x, place_x, rows, types, table, send_x, sems = refs
    copies = (types, table, send_x, *kept)
    weight = kept[0]
    moves = [pltpu.make_async_copy(a, b, sems.at[i]) for i, (a, b) in enumerate(zip(inputs, copies))]
    for move in moves:
        move.start()
    rows[...] = jnp.zeros_like(rows)
    for move in moves[:4]:
        move.wait()
    rows[0:6, :] = table[...].astype(f32)
    kinds = columns(types[...].astype(f32))
    lane = lax.broadcasted_iota(i32, (ATOMS, 128), 1).astype(f32)
    onehot = jnp.where(kinds == lane, 1.0, 0.0).astype(bf16)
    features = mm(onehot, rows[...].astype(bf16)).astype(bf16)
    projected = mm(features, weight[0]).astype(bf16)
    feat[...] = features
    proj[...] = projected
    pick = picker(send_x[...], ATOMS)
    place_into(place_x, send_x[...])
    pick_x[...] = pick
    chosen = mm(pick, projected).astype(bf16)
    up[...] = chosen[0:GX]
    down[...] = chosen[GX:]
    for move in moves[4:]:
        move.wait()


def lists_kernel(send_y, send_z, pick_y, pick_z, place_y, place_z):
    ids_y, ids_z = send_y[...], padded(send_z[...])
    pick_y[...] = picker(ids_y, OFF_Y)
    pick_z[...] = picker(ids_z, OFF_Z)
    place_into(place_y, ids_y)
    place_into(place_z, ids_z)


def onehot_kernel(index, onehot):
    ids = padded(index[...])
    sub = lax.broadcasted_iota(i32, (ROWS, ATOMS), 0)
    for k in range(SLOTS):
        here = slice(k * ATOMS, (k + 1) * ATOMS)
        onehot[:, here] = jnp.where(sub == ids[k : k + 1, :], 1.0, 0.0).astype(bf16)


def weights_into(out, radius, base, decay_row):
    rate = columns(-decay_row)
    for k in range(SLOTS):
        here = slice(k * ATOMS, (k + 1) * ATOMS)
        out[:, here] = (base[k : k + 1, :] * jnp.exp(rate * radius[k : k + 1, :])).astype(bf16)


def radial_kernel(count, delta, decay, w, slope, unit, radius_out, base_out):
    d = [delta[n] for n in range(3)]
    radius = jnp.sqrt(d[0] * d[0] + d[1] * d[1] + d[2] * d[2])
    slot = lax.broadcasted_iota(i32, (SLOTS, ATOMS), 0)
    alive = jnp.where(slot < count[...], 1.0, 0.0)
    half = (math.pi / (2.0 * cutoff)) * radius
    cosine, sine = jnp.cos(half), jnp.sin(half)
    base = alive * (cosine * cosine) * (1.0 / math.sqrt(SLOTS)) / radius
    slope[...] = -(math.pi / cutoff) * sine / cosine - 1.0 / radius
    for n in range(3):
        unit[n] = d[n] / radius
    radius_out[...] = radius
    base_out[...] = base
    weights_into(w, radius, base, decay[0:1, :])


def later_weights_kernel(radius, base, decay, w, *, layer):
    weights_into(w, radius[...], base[...], decay[layer : layer + 1, :])


def pick_y_kernel(proj, lower, higher, pick, ready, up, down, table):
    table[0:ATOMS] = proj[...]
    table[OFF_X : OFF_X + GX] = lower[...]
    table[OFF_X + GX : OFF_X + 2 * GX] = higher[...]
    table[OFF_X + 2 * GX : OFF_Y] = jnp.zeros((PAD, C), bf16)
    chosen = mm(pick[...], table[...]).astype(bf16)
    up[...] = chosen[0:GY]
    down[...] = chosen[GY:]


def pick_z_kernel(proj, x_lower, x_higher, y_lower, y_higher, pick, ready, up, down, table):
    table[0:ATOMS] = proj[...]
    table[OFF_X : OFF_X + GX] = x_lower[...]
    table[OFF_X + GX : OFF_X + 2 * GX] = x_higher[...]
    table[OFF_X + 2 * GX : OFF_Y] = jnp.zeros((PAD, C), bf16)
    table[OFF_Y : OFF_Y + GY] = y_lower[...]
    table[OFF_Y + GY : OFF_Z] = y_higher[...]
    chosen = mm(pick[...], table[...]).astype(bf16)
    up[...] = chosen[0:GZ]
    down[...] = chosen[GZ:]


def turned(rows):
    return rows.astype(f32).T.astype(bf16)


def low_gather_kernel(proj, x_lower, x_higher, y_lower, y_higher, onehot, low, table):
    table[0:ATOMS] = proj[...]
    table[OFF_X : OFF_X + GX] = x_lower[...]
    table[OFF_X + GX : OFF_X + 2 * GX] = x_higher[...]
    table[OFF_X + 2 * GX : OFF_Y] = jnp.zeros((PAD, C), bf16)
    table[OFF_Y : OFF_Y + GY] = y_lower[...]
    table[OFF_Y + GY : OFF_Z] = y_higher[...]
    rows = turned(table[...])
    for start in range(0, PAIRS, CHUNK):
        here = slice(start, start + CHUNK)
        low[:, here] = mm(rows, onehot[0:OFF_Z, here]).astype(bf16)


def forward_part(z_lower, z_higher, low, onehot, w, prod):
    rows = turned(jnp.concatenate([z_lower[...], z_higher[...]], axis=0))
    total = jnp.zeros((C, ATOMS), f32)
    for start in range(0, PAIRS, CHUNK):
        here = slice(start, start + CHUNK)
        gathered = mm(rows, onehot[OFF_Z:ROWS, here]) + low[:, here].astype(f32)
        m = gathered * w[:, here].astype(f32)
        prod[:, here] = m.astype(bf16)
        for inner in range(0, CHUNK, ATOMS):
            total = total + m[:, inner : inner + ATOMS]
    return total.T


def layer_kernel(
    z_lower, z_higher, low, feat, onehot, w, self_weight, next_weight, pick_x,
    new_feat, tanh_out, prod, new_proj, up, down, *, layer,
):
    preact = forward_part(z_lower, z_higher, low, onehot, w, prod)
    preact = preact + mm(feat[...], self_weight[layer])
    t = jnp.tanh(preact)
    tanh_out[...] = t
    features = (feat[...].astype(f32) + t).astype(bf16)
    new_feat[...] = features
    projected = mm(features, next_weight[layer + 1]).astype(bf16)
    new_proj[...] = projected
    chosen = mm(pick_x[...], projected).astype(bf16)
    up[...] = chosen[0:GX]
    down[...] = chosen[GX:]


def backward_sums(prod, start, wide, rates, slope):
    a = prod[:, start : start + CHUNK].astype(f32) * wide
    s1 = jnp.sum(a, axis=0, keepdims=True)
    s2 = jnp.sum(a * rates, axis=0, keepdims=True)
    out = []
    for inner in range(0, CHUNK, ATOMS):
        k = (start + inner) // ATOMS
        here = slice(inner, inner + ATOMS)
        out.append(slope[k : k + 1, :] * s1[:, here] - s2[:, here])
    return out


def wide_rows(x):
    return jnp.concatenate([x] * (CHUNK // ATOMS), axis=1)


def ghost_rows(rows, z_lower, z_higher):
    z_lower[...] = rows[0:GZ].astype(bf16)
    z_higher[...] = rows[GZ:].astype(bf16)


def terms_part(pg, w, onehot, terms, z_lower, z_higher):
    wide = wide_rows(pg.T)
    for start in range(0, PAIRS, CHUNK):
        here = slice(start, start + CHUNK)
        terms[:, here] = (w[:, here].astype(f32) * wide).astype(bf16)
    ghost_rows(mm_nt(onehot[OFF_Z:ROWS, :], terms[...]), z_lower, z_higher)


def rest_kernel(terms, onehot, kept):
    kept[...] = mm_nt(onehot[0:OFF_Z, :], terms[...])


def force_rest_kernel(terms, onehot, kept):
    rows = mm_nt(onehot[0:OFF_Z, :], terms[...])
    kept[...] = jnp.concatenate([rows, jnp.zeros((OFF_Z, C - rows.shape[1]), f32)], axis=1)


def sums_kernel(prod, pg, decay, slope, *refs, layer):
    radius_grad = refs[-1]
    wide, rates = wide_rows(pg[...].T), wide_rows(columns(decay[layer : layer + 1, :]))
    parts = []
    for start in range(0, PAIRS, CHUNK):
        parts += backward_sums(prod, start, wide, rates, slope)
    total = jnp.concatenate(parts, axis=0)
    radius_grad[...] = total + refs[0][...] if len(refs) > 1 else total


def top_kernel(
    zl, zh, low, feat, onehot, w, self_weight, energy_proj, energy_out,
    energy, gradient_out, pg_out, prod, terms, z_lower, z_higher,
):
    preact = forward_part(zl, zh, low, onehot, w, prod) + mm(feat[...], self_weight[2])
    t = jnp.tanh(preact)
    features = (feat[...].astype(f32) + t).astype(bf16)
    readout = jnp.tanh(mm(features, energy_proj[...]))
    out_row = energy_out[...]
    energy[...] = jnp.sum((readout * out_row).T, axis=0, keepdims=True)
    gradient = split_nt((1.0 - readout * readout) * out_row, energy_proj[...])
    pg = gradient * (1.0 - t * t)
    gradient_out[...] = gradient
    pg_out[...] = pg
    terms_part(pg, w, onehot, terms, z_lower, z_higher)


def return_z_kernel(kept, plus, minus, place, rest, y_lower, y_higher):
    pieces = jnp.concatenate([minus[...], plus[...]], axis=0)
    total = kept[...] + mm(place[...], pieces)
    rest[...] = total[0:UNPADDED]
    y_lower[...] = total[OFF_Y : OFF_Y + GY].astype(bf16)
    y_higher[...] = total[OFF_Y + GY : OFF_Z].astype(bf16)


def return_y_kernel(kept, plus, minus, place, *refs):
    own, x_lower, x_higher = refs[-3:]
    pieces = jnp.concatenate([minus[...], plus[...]], axis=0)
    total = kept[...] + mm(place[...], pieces)
    own[...] = total[0:ATOMS]
    x_lower[...] = total[OFF_X : OFF_X + GX].astype(bf16)
    x_higher[...] = total[OFF_X + GX :].astype(bf16)


def down_step(own, plus, minus, place, gradient, pg, self_weight, message_weight, layer):
    pieces = jnp.concatenate([minus[...], plus[...]], axis=0)
    row_sum = own[...] + mm(place[...], pieces)
    return (
        gradient[...]
        + split_nt(pg[...], self_weight[layer])
        + split_nt(row_sum, message_weight[layer])
    )


def middle_kernel(
    own, plus, minus, place, gradient_in, pg_in, self_weight, message_weight, t, w, onehot,
    gradient_out, pg_out, terms, z_lower, z_higher,
):
    gradient = down_step(own, plus, minus, place, gradient_in, pg_in, self_weight, message_weight, 2)
    activation = t[...]
    pg = gradient * (1.0 - activation * activation)
    gradient_out[...] = gradient
    pg_out[...] = pg
    terms_part(pg, w, onehot, terms, z_lower, z_higher)


def bottom_kernel(
    own, plus, minus, place, gradient_in, pg_in, self_weight, message_weight,
    t, prod, decay, slope, onehot, radius_in, unit,
    own_force, terms, z_lower, z_higher, rows,
):
    gradient = down_step(own, plus, minus, place, gradient_in, pg_in, self_weight, message_weight, 1)
    activation = t[...]
    pg = gradient * (1.0 - activation * activation)
    wide, rates = wide_rows(pg.T), wide_rows(columns(decay[0:1, :]))
    rows[...] = jnp.zeros_like(rows)
    sums = [jnp.zeros((1, ATOMS), f32)] * 3
    for start in range(0, PAIRS, CHUNK):
        for i, part in enumerate(backward_sums(prod, start, wide, rates, slope)):
            k = start // ATOMS + i
            total = radius_in[k : k + 1, :] + part
            for n in range(3):
                pushed = total * unit[n, k : k + 1, :]
                sums[n] = sums[n] + pushed
                rows[n : n + 1, k * ATOMS : (k + 1) * ATOMS] = pushed
    terms[...] = rows[...].astype(bf16)
    ghosts = mm_nt(onehot[OFF_Z:ROWS, :], terms[...])
    padding = jnp.zeros((2 * GZ, C - ghosts.shape[1]), f32)
    ghost_rows(jnp.concatenate([ghosts, padding], axis=1), z_lower, z_higher)
    for n in range(3):
        own_force[n : n + 1, :] = sums[n]


def final_kernel(own, plus, minus, place, own_force, forces):
    pieces = jnp.concatenate([minus[...], plus[...]], axis=0)
    row_sum = own[...] + mm(place[...], pieces)
    forces[...] = own_force[...] - row_sum.T[0:3, :]


def spread(proj, up, down, pick_y, pick_z, onehot, ready):
    x = swap(up, down, "gx")
    sends = call(
        pick_y_kernel,
        [shape((GY, C), bf16)] * 2,
        [pltpu.VMEM((OFF_Y, C), bf16)],
    )(proj, *x, pick_y, ready[0])
    y = swap(*sends, "gy")
    sends = call(
        pick_z_kernel,
        [shape((GZ, C), bf16)] * 2,
        [pltpu.VMEM((OFF_Z, C), bf16)],
    )(proj, *x, *y, pick_z, ready[1])
    z = swap(*sends, "gz")
    low = call(
        low_gather_kernel, shape((C, PAIRS), bf16), [pltpu.VMEM((OFF_Z, C), bf16)]
    )(proj, *x, *y, onehot)
    return (*z, low)


def retract(terms, z_lower, z_higher, onehot, place_y, place_z, rest, ready=()):
    arrived = swap(z_higher, z_lower, "gz")
    kept = call(rest, shape((OFF_Z, C), f32))(terms, onehot)
    kept, y_lower, y_higher = call(
        return_z_kernel,
        [shape((UNPADDED, C), f32), shape((GY, C), bf16), shape((GY, C), bf16)],
    )(kept, *arrived, place_z)
    arrived = swap(y_higher, y_lower, "gy")
    own, x_lower, x_higher = call(
        return_y_kernel,
        [shape((ATOMS, C), f32), shape((GX, C), bf16), shape((GX, C), bf16)],
    )(kept, *arrived, place_y, *ready)
    arrived = swap(x_higher, x_lower, "gx")
    return (own, *arrived)


def local(
    atom_types,
    type_table,
    neighbor_index,
    neighbor_count,
    displacement,
    send_x,
    send_y,
    send_z,
    message_weight,
    self_weight,
    decay,
    energy_proj,
    energy_out,
):
    inputs = (
        atom_types.reshape(1, ATOMS),
        type_table,
        send_x,
        message_weight,
        send_y,
        send_z,
        neighbor_index.T,
        neighbor_count.reshape(1, ATOMS),
        jnp.swapaxes(displacement, 1, 2),
        decay,
        self_weight,
        energy_proj,
        energy_out.reshape(1, C),
    )
    inputs = [pltpu.with_memory_space_constraint(a, pltpu.HBM) for a in inputs]
    *loaded, features, proj, up, down, pick_x, place_x = call(
        first_kernel,
        [
            *[shape(a.shape, a.dtype) for a in inputs[3:]],
            shape((ATOMS, C), bf16),
            shape((ATOMS, C), bf16),
            shape((GX, C), bf16),
            shape((GX, C), bf16),
            shape((2 * GX, ATOMS), bf16),
            shape((ATOMS, 2 * GX), bf16),
        ],
        [
            pltpu.VMEM((128, C), f32),
            *[pltpu.VMEM(a.shape, a.dtype) for a in inputs[:3]],
            pltpu.SemaphoreType.DMA((LOADED,)),
        ],
        in_specs=[pl.BlockSpec(memory_space=pltpu.HBM)] * LOADED,
    )(*inputs)
    message_weight, send_y, send_z, index, count, delta = loaded[:6]
    decay, self_weight, energy_proj, energy_row = loaded[6:]
    pick_y, pick_z, place_y, place_z = call(
        lists_kernel,
        [
            shape((2 * GY, OFF_Y), bf16),
            shape((2 * GZ, OFF_Z), bf16),
            shape((UNPADDED, 2 * GY), bf16),
            shape((OFF_Z, 2 * GZ), bf16),
        ],
    )(send_y, send_z)
    onehot = call(onehot_kernel, shape((ROWS, PAIRS), bf16))(index)
    w0, slope, unit, radius, base = call(
        radial_kernel,
        [
            shape((C, PAIRS), bf16),
            shape((SLOTS, ATOMS), f32),
            shape((3, SLOTS, ATOMS), f32),
            shape((SLOTS, ATOMS), f32),
            shape((SLOTS, ATOMS), f32),
        ],
    )(count, delta, decay)
    weights = [w0]
    for layer in (1, 2):
        body = lambda *refs, layer=layer: later_weights_kernel(*refs, layer=layer)
        weights.append(call(body, shape((C, PAIRS), bf16))(radius, base, decay))
    w0, w1, w2 = weights
    lists = (pick_y, pick_z, onehot)
    saved = []
    ready = ((w0, onehot), (pick_y, w1), (pick_y, w2))
    for layer in range(2):
        ghosts = spread(proj, up, down, *lists, ready[layer])
        body = lambda *refs, layer=layer: layer_kernel(*refs, layer=layer)
        features, t, prod, proj, up, down = call(
            body,
            [
                shape((ATOMS, C), bf16),
                shape((ATOMS, C), f32),
                shape((C, PAIRS), bf16),
                shape((ATOMS, C), bf16),
                shape((GX, C), bf16),
                shape((GX, C), bf16),
            ],
        )(*ghosts, features, onehot, weights[layer], self_weight, message_weight, pick_x)
        saved.append((t, prod))
    ghosts = spread(proj, up, down, *lists, ready[2])
    row_shapes = [shape((ATOMS, C), f32), shape((ATOMS, C), f32)]
    terms_shape = shape((C, PAIRS), bf16)
    ghost_shapes = [shape((GZ, C), bf16), shape((GZ, C), bf16)]
    radius_shape = shape((SLOTS, ATOMS), f32)
    energy, gradient, pg, prod, *back = call(
        top_kernel,
        [shape((1, ATOMS), f32), *row_shapes, terms_shape, terms_shape, *ghost_shapes],
    )(*ghosts, features, onehot, w2, self_weight, energy_proj, energy_row)
    places = (onehot, place_y, place_z)
    sums = lambda *refs: sums_kernel(*refs, layer=2)
    radius_grad = call(sums, radius_shape)(prod, pg, decay, slope)
    returned = retract(*back, *places, rest_kernel, [radius_grad])
    t, prod = saved[1]
    gradient, pg, *back = call(middle_kernel, [*row_shapes, terms_shape, *ghost_shapes])(
        *returned, place_x, gradient, pg, self_weight, message_weight, t, w1, onehot
    )
    sums = lambda *refs: sums_kernel(*refs, layer=1)
    radius_grad = call(sums, radius_shape)(prod, pg, decay, slope, radius_grad)
    returned = retract(*back, *places, rest_kernel, [radius_grad])
    t, prod = saved[0]
    own_force, *back = call(
        bottom_kernel,
        [shape((3, ATOMS), f32), shape((16, PAIRS), bf16), *ghost_shapes],
        [pltpu.VMEM((16, PAIRS), f32)],
    )(
        *returned, place_x, gradient, pg, self_weight, message_weight, t, prod, decay, slope,
        onehot, radius_grad, unit,
    )
    returned = retract(*back, *places, force_rest_kernel)
    forces = call(final_kernel, shape((3, ATOMS), f32))(*returned, place_x, own_force)
    return (energy.reshape(ATOMS), forces)


def solution(mesh):
    split = ("gx", "gy", "gz")
    return jax.shard_map(
        local,
        mesh=mesh,
        in_specs=(
            P(split),
            P(),
            P(split, None),
            P(split),
            P(None, split, None),
            P(None, split),
            P(None, split),
            P(None, split),
            P(),
            P(),
            P(),
            P(),
            P(),
        ),
        out_specs=(P(split), P(None, split)),
        check_vma=False,
    )
```

```python
import math

import jax
import jax.numpy as jnp
from jax import lax
from jax.experimental import pallas as pl
from jax.experimental.pallas import tpu as pltpu
from jax.sharding import PartitionSpec as P

cutoff = 4.0
ATOMS = 128
C = 128
SLOTS = 48
GX, GY, GZ = 32, 64, 64
LOADED = 13
OFF_X, OFF_Y, OFF_Z, ROWS = 128, 256, 384, 512
PAD = 64
UNPADDED = ATOMS + 2 * GX
PAIRS = ATOMS * SLOTS
CHUNK = 256
f32, bf16, i32 = jnp.float32, jnp.bfloat16, jnp.int32
NT = (((1,), (1,)), ((), ()))


def shape(dims, dtype):
    return jax.ShapeDtypeStruct(dims, dtype)


def call(body, outs, scratch=(), limit=4, in_specs=None):
    more = {} if in_specs is None else {"in_specs": in_specs}
    return pl.pallas_call(
        body,
        out_shape=outs,
        **more,
        scratch_shapes=list(scratch),
        compiler_params=pltpu.CompilerParams(vmem_limit_bytes=limit * 1024 * 1024),
    )


def along(axis, distance):
    size = lax.axis_size(axis)
    return [(i, (i + distance) % size) for i in range(size)]


def swap(to_higher, to_lower, axis):
    from_lower = lax.ppermute(to_higher, axis, along(axis, 1))
    from_higher = lax.ppermute(to_lower, axis, along(axis, -1))
    return from_lower, from_higher


def mm(a, b):
    return jnp.dot(a, b, preferred_element_type=f32)


def mm_nt(a, b):
    return lax.dot_general(a, b, NT, preferred_element_type=f32)


def split_nt(a, b):
    high = a.astype(bf16)
    low = (a - high.astype(f32)).astype(bf16)
    return mm_nt(high, b) + mm_nt(low, b)


def columns(row):
    return jnp.broadcast_to(row, (128, row.shape[1])).T


def padded(ids):
    return jnp.where(ids >= UNPADDED, ids + PAD, ids)


def picker(lists, extent):
    ids = jnp.concatenate([columns(lists[n : n + 1, :].astype(f32)) for n in range(2)], axis=0)
    parts = []
    for start in range(0, extent, 128):
        lane = (lax.broadcasted_iota(i32, ids.shape, 1) + start).astype(f32)
        parts.append(jnp.where(ids == lane, 1.0, 0.0).astype(bf16))
    return jnp.concatenate(parts, axis=1) if len(parts) > 1 else parts[0]


def place_into(out, lists):
    n = lists.shape[1]
    sub = lax.broadcasted_iota(i32, (out.shape[0], n), 0)
    for side in range(2):
        out[:, side * n : (side + 1) * n] = jnp.where(
            sub == lists[side : side + 1, :], 1.0, 0.0
        ).astype(bf16)


def first_kernel(*refs):
    inputs, refs = refs[:LOADED], refs[LOADED:]
    kept, refs = refs[: LOADED - 3], refs[LOADED - 3 :]
    feat, proj, up, down, pick_x, place_x, rows, types, table, send_x, sems = refs
    copies = (types, table, send_x, *kept)
    weight = kept[0]
    moves = [pltpu.make_async_copy(a, b, sems.at[i]) for i, (a, b) in enumerate(zip(inputs, copies))]
    for move in moves:
        move.start()
    rows[...] = jnp.zeros_like(rows)
    for move in moves[:4]:
        move.wait()
    rows[0:6, :] = table[...].astype(f32)
    kinds = columns(types[...].astype(f32))
    lane = lax.broadcasted_iota(i32, (ATOMS, 128), 1).astype(f32)
    onehot = jnp.where(kinds == lane, 1.0, 0.0).astype(bf16)
    per_type = rows[...].astype(bf16)
    projected = mm(per_type, weight[0]).astype(bf16)
    pick = picker(send_x[...], ATOMS)
    chosen = mm(mm(pick, onehot).astype(bf16), projected).astype(bf16)
    up[...] = chosen[0:GX]
    down[...] = chosen[GX:]
    proj[...] = mm(onehot, projected).astype(bf16)
    feat[...] = mm(onehot, per_type).astype(bf16)
    pick_x[...] = pick
    place_into(place_x, send_x[...])
    for move in moves[4:]:
        move.wait()


def lists_kernel(send_y, send_z, pick_y, pick_z, place_y, place_z):
    ids_y, ids_z = send_y[...], padded(send_z[...])
    pick_y[...] = picker(ids_y, OFF_Y)
    pick_z[...] = picker(ids_z, OFF_Z)
    place_into(place_y, ids_y)
    place_into(place_z, ids_z)


def onehot_kernel(index, onehot):
    ids = padded(index[...])
    sub = lax.broadcasted_iota(i32, (ROWS, ATOMS), 0)
    for k in range(SLOTS):
        here = slice(k * ATOMS, (k + 1) * ATOMS)
        onehot[:, here] = jnp.where(sub == ids[k : k + 1, :], 1.0, 0.0).astype(bf16)


def weights_into(out, radius, base, decay_row):
    rate = columns(-decay_row)
    for k in range(SLOTS):
        here = slice(k * ATOMS, (k + 1) * ATOMS)
        out[:, here] = (base[k : k + 1, :] * jnp.exp(rate * radius[k : k + 1, :])).astype(bf16)


def radial_kernel(count, delta, decay, w, slope, unit, radius_out, base_out):
    d = [delta[n] for n in range(3)]
    radius = jnp.sqrt(d[0] * d[0] + d[1] * d[1] + d[2] * d[2])
    slot = lax.broadcasted_iota(i32, (SLOTS, ATOMS), 0)
    alive = jnp.where(slot < count[...], 1.0, 0.0)
    half = (math.pi / (2.0 * cutoff)) * radius
    cosine, sine = jnp.cos(half), jnp.sin(half)
    base = alive * (cosine * cosine) * (1.0 / math.sqrt(SLOTS)) / radius
    slope[...] = -(math.pi / cutoff) * sine / cosine - 1.0 / radius
    for n in range(3):
        unit[n] = d[n] / radius
    radius_out[...] = radius
    base_out[...] = base
    weights_into(w, radius, base, decay[0:1, :])


def later_weights_kernel(radius, base, decay, w, *, layer):
    weights_into(w, radius[...], base[...], decay[layer : layer + 1, :])


def pick_y_kernel(proj, lower, higher, pick, ready, up, down, table):
    table[0:ATOMS] = proj[...]
    table[OFF_X : OFF_X + GX] = lower[...]
    table[OFF_X + GX : OFF_X + 2 * GX] = higher[...]
    table[OFF_X + 2 * GX : OFF_Y] = jnp.zeros((PAD, C), bf16)
    chosen = mm(pick[...], table[...]).astype(bf16)
    up[...] = chosen[0:GY]
    down[...] = chosen[GY:]


def pick_z_kernel(proj, x_lower, x_higher, y_lower, y_higher, pick, ready, up, down, table):
    table[0:ATOMS] = proj[...]
    table[OFF_X : OFF_X + GX] = x_lower[...]
    table[OFF_X + GX : OFF_X + 2 * GX] = x_higher[...]
    table[OFF_X + 2 * GX : OFF_Y] = jnp.zeros((PAD, C), bf16)
    table[OFF_Y : OFF_Y + GY] = y_lower[...]
    table[OFF_Y + GY : OFF_Z] = y_higher[...]
    chosen = mm(pick[...], table[...]).astype(bf16)
    up[...] = chosen[0:GZ]
    down[...] = chosen[GZ:]


def turned(rows):
    return rows.astype(f32).T.astype(bf16)


def low_gather_kernel(proj, x_lower, x_higher, y_lower, y_higher, onehot, low, table):
    table[0:ATOMS] = proj[...]
    table[OFF_X : OFF_X + GX] = x_lower[...]
    table[OFF_X + GX : OFF_X + 2 * GX] = x_higher[...]
    table[OFF_X + 2 * GX : OFF_Y] = jnp.zeros((PAD, C), bf16)
    table[OFF_Y : OFF_Y + GY] = y_lower[...]
    table[OFF_Y + GY : OFF_Z] = y_higher[...]
    rows = turned(table[...])
    for start in range(0, PAIRS, CHUNK):
        here = slice(start, start + CHUNK)
        low[:, here] = mm(rows, onehot[0:OFF_Z, here]).astype(bf16)


def forward_part(z_lower, z_higher, low, onehot, w, prod):
    rows = turned(jnp.concatenate([z_lower[...], z_higher[...]], axis=0))
    total = jnp.zeros((C, ATOMS), f32)
    for start in range(0, PAIRS, CHUNK):
        here = slice(start, start + CHUNK)
        gathered = mm(rows, onehot[OFF_Z:ROWS, here]).astype(bf16) + low[:, here]
        m = gathered * w[:, here]
        prod[:, here] = m
        for inner in range(0, CHUNK, ATOMS):
            total = total + m[:, inner : inner + ATOMS].astype(f32)
    return total.T


def layer_kernel(
    z_lower, z_higher, low, feat, onehot, w, self_weight, next_weight, pick_x,
    new_feat, tanh_out, prod, new_proj, up, down, *, layer,
):
    preact = forward_part(z_lower, z_higher, low, onehot, w, prod)
    preact = preact + mm(feat[...], self_weight[layer])
    t = jnp.tanh(preact)
    tanh_out[...] = t
    features = (feat[...].astype(f32) + t).astype(bf16)
    new_feat[...] = features
    projected = mm(features, next_weight[layer + 1]).astype(bf16)
    new_proj[...] = projected
    chosen = mm(pick_x[...], projected).astype(bf16)
    up[...] = chosen[0:GX]
    down[...] = chosen[GX:]


def sum_rows(decay_row):
    high = decay_row.astype(bf16).astype(f32)
    rows = [jnp.ones_like(decay_row), high, decay_row - high, jnp.zeros((13, C), f32)]
    return jnp.concatenate(rows, axis=0).astype(bf16)


def backward_sums(prod, start, wide, rows, slope):
    s = mm(rows, prod[:, start : start + CHUNK] * wide)
    out = []
    for inner in range(0, CHUNK, ATOMS):
        k = (start + inner) // ATOMS
        here = slice(inner, inner + ATOMS)
        out.append(slope[k : k + 1, :] * s[0:1, here] - (s[1:2, here] + s[2:3, here]))
    return out


def wide_rows(x):
    return jnp.concatenate([x] * (CHUNK // ATOMS), axis=1)


def ghost_rows(rows, z_lower, z_higher):
    z_lower[...] = rows[0:GZ].astype(bf16)
    z_higher[...] = rows[GZ:].astype(bf16)


def terms_part(pg, w, onehot, terms, z_lower, z_higher):
    wide = wide_rows(pg.T.astype(bf16))
    for start in range(0, PAIRS, CHUNK):
        here = slice(start, start + CHUNK)
        terms[:, here] = w[:, here] * wide
    ghost_rows(mm_nt(onehot[OFF_Z:ROWS, :], terms[...]), z_lower, z_higher)


def rest_kernel(terms, onehot, kept):
    kept[...] = mm_nt(onehot[0:OFF_Z, :], terms[...])


def force_rest_kernel(terms, onehot, kept):
    rows = mm_nt(onehot[0:OFF_Z, :], terms[...])
    kept[...] = jnp.concatenate([rows, jnp.zeros((OFF_Z, C - rows.shape[1]), f32)], axis=1)


def sums_kernel(prod, pg, decay, slope, *refs, layer):
    wide, rows = wide_rows(pg[...].T.astype(bf16)), sum_rows(decay[layer : layer + 1, :])
    parts = []
    for start in range(0, PAIRS, CHUNK):
        parts += backward_sums(prod, start, wide, rows, slope)
    total = jnp.concatenate(parts, axis=0)
    if layer == 2:
        readout, out_row, radius_grad, energy = refs
        energy[...] = jnp.sum((readout[...] * out_row[...]).T, axis=0, keepdims=True)
        radius_grad[...] = total
    else:
        before, radius_grad = refs
        radius_grad[...] = before[...] + total


def top_kernel(
    zl, zh, low, feat, onehot, w, self_weight, energy_proj, energy_out,
    readout_out, gradient_out, pg_out, prod, terms, z_lower, z_higher,
):
    preact = forward_part(zl, zh, low, onehot, w, prod) + mm(feat[...], self_weight[2])
    t = jnp.tanh(preact)
    features = (feat[...].astype(f32) + t).astype(bf16)
    readout = jnp.tanh(mm(features, energy_proj[...]))
    out_row = energy_out[...]
    readout_out[...] = readout
    gradient = split_nt((1.0 - readout * readout) * out_row, energy_proj[...])
    pg = gradient * (1.0 - t * t)
    gradient_out[...] = gradient
    pg_out[...] = pg
    terms_part(pg, w, onehot, terms, z_lower, z_higher)


def return_z_kernel(kept, plus, minus, place, rest, y_lower, y_higher):
    pieces = jnp.concatenate([minus[...], plus[...]], axis=0)
    total = kept[...] + mm(place[...], pieces)
    rest[...] = total[0:UNPADDED]
    y_lower[...] = total[OFF_Y : OFF_Y + GY].astype(bf16)
    y_higher[...] = total[OFF_Y + GY : OFF_Z].astype(bf16)


def return_y_kernel(kept, plus, minus, place, *refs):
    own, x_lower, x_higher = refs[-3:]
    pieces = jnp.concatenate([minus[...], plus[...]], axis=0)
    total = kept[...] + mm(place[...], pieces)
    own[...] = total[0:ATOMS]
    x_lower[...] = total[OFF_X : OFF_X + GX].astype(bf16)
    x_higher[...] = total[OFF_X + GX :].astype(bf16)


def down_step(own, plus, minus, place, gradient, pg, self_weight, message_weight, layer):
    pieces = jnp.concatenate([minus[...], plus[...]], axis=0)
    row_sum = own[...] + mm(place[...], pieces)
    return (
        gradient[...]
        + split_nt(pg[...], self_weight[layer])
        + split_nt(row_sum, message_weight[layer])
    )


def middle_kernel(
    own, plus, minus, place, gradient_in, pg_in, self_weight, message_weight, t, w, onehot,
    gradient_out, pg_out, terms, z_lower, z_higher,
):
    gradient = down_step(own, plus, minus, place, gradient_in, pg_in, self_weight, message_weight, 2)
    activation = t[...]
    pg = gradient * (1.0 - activation * activation)
    gradient_out[...] = gradient
    pg_out[...] = pg
    terms_part(pg, w, onehot, terms, z_lower, z_higher)


def bottom_kernel(
    own, plus, minus, place, gradient_in, pg_in, self_weight, message_weight,
    t, prod, decay, slope, onehot, radius_in, unit,
    own_force, terms, z_lower, z_higher, rows,
):
    gradient = down_step(own, plus, minus, place, gradient_in, pg_in, self_weight, message_weight, 1)
    activation = t[...]
    pg = gradient * (1.0 - activation * activation)
    wide, weighted = wide_rows(pg.T.astype(bf16)), sum_rows(decay[0:1, :])
    rows[...] = jnp.zeros_like(rows)
    sums = [jnp.zeros((1, ATOMS), f32)] * 3
    for start in range(0, PAIRS, CHUNK):
        for i, part in enumerate(backward_sums(prod, start, wide, weighted, slope)):
            k = start // ATOMS + i
            total = radius_in[k : k + 1, :] + part
            for n in range(3):
                pushed = total * unit[n, k : k + 1, :]
                sums[n] = sums[n] + pushed
                rows[n : n + 1, k * ATOMS : (k + 1) * ATOMS] = pushed
    terms[...] = rows[...].astype(bf16)
    ghosts = mm_nt(onehot[OFF_Z:ROWS, :], terms[...])
    padding = jnp.zeros((2 * GZ, C - ghosts.shape[1]), f32)
    ghost_rows(jnp.concatenate([ghosts, padding], axis=1), z_lower, z_higher)
    for n in range(3):
        own_force[n : n + 1, :] = sums[n]


def final_kernel(own, plus, minus, place, own_force, forces):
    pieces = jnp.concatenate([minus[...], plus[...]], axis=0)
    row_sum = own[...] + mm(place[...], pieces)
    forces[...] = own_force[...] - row_sum.T[0:3, :]


def spread(proj, up, down, pick_y, pick_z, onehot, ready):
    x = swap(up, down, "gx")
    sends = call(
        pick_y_kernel,
        [shape((GY, C), bf16)] * 2,
        [pltpu.VMEM((OFF_Y, C), bf16)],
    )(proj, *x, pick_y, ready[0])
    y = swap(*sends, "gy")
    sends = call(
        pick_z_kernel,
        [shape((GZ, C), bf16)] * 2,
        [pltpu.VMEM((OFF_Z, C), bf16)],
    )(proj, *x, *y, pick_z, ready[1])
    z = swap(*sends, "gz")
    low = call(
        low_gather_kernel, shape((C, PAIRS), bf16), [pltpu.VMEM((OFF_Z, C), bf16)]
    )(proj, *x, *y, onehot)
    return (*z, low)


def retract(terms, z_lower, z_higher, onehot, place_y, place_z, rest, ready=()):
    arrived = swap(z_higher, z_lower, "gz")
    kept = call(rest, shape((OFF_Z, C), f32))(terms, onehot)
    kept, y_lower, y_higher = call(
        return_z_kernel,
        [shape((UNPADDED, C), f32), shape((GY, C), bf16), shape((GY, C), bf16)],
    )(kept, *arrived, place_z)
    arrived = swap(y_higher, y_lower, "gy")
    own, x_lower, x_higher = call(
        return_y_kernel,
        [shape((ATOMS, C), f32), shape((GX, C), bf16), shape((GX, C), bf16)],
    )(kept, *arrived, place_y, *ready)
    arrived = swap(x_higher, x_lower, "gx")
    return (own, *arrived)


def local(
    atom_types,
    type_table,
    neighbor_index,
    neighbor_count,
    displacement,
    send_x,
    send_y,
    send_z,
    message_weight,
    self_weight,
    decay,
    energy_proj,
    energy_out,
):
    inputs = (
        atom_types.reshape(1, ATOMS),
        type_table,
        send_x,
        message_weight,
        send_y,
        send_z,
        neighbor_index.T,
        neighbor_count.reshape(1, ATOMS),
        jnp.swapaxes(displacement, 1, 2),
        decay,
        self_weight,
        energy_proj,
        energy_out.reshape(1, C),
    )
    inputs = [pltpu.with_memory_space_constraint(a, pltpu.HBM) for a in inputs]
    *loaded, features, proj, up, down, pick_x, place_x = call(
        first_kernel,
        [
            *[shape(a.shape, a.dtype) for a in inputs[3:]],
            shape((ATOMS, C), bf16),
            shape((ATOMS, C), bf16),
            shape((GX, C), bf16),
            shape((GX, C), bf16),
            shape((2 * GX, ATOMS), bf16),
            shape((ATOMS, 2 * GX), bf16),
        ],
        [
            pltpu.VMEM((128, C), f32),
            *[pltpu.VMEM(a.shape, a.dtype) for a in inputs[:3]],
            pltpu.SemaphoreType.DMA((LOADED,)),
        ],
        in_specs=[pl.BlockSpec(memory_space=pltpu.HBM)] * LOADED,
    )(*inputs)
    message_weight, send_y, send_z, index, count, delta = loaded[:6]
    decay, self_weight, energy_proj, energy_row = loaded[6:]
    pick_y, pick_z, place_y, place_z = call(
        lists_kernel,
        [
            shape((2 * GY, OFF_Y), bf16),
            shape((2 * GZ, OFF_Z), bf16),
            shape((UNPADDED, 2 * GY), bf16),
            shape((OFF_Z, 2 * GZ), bf16),
        ],
    )(send_y, send_z)
    onehot = call(onehot_kernel, shape((ROWS, PAIRS), bf16))(index)
    w0, slope, unit, radius, base = call(
        radial_kernel,
        [
            shape((C, PAIRS), bf16),
            shape((SLOTS, ATOMS), f32),
            shape((3, SLOTS, ATOMS), f32),
            shape((SLOTS, ATOMS), f32),
            shape((SLOTS, ATOMS), f32),
        ],
    )(count, delta, decay)
    weights = [w0]
    for layer in (1, 2):
        body = lambda *refs, layer=layer: later_weights_kernel(*refs, layer=layer)
        weights.append(call(body, shape((C, PAIRS), bf16))(radius, base, decay))
    w0, w1, w2 = weights
    lists = (pick_y, pick_z, onehot)
    saved = []
    ready = ((w0, onehot), (pick_y, w1), (pick_y, w2))
    for layer in range(2):
        ghosts = spread(proj, up, down, *lists, ready[layer])
        body = lambda *refs, layer=layer: layer_kernel(*refs, layer=layer)
        features, t, prod, proj, up, down = call(
            body,
            [
                shape((ATOMS, C), bf16),
                shape((ATOMS, C), f32),
                shape((C, PAIRS), bf16),
                shape((ATOMS, C), bf16),
                shape((GX, C), bf16),
                shape((GX, C), bf16),
            ],
        )(*ghosts, features, onehot, weights[layer], self_weight, message_weight, pick_x)
        saved.append((t, prod))
    ghosts = spread(proj, up, down, *lists, ready[2])
    row_shapes = [shape((ATOMS, C), f32), shape((ATOMS, C), f32)]
    terms_shape = shape((C, PAIRS), bf16)
    ghost_shapes = [shape((GZ, C), bf16), shape((GZ, C), bf16)]
    radius_shape = shape((SLOTS, ATOMS), f32)
    readout, gradient, pg, prod, *back = call(
        top_kernel,
        [shape((ATOMS, C), f32), *row_shapes, terms_shape, terms_shape, *ghost_shapes],
    )(*ghosts, features, onehot, w2, self_weight, energy_proj, energy_row)
    places = (onehot, place_y, place_z)
    sums = lambda *refs: sums_kernel(*refs, layer=2)
    radius_grad, energy = call(sums, [radius_shape, shape((1, ATOMS), f32)])(
        prod, pg, decay, slope, readout, energy_row
    )
    returned = retract(*back, *places, rest_kernel, [radius_grad])
    t, prod = saved[1]
    gradient, pg, *back = call(middle_kernel, [*row_shapes, terms_shape, *ghost_shapes])(
        *returned, place_x, gradient, pg, self_weight, message_weight, t, w1, onehot
    )
    sums = lambda *refs: sums_kernel(*refs, layer=1)
    radius_grad = call(sums, radius_shape)(prod, pg, decay, slope, radius_grad)
    returned = retract(*back, *places, rest_kernel, [radius_grad])
    t, prod = saved[0]
    own_force, *back = call(
        bottom_kernel,
        [shape((3, ATOMS), f32), shape((16, PAIRS), bf16), *ghost_shapes],
        [pltpu.VMEM((16, PAIRS), f32)],
    )(
        *returned, place_x, gradient, pg, self_weight, message_weight, t, prod, decay, slope,
        onehot, radius_grad, unit,
    )
    returned = retract(*back, *places, force_rest_kernel)
    forces = call(final_kernel, shape((3, ATOMS), f32))(*returned, place_x, own_force)
    return (energy.reshape(ATOMS), forces)


def solution(mesh):
    split = ("gx", "gy", "gz")
    return jax.shard_map(
        local,
        mesh=mesh,
        in_specs=(
            P(split),
            P(),
            P(split, None),
            P(split),
            P(None, split, None),
            P(None, split),
            P(None, split),
            P(None, split),
            P(),
            P(),
            P(),
            P(),
            P(),
        ),
        out_specs=(P(split), P(None, split)),
        check_vma=False,
    )
```

```python
import math

import jax
import jax.numpy as jnp
from jax import lax
from jax.experimental import pallas as pl
from jax.experimental.pallas import tpu as pltpu
from jax.sharding import PartitionSpec as P

cutoff = 4.0
ATOMS = 128
C = 128
SLOTS = 48
GX, GY, GZ = 32, 64, 64
LOADED = 13
OFF_X, OFF_Y, OFF_Z, ROWS = 128, 256, 384, 512
PAD = 64
UNPADDED = ATOMS + 2 * GX
PAIRS = ATOMS * SLOTS
CHUNK = 256
f32, bf16, i32 = jnp.float32, jnp.bfloat16, jnp.int32
NT = (((1,), (1,)), ((), ()))


def shape(dims, dtype):
    return jax.ShapeDtypeStruct(dims, dtype)


def call(body, outs, scratch=(), limit=4, in_specs=None):
    more = {} if in_specs is None else {"in_specs": in_specs}
    return pl.pallas_call(
        body,
        out_shape=outs,
        **more,
        scratch_shapes=list(scratch),
        compiler_params=pltpu.CompilerParams(vmem_limit_bytes=limit * 1024 * 1024),
    )


def along(axis, distance):
    size = lax.axis_size(axis)
    return [(i, (i + distance) % size) for i in range(size)]


def swap(to_higher, to_lower, axis):
    from_lower = lax.ppermute(to_higher, axis, along(axis, 1))
    from_higher = lax.ppermute(to_lower, axis, along(axis, -1))
    return from_lower, from_higher


def trade(first, second, axis):
    size = lax.axis_size(axis)
    out = []
    for block, odd in ((first, 0), (second, 1)):
        route = [(i, (i + (1 if i % 2 == odd else -1)) % size) for i in range(size)]
        out.append(lax.ppermute(block, axis, route))
    return out


def odd_in(axis):
    return lax.rem(lax.axis_index(axis), 2) == 1


def mm(a, b):
    return jnp.dot(a, b, preferred_element_type=f32)


def mm_nt(a, b):
    return lax.dot_general(a, b, NT, preferred_element_type=f32)


def split_nt(a, b):
    high = a.astype(bf16)
    low = (a - high.astype(f32)).astype(bf16)
    return mm_nt(high, b) + mm_nt(low, b)


def columns(row):
    return jnp.broadcast_to(row, (128, row.shape[1])).T


def padded(ids):
    return jnp.where(ids >= UNPADDED, ids + PAD, ids)


def picker(lists, extent):
    ids = jnp.concatenate([columns(lists[n : n + 1, :].astype(f32)) for n in range(2)], axis=0)
    parts = []
    for start in range(0, extent, 128):
        lane = (lax.broadcasted_iota(i32, ids.shape, 1) + start).astype(f32)
        parts.append(jnp.where(ids == lane, 1.0, 0.0).astype(bf16))
    return jnp.concatenate(parts, axis=1) if len(parts) > 1 else parts[0]


def place_into(out, lists):
    n = lists.shape[1]
    sub = lax.broadcasted_iota(i32, (out.shape[0], n), 0)
    for side in range(2):
        out[:, side * n : (side + 1) * n] = jnp.where(
            sub == lists[side : side + 1, :], 1.0, 0.0
        ).astype(bf16)


def first_kernel(*refs):
    inputs, refs = refs[:LOADED], refs[LOADED:]
    kept, refs = refs[: LOADED - 3], refs[LOADED - 3 :]
    feat, proj, up, down, pick_x, place_x, rows, types, table, send_x, sems = refs
    copies = (types, table, send_x, *kept)
    weight = kept[0]
    moves = [pltpu.make_async_copy(a, b, sems.at[i]) for i, (a, b) in enumerate(zip(inputs, copies))]
    for move in moves:
        move.start()
    rows[...] = jnp.zeros_like(rows)
    for move in moves[:4]:
        move.wait()
    rows[0:6, :] = table[...].astype(f32)
    kinds = columns(types[...].astype(f32))
    lane = lax.broadcasted_iota(i32, (ATOMS, 128), 1).astype(f32)
    onehot = jnp.where(kinds == lane, 1.0, 0.0).astype(bf16)
    per_type = rows[...].astype(bf16)
    projected = mm(per_type, weight[0]).astype(bf16)
    pick = picker(send_x[...], ATOMS)
    chosen = mm(mm(pick, onehot).astype(bf16), projected).astype(bf16)
    up[...] = chosen[0:GX]
    down[...] = chosen[GX:]
    proj[...] = mm(onehot, projected).astype(bf16)
    feat[...] = mm(onehot, per_type).astype(bf16)
    pick_x[...] = pick
    place_into(place_x, send_x[...])
    for move in moves[4:]:
        move.wait()


def lists_kernel(send_y, send_z, pick_y, pick_z, place_y, place_z):
    ids_y, ids_z = send_y[...], padded(send_z[...])
    turned_z = jnp.concatenate([ids_z[1:2, :], ids_z[0:1, :]], axis=0)
    ids_z = jnp.where(odd_in("gz"), turned_z, ids_z)
    pick_y[...] = picker(ids_y, OFF_Y)
    pick_z[...] = picker(ids_z, OFF_Z)
    place_into(place_y, ids_y)
    place_into(place_z, ids_z)


def onehot_kernel(index, onehot):
    ids = padded(index[...])
    other = jnp.where(ids >= OFF_Z + GZ, ids - GZ, ids + GZ)
    ids = jnp.where((ids < OFF_Z) | odd_in("gz"), ids, other)
    sub = lax.broadcasted_iota(i32, (ROWS, ATOMS), 0)
    for k in range(SLOTS):
        here = slice(k * ATOMS, (k + 1) * ATOMS)
        onehot[:, here] = jnp.where(sub == ids[k : k + 1, :], 1.0, 0.0).astype(bf16)


def weights_into(out, radius, base, decay_row):
    rate = columns(-decay_row)
    for k in range(SLOTS):
        here = slice(k * ATOMS, (k + 1) * ATOMS)
        out[:, here] = (base[k : k + 1, :] * jnp.exp(rate * radius[k : k + 1, :])).astype(bf16)


def radial_kernel(count, delta, decay, w, slope, unit, radius_out, base_out):
    d = [delta[n] for n in range(3)]
    radius = jnp.sqrt(d[0] * d[0] + d[1] * d[1] + d[2] * d[2])
    slot = lax.broadcasted_iota(i32, (SLOTS, ATOMS), 0)
    alive = jnp.where(slot < count[...], 1.0, 0.0)
    half = (math.pi / (2.0 * cutoff)) * radius
    cosine, sine = jnp.cos(half), jnp.sin(half)
    base = alive * (cosine * cosine) * (1.0 / math.sqrt(SLOTS)) / radius
    slope[...] = -(math.pi / cutoff) * sine / cosine - 1.0 / radius
    for n in range(3):
        unit[n] = d[n] / radius
    radius_out[...] = radius
    base_out[...] = base
    weights_into(w, radius, base, decay[0:1, :])


def later_weights_kernel(radius, base, decay, w, *, layer):
    weights_into(w, radius[...], base[...], decay[layer : layer + 1, :])


def pick_y_kernel(proj, lower, higher, pick, ready, up, down, table):
    table[0:ATOMS] = proj[...]
    table[OFF_X : OFF_X + GX] = lower[...]
    table[OFF_X + GX : OFF_X + 2 * GX] = higher[...]
    table[OFF_X + 2 * GX : OFF_Y] = jnp.zeros((PAD, C), bf16)
    chosen = mm(pick[...], table[...]).astype(bf16)
    up[...] = chosen[0:GY]
    down[...] = chosen[GY:]


def pick_z_kernel(proj, x_lower, x_higher, y_lower, y_higher, pick, ready, up, down, table):
    table[0:ATOMS] = proj[...]
    table[OFF_X : OFF_X + GX] = x_lower[...]
    table[OFF_X + GX : OFF_X + 2 * GX] = x_higher[...]
    table[OFF_X + 2 * GX : OFF_Y] = jnp.zeros((PAD, C), bf16)
    table[OFF_Y : OFF_Y + GY] = y_lower[...]
    table[OFF_Y + GY : OFF_Z] = y_higher[...]
    chosen = mm(pick[...], table[...]).astype(bf16)
    up[...] = chosen[0:GZ]
    down[...] = chosen[GZ:]


def turned(rows):
    return rows.astype(f32).T.astype(bf16)


def low_gather_kernel(proj, x_lower, x_higher, y_lower, y_higher, onehot, low, table):
    table[0:ATOMS] = proj[...]
    table[OFF_X : OFF_X + GX] = x_lower[...]
    table[OFF_X + GX : OFF_X + 2 * GX] = x_higher[...]
    table[OFF_X + 2 * GX : OFF_Y] = jnp.zeros((PAD, C), bf16)
    table[OFF_Y : OFF_Y + GY] = y_lower[...]
    table[OFF_Y + GY : OFF_Z] = y_higher[...]
    rows = turned(table[...])
    for start in range(0, PAIRS, CHUNK):
        here = slice(start, start + CHUNK)
        low[:, here] = mm(rows, onehot[0:OFF_Z, here]).astype(bf16)


def forward_part(z_first, z_second, low, onehot, w, prod):
    rows = turned(jnp.concatenate([z_first[...], z_second[...]], axis=0))
    total = jnp.zeros((C, ATOMS), f32)
    for start in range(0, PAIRS, CHUNK):
        here = slice(start, start + CHUNK)
        gathered = mm(rows, onehot[OFF_Z:ROWS, here]).astype(bf16) + low[:, here]
        m = gathered * w[:, here]
        prod[:, here] = m
        for inner in range(0, CHUNK, ATOMS):
            total = total + m[:, inner : inner + ATOMS].astype(f32)
    return total.T


def layer_kernel(
    z_first, z_second, low, feat, onehot, w, self_weight, next_weight, pick_x,
    new_feat, tanh_out, prod, new_proj, up, down, *, layer,
):
    preact = forward_part(z_first, z_second, low, onehot, w, prod)
    preact = preact + mm(feat[...], self_weight[layer])
    t = jnp.tanh(preact)
    tanh_out[...] = t
    features = (feat[...].astype(f32) + t).astype(bf16)
    new_feat[...] = features
    projected = mm(features, next_weight[layer + 1]).astype(bf16)
    new_proj[...] = projected
    chosen = mm(pick_x[...], projected).astype(bf16)
    up[...] = chosen[0:GX]
    down[...] = chosen[GX:]


def sum_rows(decay_row):
    high = decay_row.astype(bf16).astype(f32)
    rows = [jnp.ones_like(decay_row), high, decay_row - high, jnp.zeros((13, C), f32)]
    return jnp.concatenate(rows, axis=0).astype(bf16)


def backward_sums(prod, start, wide, rows, slope):
    s = mm(rows, prod[:, start : start + CHUNK] * wide)
    out = []
    for inner in range(0, CHUNK, ATOMS):
        k = (start + inner) // ATOMS
        here = slice(inner, inner + ATOMS)
        out.append(slope[k : k + 1, :] * s[0:1, here] - (s[1:2, here] + s[2:3, here]))
    return out


def wide_rows(x):
    return jnp.concatenate([x] * (CHUNK // ATOMS), axis=1)


def ghost_rows(rows, z_first, z_second):
    z_first[...] = rows[0:GZ].astype(bf16)
    z_second[...] = rows[GZ:].astype(bf16)


def terms_part(pg, w, onehot, terms, z_first, z_second):
    wide = wide_rows(pg.T.astype(bf16))
    for start in range(0, PAIRS, CHUNK):
        here = slice(start, start + CHUNK)
        terms[:, here] = w[:, here] * wide
    ghost_rows(mm_nt(onehot[OFF_Z:ROWS, :], terms[...]), z_first, z_second)


def rest_kernel(terms, onehot, kept):
    kept[...] = mm_nt(onehot[0:OFF_Z, :], terms[...])


def force_rest_kernel(terms, onehot, kept):
    rows = mm_nt(onehot[0:OFF_Z, :], terms[...])
    kept[...] = jnp.concatenate([rows, jnp.zeros((OFF_Z, C - rows.shape[1]), f32)], axis=1)


def sums_kernel(prod, pg, decay, slope, *refs, layer):
    wide, rows = wide_rows(pg[...].T.astype(bf16)), sum_rows(decay[layer : layer + 1, :])
    parts = []
    for start in range(0, PAIRS, CHUNK):
        parts += backward_sums(prod, start, wide, rows, slope)
    total = jnp.concatenate(parts, axis=0)
    if layer == 2:
        readout, out_row, radius_grad, energy = refs
        energy[...] = jnp.sum((readout[...] * out_row[...]).T, axis=0, keepdims=True)
        radius_grad[...] = total
    else:
        before, radius_grad = refs
        radius_grad[...] = before[...] + total


def top_kernel(
    zl, zh, low, feat, onehot, w, self_weight, energy_proj, energy_out,
    readout_out, gradient_out, pg_out, prod, terms, z_first, z_second,
):
    preact = forward_part(zl, zh, low, onehot, w, prod) + mm(feat[...], self_weight[2])
    t = jnp.tanh(preact)
    features = (feat[...].astype(f32) + t).astype(bf16)
    readout = jnp.tanh(mm(features, energy_proj[...]))
    out_row = energy_out[...]
    readout_out[...] = readout
    gradient = split_nt((1.0 - readout * readout) * out_row, energy_proj[...])
    pg = gradient * (1.0 - t * t)
    gradient_out[...] = gradient
    pg_out[...] = pg
    terms_part(pg, w, onehot, terms, z_first, z_second)


def return_z_kernel(kept, first, second, place, rest, y_lower, y_higher):
    pieces = jnp.concatenate([first[...], second[...]], axis=0)
    total = kept[...] + mm(place[...], pieces)
    rest[...] = total[0:UNPADDED]
    y_lower[...] = total[OFF_Y : OFF_Y + GY].astype(bf16)
    y_higher[...] = total[OFF_Y + GY : OFF_Z].astype(bf16)


def return_y_kernel(kept, plus, minus, place, *refs):
    own, x_lower, x_higher = refs[-3:]
    pieces = jnp.concatenate([minus[...], plus[...]], axis=0)
    total = kept[...] + mm(place[...], pieces)
    own[...] = total[0:ATOMS]
    x_lower[...] = total[OFF_X : OFF_X + GX].astype(bf16)
    x_higher[...] = total[OFF_X + GX :].astype(bf16)


def down_step(own, plus, minus, place, gradient, pg, self_weight, message_weight, layer):
    pieces = jnp.concatenate([minus[...], plus[...]], axis=0)
    row_sum = own[...] + mm(place[...], pieces)
    return (
        gradient[...]
        + split_nt(pg[...], self_weight[layer])
        + split_nt(row_sum, message_weight[layer])
    )


def middle_kernel(
    own, plus, minus, place, gradient_in, pg_in, self_weight, message_weight, t, w, onehot,
    gradient_out, pg_out, terms, z_first, z_second,
):
    gradient = down_step(own, plus, minus, place, gradient_in, pg_in, self_weight, message_weight, 2)
    activation = t[...]
    pg = gradient * (1.0 - activation * activation)
    gradient_out[...] = gradient
    pg_out[...] = pg
    terms_part(pg, w, onehot, terms, z_first, z_second)


def bottom_kernel(
    own, plus, minus, place, gradient_in, pg_in, self_weight, message_weight,
    t, prod, decay, slope, onehot, radius_in, unit,
    own_force, terms, z_first, z_second, rows,
):
    gradient = down_step(own, plus, minus, place, gradient_in, pg_in, self_weight, message_weight, 1)
    activation = t[...]
    pg = gradient * (1.0 - activation * activation)
    wide, weighted = wide_rows(pg.T.astype(bf16)), sum_rows(decay[0:1, :])
    rows[...] = jnp.zeros_like(rows)
    sums = [jnp.zeros((1, ATOMS), f32)] * 3
    for start in range(0, PAIRS, CHUNK):
        for i, part in enumerate(backward_sums(prod, start, wide, weighted, slope)):
            k = start // ATOMS + i
            total = radius_in[k : k + 1, :] + part
            for n in range(3):
                pushed = total * unit[n, k : k + 1, :]
                sums[n] = sums[n] + pushed
                rows[n : n + 1, k * ATOMS : (k + 1) * ATOMS] = pushed
    terms[...] = rows[...].astype(bf16)
    ghosts = mm_nt(onehot[OFF_Z:ROWS, :], terms[...])
    padding = jnp.zeros((2 * GZ, C - ghosts.shape[1]), f32)
    ghost_rows(jnp.concatenate([ghosts, padding], axis=1), z_first, z_second)
    for n in range(3):
        own_force[n : n + 1, :] = sums[n]


def final_kernel(own, plus, minus, place, own_force, forces):
    pieces = jnp.concatenate([minus[...], plus[...]], axis=0)
    row_sum = own[...] + mm(place[...], pieces)
    forces[...] = own_force[...] - row_sum.T[0:3, :]


def spread(proj, up, down, pick_y, pick_z, onehot, ready):
    x = swap(up, down, "gx")
    sends = call(
        pick_y_kernel,
        [shape((GY, C), bf16)] * 2,
        [pltpu.VMEM((OFF_Y, C), bf16)],
    )(proj, *x, pick_y, ready[0])
    y = swap(*sends, "gy")
    sends = call(
        pick_z_kernel,
        [shape((GZ, C), bf16)] * 2,
        [pltpu.VMEM((OFF_Z, C), bf16)],
    )(proj, *x, *y, pick_z, ready[1])
    z = trade(*sends, "gz")
    low = call(
        low_gather_kernel, shape((C, PAIRS), bf16), [pltpu.VMEM((OFF_Z, C), bf16)]
    )(proj, *x, *y, onehot)
    return (*z, low)


def retract(terms, z_first, z_second, onehot, place_y, place_z, rest, ready=()):
    arrived = trade(z_first, z_second, "gz")
    kept = call(rest, shape((OFF_Z, C), f32))(terms, onehot)
    kept, y_lower, y_higher = call(
        return_z_kernel,
        [shape((UNPADDED, C), f32), shape((GY, C), bf16), shape((GY, C), bf16)],
    )(kept, *arrived, place_z)
    arrived = swap(y_higher, y_lower, "gy")
    own, x_lower, x_higher = call(
        return_y_kernel,
        [shape((ATOMS, C), f32), shape((GX, C), bf16), shape((GX, C), bf16)],
    )(kept, *arrived, place_y, *ready)
    arrived = swap(x_higher, x_lower, "gx")
    return (own, *arrived)


def local(
    atom_types,
    type_table,
    neighbor_index,
    neighbor_count,
    displacement,
    send_x,
    send_y,
    send_z,
    message_weight,
    self_weight,
    decay,
    energy_proj,
    energy_out,
):
    inputs = (
        atom_types.reshape(1, ATOMS),
        type_table,
        send_x,
        message_weight,
        send_y,
        send_z,
        neighbor_index.T,
        neighbor_count.reshape(1, ATOMS),
        jnp.swapaxes(displacement, 1, 2),
        decay,
        self_weight,
        energy_proj,
        energy_out.reshape(1, C),
    )
    inputs = [pltpu.with_memory_space_constraint(a, pltpu.HBM) for a in inputs]
    *loaded, features, proj, up, down, pick_x, place_x = call(
        first_kernel,
        [
            *[shape(a.shape, a.dtype) for a in inputs[3:]],
            shape((ATOMS, C), bf16),
            shape((ATOMS, C), bf16),
            shape((GX, C), bf16),
            shape((GX, C), bf16),
            shape((2 * GX, ATOMS), bf16),
            shape((ATOMS, 2 * GX), bf16),
        ],
        [
            pltpu.VMEM((128, C), f32),
            *[pltpu.VMEM(a.shape, a.dtype) for a in inputs[:3]],
            pltpu.SemaphoreType.DMA((LOADED,)),
        ],
        in_specs=[pl.BlockSpec(memory_space=pltpu.HBM)] * LOADED,
    )(*inputs)
    message_weight, send_y, send_z, index, count, delta = loaded[:6]
    decay, self_weight, energy_proj, energy_row = loaded[6:]
    pick_y, pick_z, place_y, place_z = call(
        lists_kernel,
        [
            shape((2 * GY, OFF_Y), bf16),
            shape((2 * GZ, OFF_Z), bf16),
            shape((UNPADDED, 2 * GY), bf16),
            shape((OFF_Z, 2 * GZ), bf16),
        ],
    )(send_y, send_z)
    onehot = call(onehot_kernel, shape((ROWS, PAIRS), bf16))(index)
    w0, slope, unit, radius, base = call(
        radial_kernel,
        [
            shape((C, PAIRS), bf16),
            shape((SLOTS, ATOMS), f32),
            shape((3, SLOTS, ATOMS), f32),
            shape((SLOTS, ATOMS), f32),
            shape((SLOTS, ATOMS), f32),
        ],
    )(count, delta, decay)
    weights = [w0]
    for layer in (1, 2):
        body = lambda *refs, layer=layer: later_weights_kernel(*refs, layer=layer)
        weights.append(call(body, shape((C, PAIRS), bf16))(radius, base, decay))
    w0, w1, w2 = weights
    lists = (pick_y, pick_z, onehot)
    saved = []
    ready = ((w0, onehot), (pick_y, w1), (pick_y, w2))
    for layer in range(2):
        ghosts = spread(proj, up, down, *lists, ready[layer])
        body = lambda *refs, layer=layer: layer_kernel(*refs, layer=layer)
        features, t, prod, proj, up, down = call(
            body,
            [
                shape((ATOMS, C), bf16),
                shape((ATOMS, C), f32),
                shape((C, PAIRS), bf16),
                shape((ATOMS, C), bf16),
                shape((GX, C), bf16),
                shape((GX, C), bf16),
            ],
        )(*ghosts, features, onehot, weights[layer], self_weight, message_weight, pick_x)
        saved.append((t, prod))
    ghosts = spread(proj, up, down, *lists, ready[2])
    row_shapes = [shape((ATOMS, C), f32), shape((ATOMS, C), f32)]
    terms_shape = shape((C, PAIRS), bf16)
    ghost_shapes = [shape((GZ, C), bf16), shape((GZ, C), bf16)]
    radius_shape = shape((SLOTS, ATOMS), f32)
    readout, gradient, pg, prod, *back = call(
        top_kernel,
        [shape((ATOMS, C), f32), *row_shapes, terms_shape, terms_shape, *ghost_shapes],
    )(*ghosts, features, onehot, w2, self_weight, energy_proj, energy_row)
    places = (onehot, place_y, place_z)
    sums = lambda *refs: sums_kernel(*refs, layer=2)
    radius_grad, energy = call(sums, [radius_shape, shape((1, ATOMS), f32)])(
        prod, pg, decay, slope, readout, energy_row
    )
    returned = retract(*back, *places, rest_kernel, [radius_grad])
    t, prod = saved[1]
    gradient, pg, *back = call(middle_kernel, [*row_shapes, terms_shape, *ghost_shapes])(
        *returned, place_x, gradient, pg, self_weight, message_weight, t, w1, onehot
    )
    sums = lambda *refs: sums_kernel(*refs, layer=1)
    radius_grad = call(sums, radius_shape)(prod, pg, decay, slope, radius_grad)
    returned = retract(*back, *places, rest_kernel, [radius_grad])
    t, prod = saved[0]
    own_force, *back = call(
        bottom_kernel,
        [shape((3, ATOMS), f32), shape((16, PAIRS), bf16), *ghost_shapes],
        [pltpu.VMEM((16, PAIRS), f32)],
    )(
        *returned, place_x, gradient, pg, self_weight, message_weight, t, prod, decay, slope,
        onehot, radius_grad, unit,
    )
    returned = retract(*back, *places, force_rest_kernel)
    forces = call(final_kernel, shape((3, ATOMS), f32))(*returned, place_x, own_force)
    return (energy.reshape(ATOMS), forces)


def solution(mesh):
    split = ("gx", "gy", "gz")
    return jax.shard_map(
        local,
        mesh=mesh,
        in_specs=(
            P(split),
            P(),
            P(split, None),
            P(split),
            P(None, split, None),
            P(None, split),
            P(None, split),
            P(None, split),
            P(),
            P(),
            P(),
            P(),
            P(),
        ),
        out_specs=(P(split), P(None, split)),
        check_vma=False,
    )
```

```python
import math

import jax
import jax.numpy as jnp
from jax import lax
from jax.experimental import pallas as pl
from jax.experimental.pallas import tpu as pltpu
from jax.sharding import PartitionSpec as P

cutoff = 4.0
ATOMS = 128
C = 128
SLOTS = 48
GX, GY, GZ = 32, 64, 64
LOADED = 13
OFF_X, OFF_Y, OFF_Z, ROWS = 128, 256, 384, 512
PAD = 64
UNPADDED = ATOMS + 2 * GX
PAIRS = ATOMS * SLOTS
CHUNK = 256
f32, bf16, i32 = jnp.float32, jnp.bfloat16, jnp.int32
NT = (((1,), (1,)), ((), ()))


def shape(dims, dtype):
    return jax.ShapeDtypeStruct(dims, dtype)


def call(body, outs, scratch=(), limit=4, in_specs=None):
    more = {} if in_specs is None else {"in_specs": in_specs}
    return pl.pallas_call(
        body,
        out_shape=outs,
        **more,
        scratch_shapes=list(scratch),
        compiler_params=pltpu.CompilerParams(vmem_limit_bytes=limit * 1024 * 1024),
    )


def along(axis, distance):
    size = lax.axis_size(axis)
    return [(i, (i + distance) % size) for i in range(size)]


def swap(to_higher, to_lower, axis):
    from_lower = lax.ppermute(to_higher, axis, along(axis, 1))
    from_higher = lax.ppermute(to_lower, axis, along(axis, -1))
    return from_lower, from_higher


def mm(a, b):
    return jnp.dot(a, b, preferred_element_type=f32)


def mm_nt(a, b):
    return lax.dot_general(a, b, NT, preferred_element_type=f32)


def split_nt(a, b):
    high = a.astype(bf16)
    low = (a - high.astype(f32)).astype(bf16)
    return mm_nt(b, high) + mm_nt(b, low)


def columns(row):
    return jnp.broadcast_to(row, (128, row.shape[1])).T


def padded(ids):
    return jnp.where(ids >= UNPADDED, ids + PAD, ids)


def picker(lists, extent):
    ids = jnp.concatenate([columns(lists[n : n + 1, :].astype(f32)) for n in range(2)], axis=0)
    parts = []
    for start in range(0, extent, 128):
        lane = (lax.broadcasted_iota(i32, ids.shape, 1) + start).astype(f32)
        parts.append(jnp.where(ids == lane, 1.0, 0.0).astype(bf16))
    return jnp.concatenate(parts, axis=1) if len(parts) > 1 else parts[0]


def place_into(out, lists):
    n = lists.shape[1]
    sub = lax.broadcasted_iota(i32, (out.shape[0], n), 0)
    for side in range(2):
        out[:, side * n : (side + 1) * n] = jnp.where(
            sub == lists[side : side + 1, :], 1.0, 0.0
        ).astype(bf16)


def first_kernel(*refs):
    inputs, refs = refs[:LOADED], refs[LOADED:]
    kept, refs = refs[: LOADED - 3], refs[LOADED - 3 :]
    feat, proj, up, down, pick_x, place_x, rows, types, table, send_x, sems = refs
    weight = kept[0]
    pairs = [(inputs[3].at[0], weight.at[0])]
    pairs += zip(inputs[:3], (types, table, send_x))
    pairs += [(inputs[3].at[1:], weight.at[1:])]
    pairs += zip(inputs[4:], kept[1:])
    moves = [pltpu.make_async_copy(a, b, sems.at[i]) for i, (a, b) in enumerate(pairs)]
    for move in moves:
        move.start()
    rows[...] = jnp.zeros_like(rows)
    for move in moves[:4]:
        move.wait()
    rows[0:6, :] = table[...].astype(f32)
    kinds = columns(types[...].astype(f32))
    lane = lax.broadcasted_iota(i32, (ATOMS, 128), 1).astype(f32)
    onehot = jnp.where(kinds == lane, 1.0, 0.0).astype(bf16)
    per_type = rows[...].astype(bf16)
    projected = mm(per_type, weight[0]).astype(bf16)
    pick = picker(send_x[...], ATOMS)
    chosen = mm(mm(pick, onehot).astype(bf16), projected).astype(bf16)
    up[...] = chosen[0:GX]
    down[...] = chosen[GX:]
    proj[...] = mm(onehot, projected).astype(bf16)
    feat[...] = mm(onehot, per_type).astype(bf16)
    pick_x[...] = pick
    place_into(place_x, send_x[...])
    for move in moves[4:]:
        move.wait()


def lists_kernel(send_y, send_z, pick_y, pick_z, place_y, place_z):
    ids_y, ids_z = send_y[...], padded(send_z[...])
    pick_y[...] = picker(ids_y, OFF_Y)
    pick_z[...] = picker(ids_z, OFF_Z)
    place_into(place_y, ids_y)
    place_into(place_z, ids_z)


def onehot_kernel(index, onehot, *, start):
    ids = padded(index[...])
    sub = lax.broadcasted_iota(i32, (OFF_Y, ATOMS), 0) + start
    for k in range(SLOTS):
        here = slice(k * ATOMS, (k + 1) * ATOMS)
        onehot[:, here] = jnp.where(sub == ids[k : k + 1, :], 1.0, 0.0).astype(bf16)


def weights_into(out, radius, base, decay_row):
    rate = columns(-decay_row)
    for k in range(SLOTS):
        here = slice(k * ATOMS, (k + 1) * ATOMS)
        out[:, here] = (base[k : k + 1, :] * jnp.exp(rate * radius[k : k + 1, :])).astype(bf16)


def radial_kernel(count, delta, decay, w, slope, unit, radius_out, base_out):
    d = [delta[n] for n in range(3)]
    radius = jnp.sqrt(d[0] * d[0] + d[1] * d[1] + d[2] * d[2])
    slot = lax.broadcasted_iota(i32, (SLOTS, ATOMS), 0)
    alive = jnp.where(slot < count[...], 1.0, 0.0)
    half = (math.pi / (2.0 * cutoff)) * radius
    cosine, sine = jnp.cos(half), jnp.sin(half)
    base = alive * (cosine * cosine) * (1.0 / math.sqrt(SLOTS)) / radius
    slope[...] = -(math.pi / cutoff) * sine / cosine - 1.0 / radius
    for n in range(3):
        unit[n] = d[n] / radius
    radius_out[...] = radius
    base_out[...] = base
    weights_into(w, radius, base, decay[0:1, :])


def later_weights_kernel(radius, base, decay, w, *, layer):
    weights_into(w, radius[...], base[...], decay[layer : layer + 1, :])


def pick_y_kernel(proj, lower, higher, pick, ready, up, down, table):
    table[0:ATOMS] = proj[...]
    table[OFF_X : OFF_X + GX] = lower[...]
    table[OFF_X + GX : OFF_X + 2 * GX] = higher[...]
    table[OFF_X + 2 * GX : OFF_Y] = jnp.zeros((PAD, C), bf16)
    chosen = mm(pick[...], table[...]).astype(bf16)
    up[...] = chosen[0:GY]
    down[...] = chosen[GY:]


def pick_z_kernel(proj, x_lower, x_higher, y_lower, y_higher, pick, ready, up, down, table):
    table[0:ATOMS] = proj[...]
    table[OFF_X : OFF_X + GX] = x_lower[...]
    table[OFF_X + GX : OFF_X + 2 * GX] = x_higher[...]
    table[OFF_X + 2 * GX : OFF_Y] = jnp.zeros((PAD, C), bf16)
    table[OFF_Y : OFF_Y + GY] = y_lower[...]
    table[OFF_Y + GY : OFF_Z] = y_higher[...]
    chosen = mm(pick[...], table[...]).astype(bf16)
    up[...] = chosen[0:GZ]
    down[...] = chosen[GZ:]


def turned(rows):
    return rows.astype(f32).T.astype(bf16)


def low_gather_kernel(proj, x_lower, x_higher, y_lower, y_higher, near, far, low, table):
    table[0:ATOMS] = proj[...]
    table[OFF_X : OFF_X + GX] = x_lower[...]
    table[OFF_X + GX : OFF_X + 2 * GX] = x_higher[...]
    table[OFF_X + 2 * GX : OFF_Y] = jnp.zeros((PAD, C), bf16)
    table[OFF_Y : OFF_Y + GY] = y_lower[...]
    table[OFF_Y + GY : OFF_Z] = y_higher[...]
    rows = turned(table[...])
    for start in range(0, PAIRS, CHUNK):
        here = slice(start, start + CHUNK)
        gathered = mm(rows[:, 0:OFF_Y], near[:, here])
        gathered = gathered + mm(rows[:, OFF_Y:OFF_Z], far[0 : OFF_Z - OFF_Y, here])
        low[:, here] = gathered.astype(bf16)


def forward_part(z_lower, z_higher, low, far, w, prod):
    rows = turned(jnp.concatenate([z_lower[...], z_higher[...]], axis=0))
    total = jnp.zeros((C, ATOMS), f32)
    for start in range(0, PAIRS, CHUNK):
        here = slice(start, start + CHUNK)
        gathered = mm(rows, far[OFF_Z - OFF_Y :, here]).astype(bf16) + low[:, here]
        m = gathered * w[:, here]
        prod[:, here] = m
        for inner in range(0, CHUNK, ATOMS):
            total = total + m[:, inner : inner + ATOMS].astype(f32)
    return total


def next_rows(gather_refs, feat, weight):
    rows = feat[...]
    t = jnp.tanh(forward_part(*gather_refs) + mm(rows, weight).T)
    return t, rows.astype(f32).T + t


def layer_kernel(
    z_lower, z_higher, low, feat, far, w, self_weight, next_weight, pick_x,
    new_feat, tanh_out, prod, new_proj, up, down, *, layer,
):
    t, features = next_rows((z_lower, z_higher, low, far, w, prod), feat, self_weight[layer])
    tanh_out[...] = t
    features = features.T.astype(bf16)
    new_feat[...] = features
    projected = mm(features, next_weight[layer + 1]).astype(bf16)
    new_proj[...] = projected
    chosen = mm(pick_x[...], projected).astype(bf16)
    up[...] = chosen[0:GX]
    down[...] = chosen[GX:]


def sum_rows(decay_row):
    high = decay_row.astype(bf16).astype(f32)
    rows = [jnp.ones_like(decay_row), high, decay_row - high, jnp.zeros((13, C), f32)]
    return jnp.concatenate(rows, axis=0).astype(bf16)


def backward_sums(prod, start, wide, rows, slope):
    s = mm(rows, prod[:, start : start + CHUNK] * wide)
    out = []
    for inner in range(0, CHUNK, ATOMS):
        k = (start + inner) // ATOMS
        here = slice(inner, inner + ATOMS)
        out.append(slope[k : k + 1, :] * s[0:1, here] - (s[1:2, here] + s[2:3, here]))
    return out


def wide_rows(x):
    return jnp.concatenate([x] * (CHUNK // ATOMS), axis=1)


def ghost_rows(rows, z_lower, z_higher):
    z_lower[...] = rows[0:GZ].astype(bf16)
    z_higher[...] = rows[GZ:].astype(bf16)


def mm_split(a, b):
    high = b.astype(bf16)
    low = (b - high.astype(f32)).astype(bf16)
    return mm(a, high) + mm(a, low)


def terms_part(pg, w, far, terms, z_lower, z_higher):
    wide = wide_rows(pg.astype(bf16))
    for start in range(0, PAIRS, CHUNK):
        here = slice(start, start + CHUNK)
        terms[:, here] = w[:, here] * wide
    ghost_rows(mm_nt(far[OFF_Z - OFF_Y :, :], terms[...]), z_lower, z_higher)


def rest_kernel(terms, near, far, kept):
    kept[0:OFF_Y, :] = mm_nt(near[...], terms[...])
    kept[OFF_Y:OFF_Z, :] = mm_nt(far[0 : OFF_Z - OFF_Y, :], terms[...])


def force_rest_kernel(terms, near, far, kept):
    kept[...] = jnp.zeros_like(kept)
    n = terms.shape[0]
    kept[0:OFF_Y, 0:n] = mm_nt(near[...], terms[...])
    kept[OFF_Y:OFF_Z, 0:n] = mm_nt(far[0 : OFF_Z - OFF_Y, :], terms[...])


def sums_kernel(prod, pg, decay, slope, *refs, layer):
    wide, rows = wide_rows(pg[...].astype(bf16)), sum_rows(decay[layer : layer + 1, :])
    parts = []
    for start in range(0, PAIRS, CHUNK):
        parts += backward_sums(prod, start, wide, rows, slope)
    total = jnp.concatenate(parts, axis=0)
    if layer == 2:
        readout, out_row, radius_grad, energy = refs
        energy[...] = jnp.sum(readout[...] * columns(out_row[...]), axis=0, keepdims=True)
        radius_grad[...] = total
    else:
        before, radius_grad = refs
        radius_grad[...] = before[...] + total


def top_kernel(
    zl, zh, low, feat, far, w, self_weight, energy_proj, energy_out,
    readout_out, gradient_out, pg_out, prod, terms, z_lower, z_higher,
):
    t, features = next_rows((zl, zh, low, far, w, prod), feat, self_weight[2])
    readout = jnp.tanh(mm(turned(energy_proj[...]), features.astype(bf16)))
    readout_out[...] = readout
    upstream = (1.0 - readout * readout) * columns(energy_out[...])
    gradient = mm_split(energy_proj[...], upstream)
    pg = gradient * (1.0 - t * t)
    gradient_out[...] = gradient
    pg_out[...] = pg
    terms_part(pg, w, far, terms, z_lower, z_higher)


def return_z_kernel(kept, plus, minus, place, rest, y_lower, y_higher):
    pieces = jnp.concatenate([minus[...], plus[...]], axis=0)
    total = kept[...] + mm(place[...], pieces)
    rest[...] = total[0:UNPADDED]
    y_lower[...] = total[OFF_Y : OFF_Y + GY].astype(bf16)
    y_higher[...] = total[OFF_Y + GY : OFF_Z].astype(bf16)


def return_y_kernel(kept, plus, minus, place, *refs):
    own, x_lower, x_higher = refs[-3:]
    pieces = jnp.concatenate([minus[...], plus[...]], axis=0)
    total = kept[...] + mm(place[...], pieces)
    own[...] = total[0:ATOMS]
    x_lower[...] = total[OFF_X : OFF_X + GX].astype(bf16)
    x_higher[...] = total[OFF_X + GX :].astype(bf16)


def down_step(own, plus, minus, place, gradient, pg, self_weight, message_weight, layer):
    pieces = jnp.concatenate([minus[...], plus[...]], axis=0)
    row_sum = own[...] + mm(place[...], pieces)
    return (
        gradient[...]
        + mm_split(self_weight[layer], pg[...])
        + split_nt(row_sum, message_weight[layer])
    )


def middle_kernel(
    own, plus, minus, place, gradient_in, pg_in, self_weight, message_weight, t, w, far,
    gradient_out, pg_out, terms, z_lower, z_higher,
):
    gradient = down_step(own, plus, minus, place, gradient_in, pg_in, self_weight, message_weight, 2)
    activation = t[...]
    pg = gradient * (1.0 - activation * activation)
    gradient_out[...] = gradient
    pg_out[...] = pg
    terms_part(pg, w, far, terms, z_lower, z_higher)


def bottom_kernel(
    own, plus, minus, place, gradient_in, pg_in, self_weight, message_weight,
    t, prod, decay, slope, far, radius_in, unit,
    own_force, terms, z_lower, z_higher, rows,
):
    gradient = down_step(own, plus, minus, place, gradient_in, pg_in, self_weight, message_weight, 1)
    activation = t[...]
    pg = gradient * (1.0 - activation * activation)
    wide, weighted = wide_rows(pg.astype(bf16)), sum_rows(decay[0:1, :])
    rows[...] = jnp.zeros_like(rows)
    sums = [jnp.zeros((1, ATOMS), f32)] * 3
    for start in range(0, PAIRS, CHUNK):
        for i, part in enumerate(backward_sums(prod, start, wide, weighted, slope)):
            k = start // ATOMS + i
            total = radius_in[k : k + 1, :] + part
            for n in range(3):
                pushed = total * unit[n, k : k + 1, :]
                sums[n] = sums[n] + pushed
                rows[n : n + 1, k * ATOMS : (k + 1) * ATOMS] = pushed
    terms[...] = rows[...].astype(bf16)
    ghosts = mm_nt(far[OFF_Z - OFF_Y :, :], terms[...])
    padding = jnp.zeros((2 * GZ, C - ghosts.shape[1]), f32)
    ghost_rows(jnp.concatenate([ghosts, padding], axis=1), z_lower, z_higher)
    for n in range(3):
        own_force[n : n + 1, :] = sums[n]


def final_kernel(own, plus, minus, place, own_force, forces):
    pieces = jnp.concatenate([minus[...], plus[...]], axis=0)
    row_sum = own[...] + mm(place[...], pieces)
    forces[...] = own_force[...] - row_sum.T[0:3, :]


def spread(proj, up, down, pick_y, pick_z, near, far, ready):
    x = swap(up, down, "gx")
    sends = call(
        pick_y_kernel,
        [shape((GY, C), bf16)] * 2,
        [pltpu.VMEM((OFF_Y, C), bf16)],
    )(proj, *x, pick_y, ready[0])
    y = swap(*sends, "gy")
    sends = call(
        pick_z_kernel,
        [shape((GZ, C), bf16)] * 2,
        [pltpu.VMEM((OFF_Z, C), bf16)],
    )(proj, *x, *y, pick_z, ready[1])
    z = swap(*sends, "gz")
    low = call(
        low_gather_kernel, shape((C, PAIRS), bf16), [pltpu.VMEM((OFF_Z, C), bf16)]
    )(proj, *x, *y, near, far)
    return (*z, low)


def retract(terms, z_lower, z_higher, near, far, place_y, place_z, rest, ready=()):
    arrived = swap(z_higher, z_lower, "gz")
    kept = call(rest, shape((OFF_Z, C), f32))(terms, near, far)
    kept, y_lower, y_higher = call(
        return_z_kernel,
        [shape((UNPADDED, C), f32), shape((GY, C), bf16), shape((GY, C), bf16)],
    )(kept, *arrived, place_z)
    arrived = swap(y_higher, y_lower, "gy")
    own, x_lower, x_higher = call(
        return_y_kernel,
        [shape((ATOMS, C), f32), shape((GX, C), bf16), shape((GX, C), bf16)],
    )(kept, *arrived, place_y, *ready)
    arrived = swap(x_higher, x_lower, "gx")
    return (own, *arrived)


def local(
    atom_types,
    type_table,
    neighbor_index,
    neighbor_count,
    displacement,
    send_x,
    send_y,
    send_z,
    message_weight,
    self_weight,
    decay,
    energy_proj,
    energy_out,
):
    inputs = (
        atom_types.reshape(1, ATOMS),
        type_table,
        send_x,
        message_weight,
        send_y,
        send_z,
        neighbor_index.T,
        neighbor_count.reshape(1, ATOMS),
        jnp.swapaxes(displacement, 1, 2),
        decay,
        self_weight,
        energy_proj,
        energy_out.reshape(1, C),
    )
    inputs = [pltpu.with_memory_space_constraint(a, pltpu.HBM) for a in inputs]
    *loaded, features, proj, up, down, pick_x, place_x = call(
        first_kernel,
        [
            *[shape(a.shape, a.dtype) for a in inputs[3:]],
            shape((ATOMS, C), bf16),
            shape((ATOMS, C), bf16),
            shape((GX, C), bf16),
            shape((GX, C), bf16),
            shape((2 * GX, ATOMS), bf16),
            shape((ATOMS, 2 * GX), bf16),
        ],
        [
            pltpu.VMEM((128, C), f32),
            *[pltpu.VMEM(a.shape, a.dtype) for a in inputs[:3]],
            pltpu.SemaphoreType.DMA((LOADED + 1,)),
        ],
        in_specs=[pl.BlockSpec(memory_space=pltpu.HBM)] * LOADED,
    )(*inputs)
    message_weight, send_y, send_z, index, count, delta = loaded[:6]
    decay, self_weight, energy_proj, energy_row = loaded[6:]
    pick_y, pick_z, place_y, place_z = call(
        lists_kernel,
        [
            shape((2 * GY, OFF_Y), bf16),
            shape((2 * GZ, OFF_Z), bf16),
            shape((UNPADDED, 2 * GY), bf16),
            shape((OFF_Z, 2 * GZ), bf16),
        ],
    )(send_y, send_z)
    near, far = [
        call(lambda *refs, start=start: onehot_kernel(*refs, start=start), shape((OFF_Y, PAIRS), bf16))(
            index
        )
        for start in (0, OFF_Y)
    ]
    w0, slope, unit, radius, base = call(
        radial_kernel,
        [
            shape((C, PAIRS), bf16),
            shape((SLOTS, ATOMS), f32),
            shape((3, SLOTS, ATOMS), f32),
            shape((SLOTS, ATOMS), f32),
            shape((SLOTS, ATOMS), f32),
        ],
    )(count, delta, decay)
    weights = [w0]
    for layer in (1, 2):
        body = lambda *refs, layer=layer: later_weights_kernel(*refs, layer=layer)
        weights.append(call(body, shape((C, PAIRS), bf16))(radius, base, decay))
    w0, w1, w2 = weights
    lists = (pick_y, pick_z, near, far)
    saved = []
    ready = ((w0, near), (pick_y, w1), (pick_y, w2))
    for layer in range(2):
        ghosts = spread(proj, up, down, *lists, ready[layer])
        body = lambda *refs, layer=layer: layer_kernel(*refs, layer=layer)
        features, t, prod, proj, up, down = call(
            body,
            [
                shape((ATOMS, C), bf16),
                shape((ATOMS, C), f32),
                shape((C, PAIRS), bf16),
                shape((ATOMS, C), bf16),
                shape((GX, C), bf16),
                shape((GX, C), bf16),
            ],
        )(*ghosts, features, far, weights[layer], self_weight, message_weight, pick_x)
        saved.append((t, prod))
    ghosts = spread(proj, up, down, *lists, ready[2])
    row_shapes = [shape((ATOMS, C), f32), shape((ATOMS, C), f32)]
    terms_shape = shape((C, PAIRS), bf16)
    ghost_shapes = [shape((GZ, C), bf16), shape((GZ, C), bf16)]
    radius_shape = shape((SLOTS, ATOMS), f32)
    readout, gradient, pg, prod, *back = call(
        top_kernel,
        [shape((ATOMS, C), f32), *row_shapes, terms_shape, terms_shape, *ghost_shapes],
    )(*ghosts, features, far, w2, self_weight, energy_proj, energy_row)
    places = (near, far, place_y, place_z)
    sums = lambda *refs: sums_kernel(*refs, layer=2)
    radius_grad, energy = call(sums, [radius_shape, shape((1, ATOMS), f32)])(
        prod, pg, decay, slope, readout, energy_row
    )
    returned = retract(*back, *places, rest_kernel, [radius_grad])
    t, prod = saved[1]
    gradient, pg, *back = call(middle_kernel, [*row_shapes, terms_shape, *ghost_shapes])(
        *returned, place_x, gradient, pg, self_weight, message_weight, t, w1, far
    )
    sums = lambda *refs: sums_kernel(*refs, layer=1)
    radius_grad = call(sums, radius_shape)(prod, pg, decay, slope, radius_grad)
    returned = retract(*back, *places, rest_kernel, [radius_grad])
    t, prod = saved[0]
    own_force, *back = call(
        bottom_kernel,
        [shape((3, ATOMS), f32), shape((16, PAIRS), bf16), *ghost_shapes],
        [pltpu.VMEM((16, PAIRS), f32)],
    )(
        *returned, place_x, gradient, pg, self_weight, message_weight, t, prod, decay, slope,
        far, radius_grad, unit,
    )
    returned = retract(*back, *places, force_rest_kernel)
    forces = call(final_kernel, shape((3, ATOMS), f32))(*returned, place_x, own_force)
    return (energy.reshape(ATOMS), forces)


def solution(mesh):
    split = ("gx", "gy", "gz")
    return jax.shard_map(
        local,
        mesh=mesh,
        in_specs=(
            P(split),
            P(),
            P(split, None),
            P(split),
            P(None, split, None),
            P(None, split),
            P(None, split),
            P(None, split),
            P(),
            P(),
            P(),
            P(),
            P(),
        ),
        out_specs=(P(split), P(None, split)),
        check_vma=False,
    )
```

```python
import math

import jax
import jax.numpy as jnp
from jax import lax
from jax.experimental import pallas as pl
from jax.experimental.pallas import tpu as pltpu
from jax.sharding import PartitionSpec as P

cutoff = 4.0
ATOMS = 128
C = 128
SLOTS = 48
GX, GY, GZ = 32, 64, 64
LOADED = 13
OFF_X, OFF_Y, OFF_Z, ROWS = 128, 256, 384, 512
PAD = 64
UNPADDED = ATOMS + 2 * GX
PAIRS = ATOMS * SLOTS
CHUNK = 2 * ATOMS
f32, bf16, i32 = jnp.float32, jnp.bfloat16, jnp.int32
NT = (((1,), (1,)), ((), ()))


def shape(dims, dtype):
    return jax.ShapeDtypeStruct(dims, dtype)


def call(body, outs, scratch=(), limit=4, in_specs=None):
    more = {} if in_specs is None else {"in_specs": in_specs}
    return pl.pallas_call(
        body,
        out_shape=outs,
        **more,
        scratch_shapes=list(scratch),
        compiler_params=pltpu.CompilerParams(vmem_limit_bytes=limit * 1024 * 1024),
    )


def along(axis, distance):
    size = lax.axis_size(axis)
    return [(i, (i + distance) % size) for i in range(size)]


def swap(to_higher, to_lower, axis):
    from_lower = lax.ppermute(to_higher, axis, along(axis, 1))
    from_higher = lax.ppermute(to_lower, axis, along(axis, -1))
    return from_lower, from_higher


def mm(a, b):
    return jnp.dot(a, b, preferred_element_type=f32)


def mm_nt(a, b):
    return lax.dot_general(a, b, NT, preferred_element_type=f32)


def split_nt(a, b):
    high = a.astype(bf16)
    low = (a - high.astype(f32)).astype(bf16)
    return mm_nt(b, high) + mm_nt(b, low)


def columns(row):
    return jnp.broadcast_to(row, (128, row.shape[1])).T


def padded(ids):
    return jnp.where(ids >= UNPADDED, ids + PAD, ids)


def picker(lists, extent):
    ids = jnp.concatenate([columns(lists[n : n + 1, :].astype(f32)) for n in range(2)], axis=0)
    parts = []
    for start in range(0, extent, 128):
        lane = (lax.broadcasted_iota(i32, ids.shape, 1) + start).astype(f32)
        parts.append(jnp.where(ids == lane, 1.0, 0.0).astype(bf16))
    return jnp.concatenate(parts, axis=1) if len(parts) > 1 else parts[0]


def place_into(out, lists):
    n = lists.shape[1]
    sub = lax.broadcasted_iota(i32, (out.shape[0], n), 0)
    for side in range(2):
        out[:, side * n : (side + 1) * n] = jnp.where(
            sub == lists[side : side + 1, :], 1.0, 0.0
        ).astype(bf16)


def first_kernel(*refs):
    inputs, refs = refs[:LOADED], refs[LOADED:]
    kept, refs = refs[: LOADED - 3], refs[LOADED - 3 :]
    feat, proj, up, down, pick_x, place_x, rows, types, table, send_x, sems = refs
    weight = kept[0]
    pairs = [(inputs[3].at[0], weight.at[0])]
    pairs += zip(inputs[:3], (types, table, send_x))
    pairs += [(inputs[3].at[1:], weight.at[1:])]
    pairs += zip(inputs[4:], kept[1:])
    moves = [pltpu.make_async_copy(a, b, sems.at[i]) for i, (a, b) in enumerate(pairs)]
    for move in moves:
        move.start()
    rows[...] = jnp.zeros_like(rows)
    for move in moves[:4]:
        move.wait()
    rows[0:6, :] = table[...].astype(f32)
    kinds = columns(types[...].astype(f32))
    lane = lax.broadcasted_iota(i32, (ATOMS, 128), 1).astype(f32)
    onehot = jnp.where(kinds == lane, 1.0, 0.0).astype(bf16)
    per_type = rows[...].astype(bf16)
    projected = mm(per_type, weight[0]).astype(bf16)
    pick = picker(send_x[...], ATOMS)
    chosen = mm(mm(pick, onehot).astype(bf16), projected).astype(bf16)
    up[...] = chosen[0:GX]
    down[...] = chosen[GX:]
    proj[...] = mm(onehot, projected).astype(bf16)
    feat[...] = mm(onehot, per_type).astype(bf16)
    pick_x[...] = pick
    place_into(place_x, send_x[...])
    for move in moves[4:]:
        move.wait()


def lists_kernel(send_y, send_z, pick_y, pick_z, place_y, place_z):
    ids_y, ids_z = send_y[...], padded(send_z[...])
    pick_y[...] = picker(ids_y, OFF_Y)
    pick_z[...] = picker(ids_z, OFF_Z)
    place_into(place_y, ids_y)
    place_into(place_z, ids_z)


def onehot_kernel(index, onehot, *, start):
    ids = padded(index[...])
    sub = lax.broadcasted_iota(i32, (OFF_Y, ATOMS), 0) + start
    for k in range(SLOTS):
        here = slice(k * ATOMS, (k + 1) * ATOMS)
        onehot[:, here] = jnp.where(sub == ids[k : k + 1, :], 1.0, 0.0).astype(bf16)


def weights_into(out, radius, base, decay_row):
    rate = columns(-decay_row)
    for k in range(SLOTS):
        here = slice(k * ATOMS, (k + 1) * ATOMS)
        out[:, here] = (base[k : k + 1, :] * jnp.exp(rate * radius[k : k + 1, :])).astype(bf16)


def radial_kernel(count, delta, decay, w, slope, unit, radius_out, base_out):
    d = [delta[n] for n in range(3)]
    radius = jnp.sqrt(d[0] * d[0] + d[1] * d[1] + d[2] * d[2])
    slot = lax.broadcasted_iota(i32, (SLOTS, ATOMS), 0)
    alive = jnp.where(slot < count[...], 1.0, 0.0)
    half = (math.pi / (2.0 * cutoff)) * radius
    cosine, sine = jnp.cos(half), jnp.sin(half)
    base = alive * (cosine * cosine) * (1.0 / math.sqrt(SLOTS)) / radius
    slope[...] = -(math.pi / cutoff) * sine / cosine - 1.0 / radius
    for n in range(3):
        unit[n] = d[n] / radius
    radius_out[...] = radius
    base_out[...] = base
    weights_into(w, radius, base, decay[0:1, :])


def later_weights_kernel(radius, base, decay, w, *, layer):
    weights_into(w, radius[...], base[...], decay[layer : layer + 1, :])


def pick_y_kernel(proj, lower, higher, pick, ready, up, down, table):
    table[0:ATOMS] = proj[...]
    table[OFF_X : OFF_X + GX] = lower[...]
    table[OFF_X + GX : OFF_X + 2 * GX] = higher[...]
    table[OFF_X + 2 * GX : OFF_Y] = jnp.zeros((PAD, C), bf16)
    chosen = mm(pick[...], table[...]).astype(bf16)
    up[...] = chosen[0:GY]
    down[...] = chosen[GY:]


def pick_z_kernel(proj, x_lower, x_higher, y_lower, y_higher, pick, ready, up, down, table):
    table[0:ATOMS] = proj[...]
    table[OFF_X : OFF_X + GX] = x_lower[...]
    table[OFF_X + GX : OFF_X + 2 * GX] = x_higher[...]
    table[OFF_X + 2 * GX : OFF_Y] = jnp.zeros((PAD, C), bf16)
    table[OFF_Y : OFF_Y + GY] = y_lower[...]
    table[OFF_Y + GY : OFF_Z] = y_higher[...]
    chosen = mm(pick[...], table[...]).astype(bf16)
    up[...] = chosen[0:GZ]
    down[...] = chosen[GZ:]


def turned(rows):
    return rows.astype(f32).T.astype(bf16)


def low_gather_kernel(proj, x_lower, x_higher, y_lower, y_higher, near, far, low, table):
    table[0:ATOMS] = proj[...]
    table[OFF_X : OFF_X + GX] = x_lower[...]
    table[OFF_X + GX : OFF_X + 2 * GX] = x_higher[...]
    table[OFF_X + 2 * GX : OFF_Y] = jnp.zeros((PAD, C), bf16)
    table[OFF_Y : OFF_Y + GY] = y_lower[...]
    table[OFF_Y + GY : OFF_Z] = y_higher[...]
    rows = turned(table[...])
    for start in range(0, PAIRS, CHUNK):
        here = slice(start, start + CHUNK)
        gathered = mm(rows[:, 0:OFF_Y], near[:, here])
        gathered = gathered + mm(rows[:, OFF_Y:OFF_Z], far[0 : OFF_Z - OFF_Y, here])
        low[:, here] = gathered.astype(bf16)


def forward_part(z_lower, z_higher, low, far, w, prod):
    rows = turned(jnp.concatenate([z_lower[...], z_higher[...]], axis=0))
    total = jnp.zeros((C, ATOMS), f32)
    for start in range(0, PAIRS, CHUNK):
        here = slice(start, start + CHUNK)
        gathered = mm(rows, far[OFF_Z - OFF_Y :, here]).astype(bf16) + low[:, here]
        m = gathered * w[:, here]
        prod[:, here] = m
        total = total + (m[:, 0:ATOMS] + m[:, ATOMS:]).astype(f32)
    return total


def next_rows(total, feat, weight):
    rows = feat[...]
    t = jnp.tanh(total + mm(rows, weight).T)
    return t, rows.astype(f32).T + t


def layer_kernel(
    z_lower, z_higher, low, feat, far, w, self_weight, next_weight, pick_x,
    new_feat, tanh_out, prod, new_proj, up, down, *, layer,
):
    total = forward_part(z_lower, z_higher, low, far, w, prod)
    t, features = next_rows(total, feat, self_weight[layer])
    tanh_out[...] = t
    features = features.T.astype(bf16)
    new_feat[...] = features
    projected = mm(features, next_weight[layer + 1]).astype(bf16)
    new_proj[...] = projected
    chosen = mm(pick_x[...], projected).astype(bf16)
    up[...] = chosen[0:GX]
    down[...] = chosen[GX:]


def sum_rows(decay_row):
    high = decay_row.astype(bf16).astype(f32)
    rows = [jnp.ones_like(decay_row), high, decay_row - high, jnp.zeros((13, C), f32)]
    return jnp.concatenate(rows, axis=0).astype(bf16)


def backward_sums(prod, start, wide, rows, slope):
    s = mm(rows, prod[:, start : start + CHUNK] * wide)
    out = []
    for inner in range(0, CHUNK, ATOMS):
        k = (start + inner) // ATOMS
        here = slice(inner, inner + ATOMS)
        out.append(slope[k : k + 1, :] * s[0:1, here] - (s[1:2, here] + s[2:3, here]))
    return out


def wide_rows(x):
    return jnp.concatenate([x] * (CHUNK // ATOMS), axis=1)


def ghost_rows(rows, z_lower, z_higher):
    z_lower[...] = rows[0:GZ].astype(bf16)
    z_higher[...] = rows[GZ:].astype(bf16)


def mm_split(a, b):
    high = b.astype(bf16)
    low = (b - high.astype(f32)).astype(bf16)
    return mm(a, high) + mm(a, low)


def terms_part(pg, w, far, terms, z_lower, z_higher):
    wide = wide_rows(pg.astype(bf16))
    for start in range(0, PAIRS, CHUNK):
        here = slice(start, start + CHUNK)
        terms[:, here] = w[:, here] * wide
    ghost_rows(mm_nt(far[OFF_Z - OFF_Y :, :], terms[...]), z_lower, z_higher)


def rest_kernel(terms, near, far, kept):
    kept[0:OFF_Y, :] = mm_nt(near[...], terms[...])
    kept[OFF_Y:OFF_Z, :] = mm_nt(far[0 : OFF_Z - OFF_Y, :], terms[...])


def force_rest_kernel(terms, near, far, kept):
    kept[...] = jnp.zeros_like(kept)
    n = terms.shape[0]
    kept[0:OFF_Y, 0:n] = mm_nt(near[...], terms[...])
    kept[OFF_Y:OFF_Z, 0:n] = mm_nt(far[0 : OFF_Z - OFF_Y, :], terms[...])


def sums_kernel(prod, pg, decay, slope, *refs, layer):
    wide, rows = wide_rows(pg[...].astype(bf16)), sum_rows(decay[layer : layer + 1, :])
    parts = []
    for start in range(0, PAIRS, CHUNK):
        parts += backward_sums(prod, start, wide, rows, slope)
    total = jnp.concatenate(parts, axis=0)
    if layer == 2:
        readout, out_row, radius_grad, energy = refs
        energy[...] = jnp.sum(readout[...] * columns(out_row[...]), axis=0, keepdims=True)
        radius_grad[...] = total
    else:
        before, radius_grad = refs
        radius_grad[...] = before[...] + total


def top_sum_kernel(z_lower, z_higher, low, far, w, total, prod):
    total[...] = forward_part(z_lower, z_higher, low, far, w, prod)


def top_kernel(
    total, feat, far, w, self_weight, energy_proj, energy_out,
    readout_out, gradient_out, pg_out, terms, z_lower, z_higher,
):
    t, features = next_rows(total[...], feat, self_weight[2])
    readout = jnp.tanh(mm(turned(energy_proj[...]), features.astype(bf16)))
    readout_out[...] = readout
    upstream = (1.0 - readout * readout) * columns(energy_out[...])
    gradient = mm_split(energy_proj[...], upstream)
    pg = gradient * (1.0 - t * t)
    gradient_out[...] = gradient
    pg_out[...] = pg
    terms_part(pg, w, far, terms, z_lower, z_higher)


def return_z_kernel(kept, plus, minus, place, rest, y_lower, y_higher):
    pieces = jnp.concatenate([minus[...], plus[...]], axis=0)
    total = kept[...] + mm(place[...], pieces)
    rest[...] = total[0:UNPADDED]
    y_lower[...] = total[OFF_Y : OFF_Y + GY].astype(bf16)
    y_higher[...] = total[OFF_Y + GY : OFF_Z].astype(bf16)


def return_y_kernel(kept, plus, minus, place, *refs):
    own, x_lower, x_higher = refs[-3:]
    pieces = jnp.concatenate([minus[...], plus[...]], axis=0)
    total = kept[...] + mm(place[...], pieces)
    own[...] = total[0:ATOMS]
    x_lower[...] = total[OFF_X : OFF_X + GX].astype(bf16)
    x_higher[...] = total[OFF_X + GX :].astype(bf16)


def down_step(own, plus, minus, place, gradient, pg, self_weight, message_weight, layer):
    pieces = jnp.concatenate([minus[...], plus[...]], axis=0)
    row_sum = own[...] + mm(place[...], pieces)
    return (
        gradient[...]
        + mm_split(self_weight[layer], pg[...])
        + split_nt(row_sum, message_weight[layer])
    )


def middle_kernel(
    own, plus, minus, place, gradient_in, pg_in, self_weight, message_weight, t, w, far,
    gradient_out, pg_out, terms, z_lower, z_higher,
):
    gradient = down_step(own, plus, minus, place, gradient_in, pg_in, self_weight, message_weight, 2)
    activation = t[...]
    pg = gradient * (1.0 - activation * activation)
    gradient_out[...] = gradient
    pg_out[...] = pg
    terms_part(pg, w, far, terms, z_lower, z_higher)


def bottom_kernel(
    own, plus, minus, place, gradient_in, pg_in, self_weight, message_weight,
    t, prod, decay, slope, far, radius_in, unit,
    own_force, terms, z_lower, z_higher, rows,
):
    gradient = down_step(own, plus, minus, place, gradient_in, pg_in, self_weight, message_weight, 1)
    activation = t[...]
    pg = gradient * (1.0 - activation * activation)
    wide, weighted = wide_rows(pg.astype(bf16)), sum_rows(decay[0:1, :])
    rows[...] = jnp.zeros_like(rows)
    sums = [jnp.zeros((1, ATOMS), f32)] * 3
    for start in range(0, PAIRS, CHUNK):
        for i, part in enumerate(backward_sums(prod, start, wide, weighted, slope)):
            k = start // ATOMS + i
            total = radius_in[k : k + 1, :] + part
            for n in range(3):
                pushed = total * unit[n, k : k + 1, :]
                sums[n] = sums[n] + pushed
                rows[n : n + 1, k * ATOMS : (k + 1) * ATOMS] = pushed
    terms[...] = rows[...].astype(bf16)
    ghosts = mm_nt(far[OFF_Z - OFF_Y :, :], terms[...])
    padding = jnp.zeros((2 * GZ, C - ghosts.shape[1]), f32)
    ghost_rows(jnp.concatenate([ghosts, padding], axis=1), z_lower, z_higher)
    for n in range(3):
        own_force[n : n + 1, :] = sums[n]


def final_kernel(own, plus, minus, place, own_force, forces):
    pieces = jnp.concatenate([minus[...], plus[...]], axis=0)
    row_sum = own[...] + mm(place[...], pieces)
    forces[...] = own_force[...] - row_sum.T[0:3, :]


def spread(proj, up, down, pick_y, pick_z, near, far, ready):
    x = swap(up, down, "gx")
    sends = call(
        pick_y_kernel,
        [shape((GY, C), bf16)] * 2,
        [pltpu.VMEM((OFF_Y, C), bf16)],
    )(proj, *x, pick_y, ready[0])
    y = swap(*sends, "gy")
    sends = call(
        pick_z_kernel,
        [shape((GZ, C), bf16)] * 2,
        [pltpu.VMEM((OFF_Z, C), bf16)],
    )(proj, *x, *y, pick_z, ready[1])
    z = swap(*sends, "gz")
    low = call(
        low_gather_kernel, shape((C, PAIRS), bf16), [pltpu.VMEM((OFF_Z, C), bf16)]
    )(proj, *x, *y, near, far)
    return (*z, low)


def retract(terms, z_lower, z_higher, near, far, place_y, place_z, rest, ready=()):
    arrived = swap(z_higher, z_lower, "gz")
    kept = call(rest, shape((OFF_Z, C), f32))(terms, near, far)
    kept, y_lower, y_higher = call(
        return_z_kernel,
        [shape((UNPADDED, C), f32), shape((GY, C), bf16), shape((GY, C), bf16)],
    )(kept, *arrived, place_z)
    arrived = swap(y_higher, y_lower, "gy")
    own, x_lower, x_higher = call(
        return_y_kernel,
        [shape((ATOMS, C), f32), shape((GX, C), bf16), shape((GX, C), bf16)],
    )(kept, *arrived, place_y, *ready)
    arrived = swap(x_higher, x_lower, "gx")
    return (own, *arrived)


def local(
    atom_types,
    type_table,
    neighbor_index,
    neighbor_count,
    displacement,
    send_x,
    send_y,
    send_z,
    message_weight,
    self_weight,
    decay,
    energy_proj,
    energy_out,
):
    inputs = (
        atom_types.reshape(1, ATOMS),
        type_table,
        send_x,
        message_weight,
        send_y,
        send_z,
        neighbor_index.T,
        neighbor_count.reshape(1, ATOMS),
        jnp.swapaxes(displacement, 1, 2),
        decay,
        self_weight,
        energy_proj,
        energy_out.reshape(1, C),
    )
    inputs = [pltpu.with_memory_space_constraint(a, pltpu.HBM) for a in inputs]
    *loaded, features, proj, up, down, pick_x, place_x = call(
        first_kernel,
        [
            *[shape(a.shape, a.dtype) for a in inputs[3:]],
            shape((ATOMS, C), bf16),
            shape((ATOMS, C), bf16),
            shape((GX, C), bf16),
            shape((GX, C), bf16),
            shape((2 * GX, ATOMS), bf16),
            shape((ATOMS, 2 * GX), bf16),
        ],
        [
            pltpu.VMEM((128, C), f32),
            *[pltpu.VMEM(a.shape, a.dtype) for a in inputs[:3]],
            pltpu.SemaphoreType.DMA((LOADED + 1,)),
        ],
        in_specs=[pl.BlockSpec(memory_space=pltpu.HBM)] * LOADED,
    )(*inputs)
    message_weight, send_y, send_z, index, count, delta = loaded[:6]
    decay, self_weight, energy_proj, energy_row = loaded[6:]
    pick_y, pick_z, place_y, place_z = call(
        lists_kernel,
        [
            shape((2 * GY, OFF_Y), bf16),
            shape((2 * GZ, OFF_Z), bf16),
            shape((UNPADDED, 2 * GY), bf16),
            shape((OFF_Z, 2 * GZ), bf16),
        ],
    )(send_y, send_z)
    near, far = [
        call(lambda *refs, start=start: onehot_kernel(*refs, start=start), shape((OFF_Y, PAIRS), bf16))(
            index
        )
        for start in (0, OFF_Y)
    ]
    w0, slope, unit, radius, base = call(
        radial_kernel,
        [
            shape((C, PAIRS), bf16),
            shape((SLOTS, ATOMS), f32),
            shape((3, SLOTS, ATOMS), f32),
            shape((SLOTS, ATOMS), f32),
            shape((SLOTS, ATOMS), f32),
        ],
    )(count, delta, decay)
    weights = [w0]
    for layer in (1, 2):
        body = lambda *refs, layer=layer: later_weights_kernel(*refs, layer=layer)
        weights.append(call(body, shape((C, PAIRS), bf16))(radius, base, decay))
    w0, w1, w2 = weights
    lists = (pick_y, pick_z, near, far)
    saved = []
    ready = ((w0, near), (pick_y, w1), (pick_y, w2))
    for layer in range(2):
        ghosts = spread(proj, up, down, *lists, ready[layer])
        body = lambda *refs, layer=layer: layer_kernel(*refs, layer=layer)
        features, t, prod, proj, up, down = call(
            body,
            [
                shape((ATOMS, C), bf16),
                shape((ATOMS, C), f32),
                shape((C, PAIRS), bf16),
                shape((ATOMS, C), bf16),
                shape((GX, C), bf16),
                shape((GX, C), bf16),
            ],
        )(*ghosts, features, far, weights[layer], self_weight, message_weight, pick_x)
        saved.append((t, prod))
    ghosts = spread(proj, up, down, *lists, ready[2])
    row_shapes = [shape((ATOMS, C), f32), shape((ATOMS, C), f32)]
    terms_shape = shape((C, PAIRS), bf16)
    ghost_shapes = [shape((GZ, C), bf16), shape((GZ, C), bf16)]
    radius_shape = shape((SLOTS, ATOMS), f32)
    total, prod = call(top_sum_kernel, [shape((C, ATOMS), f32), terms_shape])(*ghosts, far, w2)
    readout, gradient, pg, *back = call(
        top_kernel, [shape((C, ATOMS), f32), *row_shapes, terms_shape, *ghost_shapes]
    )(total, features, far, w2, self_weight, energy_proj, energy_row)
    places = (near, far, place_y, place_z)
    sums = lambda *refs: sums_kernel(*refs, layer=2)
    radius_grad, energy = call(sums, [radius_shape, shape((1, ATOMS), f32)])(
        prod, pg, decay, slope, readout, energy_row
    )
    returned = retract(*back, *places, rest_kernel, [radius_grad])
    t, prod = saved[1]
    gradient, pg, *back = call(middle_kernel, [*row_shapes, terms_shape, *ghost_shapes])(
        *returned, place_x, gradient, pg, self_weight, message_weight, t, w1, far
    )
    sums = lambda *refs: sums_kernel(*refs, layer=1)
    radius_grad = call(sums, radius_shape)(prod, pg, decay, slope, radius_grad)
    returned = retract(*back, *places, rest_kernel, [radius_grad])
    t, prod = saved[0]
    own_force, *back = call(
        bottom_kernel,
        [shape((3, ATOMS), f32), shape((16, PAIRS), bf16), *ghost_shapes],
        [pltpu.VMEM((16, PAIRS), f32)],
    )(
        *returned, place_x, gradient, pg, self_weight, message_weight, t, prod, decay, slope,
        far, radius_grad, unit,
    )
    returned = retract(*back, *places, force_rest_kernel)
    forces = call(final_kernel, shape((3, ATOMS), f32))(*returned, place_x, own_force)
    return (energy.reshape(ATOMS), forces)


def solution(mesh):
    split = ("gx", "gy", "gz")
    return jax.shard_map(
        local,
        mesh=mesh,
        in_specs=(
            P(split),
            P(),
            P(split, None),
            P(split),
            P(None, split, None),
            P(None, split),
            P(None, split),
            P(None, split),
            P(),
            P(),
            P(),
            P(),
            P(),
        ),
        out_specs=(P(split), P(None, split)),
        check_vma=False,
    )
```

```python
import math

import jax
import jax.numpy as jnp
from jax import lax
from jax.experimental import pallas as pl
from jax.experimental.pallas import tpu as pltpu
from jax.sharding import PartitionSpec as P

cutoff = 4.0
ATOMS = 128
C = 128
SLOTS = 48
GX, GY, GZ = 32, 64, 64
LOADED = 13
OFF_X, OFF_Y, OFF_Z, ROWS = 128, 256, 384, 512
PAD = 64
UNPADDED = ATOMS + 2 * GX
PAIRS = ATOMS * SLOTS
CHUNK = 2 * ATOMS
TIERS = (20, 24, 28, SLOTS)
f32, bf16, i32 = jnp.float32, jnp.bfloat16, jnp.int32
NT = (((1,), (1,)), ((), ()))


def shape(dims, dtype):
    return jax.ShapeDtypeStruct(dims, dtype)


def call(body, outs, scratch=(), limit=4, **more):
    return pl.pallas_call(
        body,
        out_shape=outs,
        **more,
        scratch_shapes=list(scratch),
        compiler_params=pltpu.CompilerParams(vmem_limit_bytes=limit * 1024 * 1024),
    )


def along(axis, distance):
    size = lax.axis_size(axis)
    return [(i, (i + distance) % size) for i in range(size)]


def swap(to_higher, to_lower, axis):
    from_lower = lax.ppermute(to_higher, axis, along(axis, 1))
    from_higher = lax.ppermute(to_lower, axis, along(axis, -1))
    return from_lower, from_higher


def mm(a, b):
    return jnp.dot(a, b, preferred_element_type=f32)


def mm_nt(a, b):
    return lax.dot_general(a, b, NT, preferred_element_type=f32)


def split_nt(a, b):
    high = a.astype(bf16)
    low = (a - high.astype(f32)).astype(bf16)
    return mm_nt(b, high) + mm_nt(b, low)


def columns(row):
    return jnp.broadcast_to(row, (128, row.shape[1])).T


def padded(ids):
    return jnp.where(ids >= UNPADDED, ids + PAD, ids)


def picker(lists, extent):
    ids = jnp.concatenate([columns(lists[n : n + 1, :].astype(f32)) for n in range(2)], axis=0)
    parts = []
    for start in range(0, extent, 128):
        lane = (lax.broadcasted_iota(i32, ids.shape, 1) + start).astype(f32)
        parts.append(jnp.where(ids == lane, 1.0, 0.0).astype(bf16))
    return jnp.concatenate(parts, axis=1) if len(parts) > 1 else parts[0]


def place_into(out, lists):
    n = lists.shape[1]
    sub = lax.broadcasted_iota(i32, (out.shape[0], n), 0)
    for side in range(2):
        out[:, side * n : (side + 1) * n] = jnp.where(
            sub == lists[side : side + 1, :], 1.0, 0.0
        ).astype(bf16)


def for_slots(count, body):
    held = count[0, 0]
    below = -1.0
    for n in TIERS:
        pl.when((held > below) & (held <= n))(lambda n=n: body(n))
        below = float(n)


def first_kernel(*refs):
    inputs, refs = refs[:LOADED], refs[LOADED:]
    kept, refs = refs[: LOADED - 3], refs[LOADED - 3 :]
    feat, proj, up, down, pick_x, place_x, rows, types, table, send_x, sems = refs
    weight = kept[0]
    pairs = [(inputs[3].at[0], weight.at[0])]
    pairs += zip(inputs[:3], (types, table, send_x))
    pairs += [(inputs[3].at[1:], weight.at[1:])]
    pairs += zip(inputs[4:], kept[1:])
    moves = [pltpu.make_async_copy(a, b, sems.at[i]) for i, (a, b) in enumerate(pairs)]
    for move in moves:
        move.start()
    rows[...] = jnp.zeros_like(rows)
    for move in moves[:4]:
        move.wait()
    rows[0:6, :] = table[...].astype(f32)
    kinds = columns(types[...].astype(f32))
    lane = lax.broadcasted_iota(i32, (ATOMS, 128), 1).astype(f32)
    onehot = jnp.where(kinds == lane, 1.0, 0.0).astype(bf16)
    per_type = rows[...].astype(bf16)
    projected = mm(per_type, weight[0]).astype(bf16)
    pick = picker(send_x[...], ATOMS)
    chosen = mm(mm(pick, onehot).astype(bf16), projected).astype(bf16)
    up[...] = chosen[0:GX]
    down[...] = chosen[GX:]
    proj[...] = mm(onehot, projected).astype(bf16)
    feat[...] = mm(onehot, per_type).astype(bf16)
    pick_x[...] = pick
    place_into(place_x, send_x[...])
    for move in moves[4:]:
        move.wait()


def lists_kernel(send_y, send_z, pick_y, pick_z, place_y, place_z):
    ids_y, ids_z = send_y[...], padded(send_z[...])
    pick_y[...] = picker(ids_y, OFF_Y)
    pick_z[...] = picker(ids_z, OFF_Z)
    place_into(place_y, ids_y)
    place_into(place_z, ids_z)


def order_kernel(index, count, delta, ids_out, alive_out, delta_out, most):
    slot = lax.broadcasted_iota(i32, (SLOTS, ATOMS), 0)
    ids = padded(index[...])
    alive = slot < count[...]
    first = jnp.where(alive & (ids >= OFF_Z), 1.0, 0.0)
    rows = lax.broadcasted_iota(i32, (SLOTS, SLOTS), 0)
    columns_ = lax.broadcasted_iota(i32, (SLOTS, SLOTS), 1)
    earlier = jnp.where(columns_ < rows, 1.0, 0.0).astype(bf16)
    before = mm(earlier, first.astype(bf16))
    number = jnp.sum(first, axis=0, keepdims=True)
    place = jnp.where(first > 0.0, before, number + slot.astype(f32) - before)
    most[...] = jnp.broadcast_to(jnp.max(number, axis=1, keepdims=True), most.shape)
    coded = jnp.where(alive, ids, ids + 2 * ROWS).astype(f32)
    held = [coded, delta[0], delta[1], delta[2]]
    sorted_rows = [[], [], [], []]
    for k in range(SLOTS):
        here = place == float(k)
        for n in range(4):
            sorted_rows[n].append(jnp.sum(jnp.where(here, held[n], 0.0), axis=0, keepdims=True))
    coded, *moved = [jnp.concatenate(r, axis=0) for r in sorted_rows]
    live = coded < float(2 * ROWS)
    alive_out[...] = jnp.where(live, 1.0, 0.0)
    ids_out[...] = jnp.where(live, coded, coded - float(2 * ROWS)).astype(i32)
    for n in range(3):
        delta_out[n] = moved[n]


def onehot_kernel(index, onehot, *, start):
    ids = index[...]
    sub = lax.broadcasted_iota(i32, (OFF_Y, ATOMS), 0) + start
    for k in range(SLOTS):
        here = slice(k * ATOMS, (k + 1) * ATOMS)
        onehot[:, here] = jnp.where(sub == ids[k : k + 1, :], 1.0, 0.0).astype(bf16)


def weights_into(out, radius, base, decay_row):
    rate = columns(-decay_row)
    for k in range(SLOTS):
        here = slice(k * ATOMS, (k + 1) * ATOMS)
        out[:, here] = (base[k : k + 1, :] * jnp.exp(rate * radius[k : k + 1, :])).astype(bf16)


def radial_kernel(alive, delta, decay, w, slope, unit, radius_out, base_out):
    d = [delta[n] for n in range(3)]
    radius = jnp.sqrt(d[0] * d[0] + d[1] * d[1] + d[2] * d[2])
    half = (math.pi / (2.0 * cutoff)) * radius
    cosine, sine = jnp.cos(half), jnp.sin(half)
    base = alive[...] * (cosine * cosine) * (1.0 / math.sqrt(SLOTS)) / radius
    slope[...] = -(math.pi / cutoff) * sine / cosine - 1.0 / radius
    for n in range(3):
        unit[n] = d[n] / radius
    radius_out[...] = radius
    base_out[...] = base
    weights_into(w, radius, base, decay[0:1, :])


def later_weights_kernel(radius, base, decay, w, *, layer):
    weights_into(w, radius[...], base[...], decay[layer : layer + 1, :])


def pick_y_kernel(proj, lower, higher, pick, *refs):
    up, down, table = refs[-3:]
    table[0:ATOMS] = proj[...]
    table[OFF_X : OFF_X + GX] = lower[...]
    table[OFF_X + GX : OFF_X + 2 * GX] = higher[...]
    table[OFF_X + 2 * GX : OFF_Y] = jnp.zeros((PAD, C), bf16)
    chosen = mm(pick[...], table[...]).astype(bf16)
    up[...] = chosen[0:GY]
    down[...] = chosen[GY:]


def pick_z_kernel(proj, x_lower, x_higher, y_lower, y_higher, pick, *refs):
    up, down, table = refs[-3:]
    table[0:ATOMS] = proj[...]
    table[OFF_X : OFF_X + GX] = x_lower[...]
    table[OFF_X + GX : OFF_X + 2 * GX] = x_higher[...]
    table[OFF_X + 2 * GX : OFF_Y] = jnp.zeros((PAD, C), bf16)
    table[OFF_Y : OFF_Y + GY] = y_lower[...]
    table[OFF_Y + GY : OFF_Z] = y_higher[...]
    chosen = mm(pick[...], table[...]).astype(bf16)
    up[...] = chosen[0:GZ]
    down[...] = chosen[GZ:]


def turned(rows):
    return rows.astype(f32).T.astype(bf16)


def low_gather_kernel(
    proj, x_lower, x_higher, y_lower, y_higher, near, far, w, prod, total_out, table
):
    table[0:ATOMS] = proj[...]
    table[OFF_X : OFF_X + GX] = x_lower[...]
    table[OFF_X + GX : OFF_X + 2 * GX] = x_higher[...]
    table[OFF_X + 2 * GX : OFF_Y] = jnp.zeros((PAD, C), bf16)
    table[OFF_Y : OFF_Y + GY] = y_lower[...]
    table[OFF_Y + GY : OFF_Z] = y_higher[...]
    rows = turned(table[...])
    total = jnp.zeros((C, ATOMS), f32)
    for start in range(0, PAIRS, CHUNK):
        here = slice(start, start + CHUNK)
        gathered = mm(rows[:, 0:OFF_Y], near[:, here])
        gathered = gathered + mm(rows[:, OFF_Y:OFF_Z], far[0 : OFF_Z - OFF_Y, here])
        m = gathered.astype(bf16) * w[:, here]
        prod[:, here] = m
        total = total + (m[:, 0:ATOMS] + m[:, ATOMS:]).astype(f32)
    total_out[...] = total


def forward_part(z_lower, z_higher, low_prod, low_total, most, far, w, prod, total_out):
    rows = turned(jnp.concatenate([z_lower[...], z_higher[...]], axis=0))

    def add(n):
        total = low_total[...]
        for start in range(0, n * ATOMS, CHUNK):
            here = slice(start, start + CHUNK)
            m = mm(rows, far[OFF_Z - OFF_Y :, here]).astype(bf16) * w[:, here]
            prod[:, here] = low_prod[:, here] + m
            total = total + (m[:, 0:ATOMS] + m[:, ATOMS:]).astype(f32)
        total_out[...] = total

    for_slots(most, add)


def next_rows(total, feat, weight):
    rows = feat[...]
    t = jnp.tanh(total + mm(rows, weight).T)
    return t, rows.astype(f32).T + t


def layer_kernel(
    z_lower, z_higher, low_prod, low_total, most, feat, far, w, self_weight, next_weight, pick_x,
    prod, new_feat, tanh_out, new_proj, up, down, total, *, layer,
):
    forward_part(z_lower, z_higher, low_prod, low_total, most, far, w, prod, total)
    t, features = next_rows(total[...], feat, self_weight[layer])
    tanh_out[...] = t
    features = features.T.astype(bf16)
    new_feat[...] = features
    projected = mm(features, next_weight[layer + 1]).astype(bf16)
    new_proj[...] = projected
    chosen = mm(pick_x[...], projected).astype(bf16)
    up[...] = chosen[0:GX]
    down[...] = chosen[GX:]


def sum_rows(decay_row):
    high = decay_row.astype(bf16).astype(f32)
    rows = [jnp.ones_like(decay_row), high, decay_row - high, jnp.zeros((13, C), f32)]
    return jnp.concatenate(rows, axis=0).astype(bf16)


def backward_sums(prod, start, wide, rows, slope):
    s = mm(rows, prod[:, start : start + CHUNK] * wide)
    out = []
    for inner in range(0, CHUNK, ATOMS):
        k = (start + inner) // ATOMS
        here = slice(inner, inner + ATOMS)
        out.append(slope[k : k + 1, :] * s[0:1, here] - (s[1:2, here] + s[2:3, here]))
    return out


def wide_rows(x):
    return jnp.concatenate([x] * (CHUNK // ATOMS), axis=1)


def ghost_rows(rows, z_lower, z_higher):
    z_lower[...] = rows[0:GZ].astype(bf16)
    z_higher[...] = rows[GZ:].astype(bf16)


def mm_split(a, b):
    high = b.astype(bf16)
    low = (b - high.astype(f32)).astype(bf16)
    return mm(a, high) + mm(a, low)


def terms_into(terms, pg, w, n):
    wide = wide_rows(pg.astype(bf16))
    for start in range(0, n * ATOMS, CHUNK):
        here = slice(start, start + CHUNK)
        terms[:, here] = w[:, here] * wide


def terms_part(pg, w, most, far, terms, z_lower, z_higher):
    def add(n):
        terms_into(terms, pg, w, n)
        here = slice(0, n * ATOMS)
        ghost_rows(mm_nt(far[OFF_Z - OFF_Y :, here], terms[:, here]), z_lower, z_higher)

    for_slots(most, add)


def rest_kernel(pg, w, near, far, kept, terms):
    terms_into(terms, pg[...], w, SLOTS)
    kept[0:OFF_Y, :] = mm_nt(near[...], terms[...])
    kept[OFF_Y:OFF_Z, :] = mm_nt(far[0 : OFF_Z - OFF_Y, :], terms[...])


def force_rest_kernel(terms, near, far, kept):
    kept[...] = jnp.zeros_like(kept)
    n = terms.shape[0]
    kept[0:OFF_Y, 0:n] = mm_nt(near[...], terms[...])
    kept[OFF_Y:OFF_Z, 0:n] = mm_nt(far[0 : OFF_Z - OFF_Y, :], terms[...])


def sums_kernel(prod, pg, decay, slope, *refs, layer):
    wide, rows = wide_rows(pg[...].astype(bf16)), sum_rows(decay[layer : layer + 1, :])
    parts = []
    for start in range(0, PAIRS, CHUNK):
        parts += backward_sums(prod, start, wide, rows, slope)
    total = jnp.concatenate(parts, axis=0)
    if layer == 2:
        readout, out_row, radius_grad, energy = refs
        energy[...] = jnp.sum(readout[...] * columns(out_row[...]), axis=0, keepdims=True)
        radius_grad[...] = total
    else:
        before, radius_grad = refs
        radius_grad[...] = before[...] + total


def top_sum_kernel(z_lower, z_higher, low_prod, low_total, most, far, w, prod, total):
    forward_part(z_lower, z_higher, low_prod, low_total, most, far, w, prod, total)


def top_kernel(
    total, feat, most, far, w, self_weight, energy_proj, energy_out,
    readout_out, gradient_out, pg_out, z_lower, z_higher, terms,
):
    t, features = next_rows(total[...], feat, self_weight[2])
    readout = jnp.tanh(mm(turned(energy_proj[...]), features.astype(bf16)))
    readout_out[...] = readout
    upstream = (1.0 - readout * readout) * columns(energy_out[...])
    gradient = mm_split(energy_proj[...], upstream)
    pg = gradient * (1.0 - t * t)
    gradient_out[...] = gradient
    pg_out[...] = pg
    terms_part(pg, w, most, far, terms, z_lower, z_higher)


def return_z_kernel(kept, plus, minus, place, rest, y_lower, y_higher):
    pieces = jnp.concatenate([minus[...], plus[...]], axis=0)
    total = kept[...] + mm(place[...], pieces)
    rest[...] = total[0:UNPADDED]
    y_lower[...] = total[OFF_Y : OFF_Y + GY].astype(bf16)
    y_higher[...] = total[OFF_Y + GY : OFF_Z].astype(bf16)


def return_y_kernel(kept, plus, minus, place, *refs):
    own, x_lower, x_higher = refs[-3:]
    pieces = jnp.concatenate([minus[...], plus[...]], axis=0)
    total = kept[...] + mm(place[...], pieces)
    own[...] = total[0:ATOMS]
    x_lower[...] = total[OFF_X : OFF_X + GX].astype(bf16)
    x_higher[...] = total[OFF_X + GX :].astype(bf16)


def down_step(own, plus, minus, place, gradient, pg, self_weight, message_weight, layer):
    pieces = jnp.concatenate([minus[...], plus[...]], axis=0)
    row_sum = own[...] + mm(place[...], pieces)
    return (
        gradient[...]
        + mm_split(self_weight[layer], pg[...])
        + split_nt(row_sum, message_weight[layer])
    )


def middle_kernel(
    own, plus, minus, place, gradient_in, pg_in, self_weight, message_weight, t, w, most, far,
    gradient_out, pg_out, z_lower, z_higher, terms,
):
    gradient = down_step(own, plus, minus, place, gradient_in, pg_in, self_weight, message_weight, 2)
    activation = t[...]
    pg = gradient * (1.0 - activation * activation)
    gradient_out[...] = gradient
    pg_out[...] = pg
    terms_part(pg, w, most, far, terms, z_lower, z_higher)


def bottom_kernel(
    own, plus, minus, place, gradient_in, pg_in, self_weight, message_weight,
    t, prod, decay, slope, far, radius_in, unit,
    own_force, terms, z_lower, z_higher, rows,
):
    gradient = down_step(own, plus, minus, place, gradient_in, pg_in, self_weight, message_weight, 1)
    activation = t[...]
    pg = gradient * (1.0 - activation * activation)
    wide, weighted = wide_rows(pg.astype(bf16)), sum_rows(decay[0:1, :])
    rows[...] = jnp.zeros_like(rows)
    sums = [jnp.zeros((1, ATOMS), f32)] * 3
    for start in range(0, PAIRS, CHUNK):
        for i, part in enumerate(backward_sums(prod, start, wide, weighted, slope)):
            k = start // ATOMS + i
            total = radius_in[k : k + 1, :] + part
            for n in range(3):
                pushed = total * unit[n, k : k + 1, :]
                sums[n] = sums[n] + pushed
                rows[n : n + 1, k * ATOMS : (k + 1) * ATOMS] = pushed
    terms[...] = rows[...].astype(bf16)
    ghosts = mm_nt(far[OFF_Z - OFF_Y :, :], terms[...])
    padding = jnp.zeros((2 * GZ, C - ghosts.shape[1]), f32)
    ghost_rows(jnp.concatenate([ghosts, padding], axis=1), z_lower, z_higher)
    for n in range(3):
        own_force[n : n + 1, :] = sums[n]


def final_kernel(own, plus, minus, place, own_force, forces):
    pieces = jnp.concatenate([minus[...], plus[...]], axis=0)
    row_sum = own[...] + mm(place[...], pieces)
    forces[...] = own_force[...] - row_sum.T[0:3, :]


def spread(proj, up, down, pick_y, pick_z, near, far, w, ready):
    x = swap(up, down, "gx")
    sends = call(
        pick_y_kernel,
        [shape((GY, C), bf16)] * 2,
        [pltpu.VMEM((OFF_Y, C), bf16)],
    )(proj, *x, pick_y, *ready[0])
    y = swap(*sends, "gy")
    sends = call(
        pick_z_kernel,
        [shape((GZ, C), bf16)] * 2,
        [pltpu.VMEM((OFF_Z, C), bf16)],
    )(proj, *x, *y, pick_z, *ready[1])
    z = swap(*sends, "gz")
    low = call(
        low_gather_kernel,
        [shape((C, PAIRS), bf16), shape((C, ATOMS), f32)],
        [pltpu.VMEM((OFF_Z, C), bf16)],
    )(proj, *x, *y, near, far, w)
    return (*z, *low)


def retract(rest, z_lower, z_higher, place_y, place_z, ready=()):
    arrived = swap(z_higher, z_lower, "gz")
    kept = rest()
    kept, y_lower, y_higher = call(
        return_z_kernel,
        [shape((UNPADDED, C), f32), shape((GY, C), bf16), shape((GY, C), bf16)],
    )(kept, *arrived, place_z)
    arrived = swap(y_higher, y_lower, "gy")
    own, x_lower, x_higher = call(
        return_y_kernel,
        [shape((ATOMS, C), f32), shape((GX, C), bf16), shape((GX, C), bf16)],
    )(kept, *arrived, place_y, *ready)
    arrived = swap(x_higher, x_lower, "gx")
    return (own, *arrived)


def local(
    atom_types,
    type_table,
    neighbor_index,
    neighbor_count,
    displacement,
    send_x,
    send_y,
    send_z,
    message_weight,
    self_weight,
    decay,
    energy_proj,
    energy_out,
):
    inputs = (
        atom_types.reshape(1, ATOMS),
        type_table,
        send_x,
        message_weight,
        send_y,
        send_z,
        neighbor_index.T,
        neighbor_count.reshape(1, ATOMS),
        jnp.swapaxes(displacement, 1, 2),
        decay,
        self_weight,
        energy_proj,
        energy_out.reshape(1, C),
    )
    inputs = [pltpu.with_memory_space_constraint(a, pltpu.HBM) for a in inputs]
    *loaded, features, proj, up, down, pick_x, place_x = call(
        first_kernel,
        [
            *[shape(a.shape, a.dtype) for a in inputs[3:]],
            shape((ATOMS, C), bf16),
            shape((ATOMS, C), bf16),
            shape((GX, C), bf16),
            shape((GX, C), bf16),
            shape((2 * GX, ATOMS), bf16),
            shape((ATOMS, 2 * GX), bf16),
        ],
        [
            pltpu.VMEM((128, C), f32),
            *[pltpu.VMEM(a.shape, a.dtype) for a in inputs[:3]],
            pltpu.SemaphoreType.DMA((LOADED + 1,)),
        ],
        in_specs=[pl.BlockSpec(memory_space=pltpu.HBM)] * LOADED,
    )(*inputs)
    message_weight, send_y, send_z, index, count, delta = loaded[:6]
    decay, self_weight, energy_proj, energy_row = loaded[6:]
    pick_y, pick_z, place_y, place_z = call(
        lists_kernel,
        [
            shape((2 * GY, OFF_Y), bf16),
            shape((2 * GZ, OFF_Z), bf16),
            shape((UNPADDED, 2 * GY), bf16),
            shape((OFF_Z, 2 * GZ), bf16),
        ],
    )(send_y, send_z)
    ids, alive, delta, most = call(
        order_kernel,
        [
            shape((SLOTS, ATOMS), i32),
            shape((SLOTS, ATOMS), f32),
            shape((3, SLOTS, ATOMS), f32),
            shape((1, ATOMS), f32),
        ],
    )(index, count, delta)
    near, far = [
        call(lambda *refs, start=start: onehot_kernel(*refs, start=start), shape((OFF_Y, PAIRS), bf16))(
            ids
        )
        for start in (0, OFF_Y)
    ]
    w0, slope, unit, radius, base = call(
        radial_kernel,
        [
            shape((C, PAIRS), bf16),
            shape((SLOTS, ATOMS), f32),
            shape((3, SLOTS, ATOMS), f32),
            shape((SLOTS, ATOMS), f32),
            shape((SLOTS, ATOMS), f32),
        ],
    )(alive, delta, decay)
    weights = [w0]
    for layer in (1, 2):
        body = lambda *refs, layer=layer: later_weights_kernel(*refs, layer=layer)
        weights.append(call(body, shape((C, PAIRS), bf16))(radius, base, decay))
    w0, w1, w2 = weights
    lists = (pick_y, pick_z, near, far)
    saved = []
    ready = (((ids,), (w0, near)), ((), (w1,)), ((), (w2,)))
    for layer in range(2):
        ghosts = spread(proj, up, down, *lists, weights[layer], ready[layer])
        body = lambda *refs, layer=layer: layer_kernel(*refs, layer=layer)
        prod, features, t, proj, up, down = call(
            body,
            [
                shape((C, PAIRS), bf16),
                shape((ATOMS, C), bf16),
                shape((C, ATOMS), f32),
                shape((ATOMS, C), bf16),
                shape((GX, C), bf16),
                shape((GX, C), bf16),
            ],
            [pltpu.VMEM((C, ATOMS), f32)],
            input_output_aliases={2: 0},
        )(*ghosts, most, features, far, weights[layer], self_weight, message_weight, pick_x)
        saved.append((t, prod))
    ghosts = spread(proj, up, down, *lists, w2, ready[2])
    square, terms_shape = shape((C, ATOMS), f32), shape((C, PAIRS), bf16)
    ghost_shapes = [shape((GZ, C), bf16), shape((GZ, C), bf16)]
    radius_shape, kept_shape = shape((SLOTS, ATOMS), f32), shape((OFF_Z, C), f32)
    room = [pltpu.VMEM((C, PAIRS), bf16)]
    places = (place_y, place_z)

    def rest(pg, w):
        return lambda: call(rest_kernel, kept_shape, room)(pg, w, near, far)

    prod, total = call(top_sum_kernel, [terms_shape, square], input_output_aliases={2: 0})(
        *ghosts, most, far, w2
    )
    readout, gradient, pg, *back = call(top_kernel, [square, square, square, *ghost_shapes], room)(
        total, features, most, far, w2, self_weight, energy_proj, energy_row
    )
    sums = lambda *refs: sums_kernel(*refs, layer=2)
    radius_grad, energy = call(sums, [radius_shape, shape((1, ATOMS), f32)])(
        prod, pg, decay, slope, readout, energy_row
    )
    returned = retract(rest(pg, w2), *back, *places, [radius_grad])
    t, prod = saved[1]
    gradient, pg, *back = call(middle_kernel, [square, square, *ghost_shapes], room)(
        *returned, place_x, gradient, pg, self_weight, message_weight, t, w1, most, far
    )
    sums = lambda *refs: sums_kernel(*refs, layer=1)
    radius_grad = call(sums, radius_shape)(prod, pg, decay, slope, radius_grad)
    returned = retract(rest(pg, w1), *back, *places, [radius_grad])
    t, prod = saved[0]
    own_force, terms, *back = call(
        bottom_kernel,
        [shape((3, ATOMS), f32), shape((16, PAIRS), bf16), *ghost_shapes],
        [pltpu.VMEM((16, PAIRS), f32)],
    )(
        *returned, place_x, gradient, pg, self_weight, message_weight, t, prod, decay, slope,
        far, radius_grad, unit,
    )
    rest = lambda: call(force_rest_kernel, kept_shape)(terms, near, far)
    returned = retract(rest, *back, *places)
    forces = call(final_kernel, shape((3, ATOMS), f32))(*returned, place_x, own_force)
    return (energy.reshape(ATOMS), forces)


def solution(mesh):
    split = ("gx", "gy", "gz")
    return jax.shard_map(
        local,
        mesh=mesh,
        in_specs=(
            P(split),
            P(),
            P(split, None),
            P(split),
            P(None, split, None),
            P(None, split),
            P(None, split),
            P(None, split),
            P(),
            P(),
            P(),
            P(),
            P(),
        ),
        out_specs=(P(split), P(None, split)),
        check_vma=False,
    )
```

```python
import math

import jax
import jax.numpy as jnp
from jax import lax
from jax.experimental import pallas as pl
from jax.experimental.pallas import tpu as pltpu
from jax.sharding import PartitionSpec as P

cutoff = 4.0
ATOMS = 128
C = 128
SLOTS = 48
GX, GY, GZ = 32, 64, 64
LOADED = 13
OFF_X, OFF_Y, OFF_Z, ROWS = 128, 256, 384, 512
PAD = 64
UNPADDED = ATOMS + 2 * GX
PAIRS = ATOMS * SLOTS
CHUNK = 2 * ATOMS
TIERS = (20, 24, 28, SLOTS)
f32, bf16, i32 = jnp.float32, jnp.bfloat16, jnp.int32
NT = (((1,), (1,)), ((), ()))


def shape(dims, dtype):
    return jax.ShapeDtypeStruct(dims, dtype)


def call(body, outs, scratch=(), limit=4, **more):
    return pl.pallas_call(
        body,
        out_shape=outs,
        **more,
        scratch_shapes=list(scratch),
        compiler_params=pltpu.CompilerParams(vmem_limit_bytes=limit * 1024 * 1024),
    )


def along(axis, distance):
    size = lax.axis_size(axis)
    return [(i, (i + distance) % size) for i in range(size)]


def swap(to_higher, to_lower, axis):
    from_lower = lax.ppermute(to_higher, axis, along(axis, 1))
    from_higher = lax.ppermute(to_lower, axis, along(axis, -1))
    return from_lower, from_higher


def mm(a, b):
    return jnp.dot(a, b, preferred_element_type=f32)


def mm_nt(a, b):
    return lax.dot_general(a, b, NT, preferred_element_type=f32)


def split_nt(a, b):
    high = a.astype(bf16)
    low = (a - high.astype(f32)).astype(bf16)
    return mm_nt(b, high) + mm_nt(b, low)


def columns(row):
    return jnp.broadcast_to(row, (128, row.shape[1])).T


def padded(ids):
    return jnp.where(ids >= UNPADDED, ids + PAD, ids)


def picker(lists, extent):
    ids = jnp.concatenate([columns(lists[n : n + 1, :].astype(f32)) for n in range(2)], axis=0)
    parts = []
    for start in range(0, extent, 128):
        lane = (lax.broadcasted_iota(i32, ids.shape, 1) + start).astype(f32)
        parts.append(jnp.where(ids == lane, 1.0, 0.0).astype(bf16))
    return jnp.concatenate(parts, axis=1) if len(parts) > 1 else parts[0]


def place_into(out, lists):
    n = lists.shape[1]
    sub = lax.broadcasted_iota(i32, (out.shape[0], n), 0)
    for side in range(2):
        out[:, side * n : (side + 1) * n] = jnp.where(
            sub == lists[side : side + 1, :], 1.0, 0.0
        ).astype(bf16)


def for_slots(count, body):
    held = count[0, 0]
    below = -1.0
    for n in TIERS:
        pl.when((held > below) & (held <= n))(lambda n=n: body(n))
        below = float(n)


def first_kernel(*refs):
    inputs, refs = refs[:LOADED], refs[LOADED:]
    kept, refs = refs[: LOADED - 3], refs[LOADED - 3 :]
    feat, proj, up, down, pick_x, place_x, rows, types, table, send_x, sems = refs
    weight = kept[0]
    pairs = [(inputs[3].at[0], weight.at[0])]
    pairs += zip(inputs[:3], (types, table, send_x))
    pairs += [(inputs[3].at[1:], weight.at[1:])]
    pairs += zip(inputs[4:], kept[1:])
    moves = [pltpu.make_async_copy(a, b, sems.at[i]) for i, (a, b) in enumerate(pairs)]
    for move in moves:
        move.start()
    rows[...] = jnp.zeros_like(rows)
    for move in moves[:4]:
        move.wait()
    rows[0:6, :] = table[...].astype(f32)
    kinds = columns(types[...].astype(f32))
    lane = lax.broadcasted_iota(i32, (ATOMS, 128), 1).astype(f32)
    onehot = jnp.where(kinds == lane, 1.0, 0.0).astype(bf16)
    per_type = rows[...].astype(bf16)
    projected = mm(per_type, weight[0]).astype(bf16)
    pick = picker(send_x[...], ATOMS)
    chosen = mm(mm(pick, onehot).astype(bf16), projected).astype(bf16)
    up[...] = chosen[0:GX]
    down[...] = chosen[GX:]
    proj[...] = mm(onehot, projected).astype(bf16)
    feat[...] = mm(onehot, per_type).astype(bf16)
    pick_x[...] = pick
    place_into(place_x, send_x[...])
    for move in moves[4:]:
        move.wait()


def lists_kernel(send_y, send_z, pick_y, pick_z, place_y, place_z):
    ids_y, ids_z = send_y[...], padded(send_z[...])
    pick_y[...] = picker(ids_y, OFF_Y)
    pick_z[...] = picker(ids_z, OFF_Z)
    place_into(place_y, ids_y)
    place_into(place_z, ids_z)


def order_kernel(index, count, delta, ids_out, alive_out, delta_out, most):
    slot = lax.broadcasted_iota(i32, (SLOTS, ATOMS), 0)
    ids = padded(index[...])
    alive = slot < count[...]
    first = jnp.where(alive & (ids >= OFF_Z), 1.0, 0.0)
    rows = lax.broadcasted_iota(i32, (SLOTS, SLOTS), 0)
    columns_ = lax.broadcasted_iota(i32, (SLOTS, SLOTS), 1)
    earlier = jnp.where(columns_ < rows, 1.0, 0.0).astype(bf16)
    before = mm(earlier, first.astype(bf16))
    number = jnp.sum(first, axis=0, keepdims=True)
    place = jnp.where(first > 0.0, before, number + slot.astype(f32) - before)
    most[...] = jnp.broadcast_to(jnp.max(number, axis=1, keepdims=True), most.shape)
    coded = jnp.where(alive, ids, ids + 2 * ROWS).astype(f32)
    held = [coded, delta[0], delta[1], delta[2]]
    sorted_rows = [[], [], [], []]
    for k in range(SLOTS):
        here = place == float(k)
        for n in range(4):
            sorted_rows[n].append(jnp.sum(jnp.where(here, held[n], 0.0), axis=0, keepdims=True))
    coded, *moved = [jnp.concatenate(r, axis=0) for r in sorted_rows]
    live = coded < float(2 * ROWS)
    alive_out[...] = jnp.where(live, 1.0, 0.0)
    ids_out[...] = jnp.where(live, coded, coded - float(2 * ROWS)).astype(i32)
    for n in range(3):
        delta_out[n] = moved[n]


def onehot_kernel(index, onehot, *, start):
    ids = index[...]
    sub = lax.broadcasted_iota(i32, (OFF_Y, ATOMS), 0) + start
    for k in range(SLOTS):
        here = slice(k * ATOMS, (k + 1) * ATOMS)
        onehot[:, here] = jnp.where(sub == ids[k : k + 1, :], 1.0, 0.0).astype(bf16)


def weights_into(out, radius, base, decay_row):
    rate = columns(-decay_row)
    for k in range(SLOTS):
        here = slice(k * ATOMS, (k + 1) * ATOMS)
        out[:, here] = (base[k : k + 1, :] * jnp.exp(rate * radius[k : k + 1, :])).astype(bf16)


def radial_kernel(alive, delta, decay, w, slope, unit, radius_out, base_out):
    d = [delta[n] for n in range(3)]
    radius = jnp.sqrt(d[0] * d[0] + d[1] * d[1] + d[2] * d[2])
    half = (math.pi / (2.0 * cutoff)) * radius
    cosine, sine = jnp.cos(half), jnp.sin(half)
    base = alive[...] * (cosine * cosine) * (1.0 / math.sqrt(SLOTS)) / radius
    slope[...] = -(math.pi / cutoff) * sine / cosine - 1.0 / radius
    for n in range(3):
        unit[n] = d[n] / radius
    radius_out[...] = radius
    base_out[...] = base
    weights_into(w, radius, base, decay[0:1, :])


def later_weights_kernel(radius, base, decay, w, *, layer):
    weights_into(w, radius[...], base[...], decay[layer : layer + 1, :])


def pick_y_kernel(proj, lower, higher, pick, *refs):
    up, down, table = refs[-3:]
    table[0:ATOMS] = proj[...]
    table[OFF_X : OFF_X + GX] = lower[...]
    table[OFF_X + GX : OFF_X + 2 * GX] = higher[...]
    table[OFF_X + 2 * GX : OFF_Y] = jnp.zeros((PAD, C), bf16)
    chosen = mm(pick[...], table[...]).astype(bf16)
    up[...] = chosen[0:GY]
    down[...] = chosen[GY:]


def pick_z_kernel(proj, x_lower, x_higher, y_lower, y_higher, pick, *refs):
    up, down, table = refs[-3:]
    table[0:ATOMS] = proj[...]
    table[OFF_X : OFF_X + GX] = x_lower[...]
    table[OFF_X + GX : OFF_X + 2 * GX] = x_higher[...]
    table[OFF_X + 2 * GX : OFF_Y] = jnp.zeros((PAD, C), bf16)
    table[OFF_Y : OFF_Y + GY] = y_lower[...]
    table[OFF_Y + GY : OFF_Z] = y_higher[...]
    chosen = mm(pick[...], table[...]).astype(bf16)
    up[...] = chosen[0:GZ]
    down[...] = chosen[GZ:]


def turned(rows):
    return rows.astype(f32).T.astype(bf16)


def low_gather_kernel(
    proj, x_lower, x_higher, y_lower, y_higher, near, far, w, prod, total_out, table
):
    table[0:ATOMS] = proj[...]
    table[OFF_X : OFF_X + GX] = x_lower[...]
    table[OFF_X + GX : OFF_X + 2 * GX] = x_higher[...]
    table[OFF_X + 2 * GX : OFF_Y] = jnp.zeros((PAD, C), bf16)
    table[OFF_Y : OFF_Y + GY] = y_lower[...]
    table[OFF_Y + GY : OFF_Z] = y_higher[...]
    rows = turned(table[...])
    total = jnp.zeros((C, ATOMS), f32)
    for start in range(0, PAIRS, CHUNK):
        here = slice(start, start + CHUNK)
        gathered = mm(rows[:, 0:OFF_Y], near[:, here])
        gathered = gathered + mm(rows[:, OFF_Y:OFF_Z], far[0 : OFF_Z - OFF_Y, here])
        m = gathered.astype(bf16) * w[:, here]
        prod[:, here] = m
        total = total + (m[:, 0:ATOMS] + m[:, ATOMS:]).astype(f32)
    total_out[...] = total


def forward_kernel(z_lower, z_higher, low_prod, low_total, most, far, w, prod, total_out):
    rows = turned(jnp.concatenate([z_lower[...], z_higher[...]], axis=0))

    def add(n):
        total = low_total[...]
        for start in range(0, n * ATOMS, CHUNK):
            here = slice(start, start + CHUNK)
            m = mm(rows, far[OFF_Z - OFF_Y :, here]).astype(bf16) * w[:, here]
            prod[:, here] = low_prod[:, here] + m
            total = total + (m[:, 0:ATOMS] + m[:, ATOMS:]).astype(f32)
        total_out[...] = total

    for_slots(most, add)


def next_rows(total, feat, weight):
    rows = feat[...]
    t = jnp.tanh(total + mm(rows, weight).T)
    return t, rows.astype(f32).T + t


def layer_kernel(
    total, feat, self_weight, next_weight, pick_x,
    new_feat, tanh_out, new_proj, up, down, *, layer,
):
    t, features = next_rows(total[...], feat, self_weight[layer])
    tanh_out[...] = t
    features = features.T.astype(bf16)
    new_feat[...] = features
    projected = mm(features, next_weight[layer + 1]).astype(bf16)
    new_proj[...] = projected
    chosen = mm(pick_x[...], projected).astype(bf16)
    up[...] = chosen[0:GX]
    down[...] = chosen[GX:]


def sum_rows(decay_row):
    high = decay_row.astype(bf16).astype(f32)
    rows = [jnp.ones_like(decay_row), high, decay_row - high, jnp.zeros((13, C), f32)]
    return jnp.concatenate(rows, axis=0).astype(bf16)


def backward_sums(prod, start, wide, rows, slope):
    s = mm(rows, prod[:, start : start + CHUNK] * wide)
    out = []
    for inner in range(0, CHUNK, ATOMS):
        k = (start + inner) // ATOMS
        here = slice(inner, inner + ATOMS)
        out.append(slope[k : k + 1, :] * s[0:1, here] - (s[1:2, here] + s[2:3, here]))
    return out


def wide_rows(x):
    return jnp.concatenate([x] * (CHUNK // ATOMS), axis=1)


def ghost_rows(rows, z_lower, z_higher):
    z_lower[...] = rows[0:GZ].astype(bf16)
    z_higher[...] = rows[GZ:].astype(bf16)


def mm_split(a, b):
    high = b.astype(bf16)
    low = (b - high.astype(f32)).astype(bf16)
    return mm(a, high) + mm(a, low)


def terms_into(terms, pg, w, n):
    wide = wide_rows(pg.astype(bf16))
    for start in range(0, n * ATOMS, CHUNK):
        here = slice(start, start + CHUNK)
        terms[:, here] = w[:, here] * wide


def terms_part(pg, w, most, far, terms, z_lower, z_higher):
    def add(n):
        terms_into(terms, pg, w, n)
        here = slice(0, n * ATOMS)
        ghost_rows(mm_nt(far[OFF_Z - OFF_Y :, here], terms[:, here]), z_lower, z_higher)

    for_slots(most, add)


def rest_kernel(pg, w, near, far, kept, terms):
    terms_into(terms, pg[...], w, SLOTS)
    kept[0:OFF_Y, :] = mm_nt(near[...], terms[...])
    kept[OFF_Y:OFF_Z, :] = mm_nt(far[0 : OFF_Z - OFF_Y, :], terms[...])


def force_rest_kernel(terms, near, far, kept):
    kept[...] = jnp.zeros_like(kept)
    n = terms.shape[0]
    kept[0:OFF_Y, 0:n] = mm_nt(near[...], terms[...])
    kept[OFF_Y:OFF_Z, 0:n] = mm_nt(far[0 : OFF_Z - OFF_Y, :], terms[...])


def sums_kernel(prod, pg, decay, slope, *refs, layer):
    wide, rows = wide_rows(pg[...].astype(bf16)), sum_rows(decay[layer : layer + 1, :])
    parts = []
    for start in range(0, PAIRS, CHUNK):
        parts += backward_sums(prod, start, wide, rows, slope)
    total = jnp.concatenate(parts, axis=0)
    if layer == 2:
        readout, out_row, radius_grad, energy = refs
        energy[...] = jnp.sum(readout[...] * columns(out_row[...]), axis=0, keepdims=True)
        radius_grad[...] = total
    else:
        before, radius_grad = refs
        radius_grad[...] = before[...] + total


def top_kernel(
    total, feat, most, far, w, self_weight, energy_proj, energy_out,
    readout_out, gradient_out, pg_out, z_lower, z_higher, terms,
):
    t, features = next_rows(total[...], feat, self_weight[2])
    readout = jnp.tanh(mm(turned(energy_proj[...]), features.astype(bf16)))
    readout_out[...] = readout
    upstream = (1.0 - readout * readout) * columns(energy_out[...])
    gradient = mm_split(energy_proj[...], upstream)
    pg = gradient * (1.0 - t * t)
    gradient_out[...] = gradient
    pg_out[...] = pg
    terms_part(pg, w, most, far, terms, z_lower, z_higher)


def return_z_kernel(kept, plus, minus, place, rest, y_lower, y_higher):
    pieces = jnp.concatenate([minus[...], plus[...]], axis=0)
    total = kept[...] + mm(place[...], pieces)
    rest[...] = total[0:UNPADDED]
    y_lower[...] = total[OFF_Y : OFF_Y + GY].astype(bf16)
    y_higher[...] = total[OFF_Y + GY : OFF_Z].astype(bf16)


def return_y_kernel(kept, plus, minus, place, *refs):
    own, x_lower, x_higher = refs[-3:]
    pieces = jnp.concatenate([minus[...], plus[...]], axis=0)
    total = kept[...] + mm(place[...], pieces)
    own[...] = total[0:ATOMS]
    x_lower[...] = total[OFF_X : OFF_X + GX].astype(bf16)
    x_higher[...] = total[OFF_X + GX :].astype(bf16)


def down_step(own, plus, minus, place, gradient, pg, self_weight, message_weight, layer):
    pieces = jnp.concatenate([minus[...], plus[...]], axis=0)
    row_sum = own[...] + mm(place[...], pieces)
    return (
        gradient[...]
        + mm_split(self_weight[layer], pg[...])
        + split_nt(row_sum, message_weight[layer])
    )


def middle_kernel(
    own, plus, minus, place, gradient_in, pg_in, self_weight, message_weight, t, w, most, far,
    gradient_out, pg_out, z_lower, z_higher, terms,
):
    gradient = down_step(own, plus, minus, place, gradient_in, pg_in, self_weight, message_weight, 2)
    activation = t[...]
    pg = gradient * (1.0 - activation * activation)
    gradient_out[...] = gradient
    pg_out[...] = pg
    terms_part(pg, w, most, far, terms, z_lower, z_higher)


def bottom_kernel(
    own, plus, minus, place, gradient_in, pg_in, self_weight, message_weight,
    t, prod, decay, slope, far, radius_in, unit,
    own_force, terms, z_lower, z_higher, rows,
):
    gradient = down_step(own, plus, minus, place, gradient_in, pg_in, self_weight, message_weight, 1)
    activation = t[...]
    pg = gradient * (1.0 - activation * activation)
    wide, weighted = wide_rows(pg.astype(bf16)), sum_rows(decay[0:1, :])
    rows[...] = jnp.zeros_like(rows)
    sums = [jnp.zeros((1, ATOMS), f32)] * 3
    for start in range(0, PAIRS, CHUNK):
        for i, part in enumerate(backward_sums(prod, start, wide, weighted, slope)):
            k = start // ATOMS + i
            total = radius_in[k : k + 1, :] + part
            for n in range(3):
                pushed = total * unit[n, k : k + 1, :]
                sums[n] = sums[n] + pushed
                rows[n : n + 1, k * ATOMS : (k + 1) * ATOMS] = pushed
    terms[...] = rows[...].astype(bf16)
    ghosts = mm_nt(far[OFF_Z - OFF_Y :, :], terms[...])
    padding = jnp.zeros((2 * GZ, C - ghosts.shape[1]), f32)
    ghost_rows(jnp.concatenate([ghosts, padding], axis=1), z_lower, z_higher)
    for n in range(3):
        own_force[n : n + 1, :] = sums[n]


def final_kernel(own, plus, minus, place, own_force, forces):
    pieces = jnp.concatenate([minus[...], plus[...]], axis=0)
    row_sum = own[...] + mm(place[...], pieces)
    forces[...] = own_force[...] - row_sum.T[0:3, :]


def spread(proj, up, down, pick_y, pick_z, near, far, w, ready):
    x = swap(up, down, "gx")
    sends = call(
        pick_y_kernel,
        [shape((GY, C), bf16)] * 2,
        [pltpu.VMEM((OFF_Y, C), bf16)],
    )(proj, *x, pick_y, *ready[0])
    y = swap(*sends, "gy")
    sends = call(
        pick_z_kernel,
        [shape((GZ, C), bf16)] * 2,
        [pltpu.VMEM((OFF_Z, C), bf16)],
    )(proj, *x, *y, pick_z, *ready[1])
    z = swap(*sends, "gz")
    low = call(
        low_gather_kernel,
        [shape((C, PAIRS), bf16), shape((C, ATOMS), f32)],
        [pltpu.VMEM((OFF_Z, C), bf16)],
    )(proj, *x, *y, near, far, w)
    return (*z, *low)


def retract(rest, z_lower, z_higher, place_y, place_z, ready=()):
    arrived = swap(z_higher, z_lower, "gz")
    kept = rest()
    kept, y_lower, y_higher = call(
        return_z_kernel,
        [shape((UNPADDED, C), f32), shape((GY, C), bf16), shape((GY, C), bf16)],
    )(kept, *arrived, place_z)
    arrived = swap(y_higher, y_lower, "gy")
    own, x_lower, x_higher = call(
        return_y_kernel,
        [shape((ATOMS, C), f32), shape((GX, C), bf16), shape((GX, C), bf16)],
    )(kept, *arrived, place_y, *ready)
    arrived = swap(x_higher, x_lower, "gx")
    return (own, *arrived)


def local(
    atom_types,
    type_table,
    neighbor_index,
    neighbor_count,
    displacement,
    send_x,
    send_y,
    send_z,
    message_weight,
    self_weight,
    decay,
    energy_proj,
    energy_out,
):
    inputs = (
        atom_types.reshape(1, ATOMS),
        type_table,
        send_x,
        message_weight,
        send_y,
        send_z,
        neighbor_index.T,
        neighbor_count.reshape(1, ATOMS),
        jnp.swapaxes(displacement, 1, 2),
        decay,
        self_weight,
        energy_proj,
        energy_out.reshape(1, C),
    )
    inputs = [pltpu.with_memory_space_constraint(a, pltpu.HBM) for a in inputs]
    *loaded, features, proj, up, down, pick_x, place_x = call(
        first_kernel,
        [
            *[shape(a.shape, a.dtype) for a in inputs[3:]],
            shape((ATOMS, C), bf16),
            shape((ATOMS, C), bf16),
            shape((GX, C), bf16),
            shape((GX, C), bf16),
            shape((2 * GX, ATOMS), bf16),
            shape((ATOMS, 2 * GX), bf16),
        ],
        [
            pltpu.VMEM((128, C), f32),
            *[pltpu.VMEM(a.shape, a.dtype) for a in inputs[:3]],
            pltpu.SemaphoreType.DMA((LOADED + 1,)),
        ],
        in_specs=[pl.BlockSpec(memory_space=pltpu.HBM)] * LOADED,
    )(*inputs)
    message_weight, send_y, send_z, index, count, delta = loaded[:6]
    decay, self_weight, energy_proj, energy_row = loaded[6:]
    pick_y, pick_z, place_y, place_z = call(
        lists_kernel,
        [
            shape((2 * GY, OFF_Y), bf16),
            shape((2 * GZ, OFF_Z), bf16),
            shape((UNPADDED, 2 * GY), bf16),
            shape((OFF_Z, 2 * GZ), bf16),
        ],
    )(send_y, send_z)
    ids, alive, delta, most = call(
        order_kernel,
        [
            shape((SLOTS, ATOMS), i32),
            shape((SLOTS, ATOMS), f32),
            shape((3, SLOTS, ATOMS), f32),
            shape((1, ATOMS), f32),
        ],
    )(index, count, delta)
    near, far = [
        call(lambda *refs, start=start: onehot_kernel(*refs, start=start), shape((OFF_Y, PAIRS), bf16))(
            ids
        )
        for start in (0, OFF_Y)
    ]
    w0, slope, unit, radius, base = call(
        radial_kernel,
        [
            shape((C, PAIRS), bf16),
            shape((SLOTS, ATOMS), f32),
            shape((3, SLOTS, ATOMS), f32),
            shape((SLOTS, ATOMS), f32),
            shape((SLOTS, ATOMS), f32),
        ],
    )(alive, delta, decay)
    weights = [w0]
    for layer in (1, 2):
        body = lambda *refs, layer=layer: later_weights_kernel(*refs, layer=layer)
        weights.append(call(body, shape((C, PAIRS), bf16))(radius, base, decay))
    w0, w1, w2 = weights
    lists = (pick_y, pick_z, near, far)
    saved = []
    square, terms_shape = shape((C, ATOMS), f32), shape((C, PAIRS), bf16)

    def forward(ghosts, w):
        outs = [terms_shape, square]
        return call(forward_kernel, outs, input_output_aliases={2: 0})(*ghosts, most, far, w)

    ready = (((ids,), (w0, near)), ((), (w1,)), ((), (w2,)))
    for layer in range(2):
        ghosts = spread(proj, up, down, *lists, weights[layer], ready[layer])
        body = lambda *refs, layer=layer: layer_kernel(*refs, layer=layer)
        prod, total = forward(ghosts, weights[layer])
        features, t, proj, up, down = call(
            body,
            [
                shape((ATOMS, C), bf16),
                square,
                shape((ATOMS, C), bf16),
                shape((GX, C), bf16),
                shape((GX, C), bf16),
            ],
        )(total, features, self_weight, message_weight, pick_x)
        saved.append((t, prod))
    ghosts = spread(proj, up, down, *lists, w2, ready[2])
    ghost_shapes = [shape((GZ, C), bf16), shape((GZ, C), bf16)]
    radius_shape, kept_shape = shape((SLOTS, ATOMS), f32), shape((OFF_Z, C), f32)
    room = [pltpu.VMEM((C, PAIRS), bf16)]
    places = (place_y, place_z)

    def rest(pg, w):
        return lambda: call(rest_kernel, kept_shape, room)(pg, w, near, far)

    prod, total = forward(ghosts, w2)
    readout, gradient, pg, *back = call(top_kernel, [square, square, square, *ghost_shapes], room)(
        total, features, most, far, w2, self_weight, energy_proj, energy_row
    )
    sums = lambda *refs: sums_kernel(*refs, layer=2)
    radius_grad, energy = call(sums, [radius_shape, shape((1, ATOMS), f32)])(
        prod, pg, decay, slope, readout, energy_row
    )
    returned = retract(rest(pg, w2), *back, *places, [radius_grad])
    t, prod = saved[1]
    gradient, pg, *back = call(middle_kernel, [square, square, *ghost_shapes], room)(
        *returned, place_x, gradient, pg, self_weight, message_weight, t, w1, most, far
    )
    sums = lambda *refs: sums_kernel(*refs, layer=1)
    radius_grad = call(sums, radius_shape)(prod, pg, decay, slope, radius_grad)
    returned = retract(rest(pg, w1), *back, *places, [radius_grad])
    t, prod = saved[0]
    own_force, terms, *back = call(
        bottom_kernel,
        [shape((3, ATOMS), f32), shape((16, PAIRS), bf16), *ghost_shapes],
        [pltpu.VMEM((16, PAIRS), f32)],
    )(
        *returned, place_x, gradient, pg, self_weight, message_weight, t, prod, decay, slope,
        far, radius_grad, unit,
    )
    rest = lambda: call(force_rest_kernel, kept_shape)(terms, near, far)
    returned = retract(rest, *back, *places)
    forces = call(final_kernel, shape((3, ATOMS), f32))(*returned, place_x, own_force)
    return (energy.reshape(ATOMS), forces)


def solution(mesh):
    split = ("gx", "gy", "gz")
    return jax.shard_map(
        local,
        mesh=mesh,
        in_specs=(
            P(split),
            P(),
            P(split, None),
            P(split),
            P(None, split, None),
            P(None, split),
            P(None, split),
            P(None, split),
            P(),
            P(),
            P(),
            P(),
            P(),
        ),
        out_specs=(P(split), P(None, split)),
        check_vma=False,
    )
```

```python
import math

import jax
import jax.numpy as jnp
from jax import lax
from jax.experimental import pallas as pl
from jax.experimental.pallas import tpu as pltpu
from jax.sharding import PartitionSpec as P

cutoff = 4.0
ATOMS = 128
C = 128
SLOTS = 48
GX, GY, GZ = 32, 64, 64
LOADED = 13
OFF_X, OFF_Y, OFF_Z, ROWS = 128, 256, 384, 512
PAD = 64
UNPADDED = ATOMS + 2 * GX
PAIRS = ATOMS * SLOTS
CHUNK = 2 * ATOMS
TIERS = (20, 24, 28, SLOTS)
f32, bf16, i32 = jnp.float32, jnp.bfloat16, jnp.int32
NT = (((1,), (1,)), ((), ()))


def shape(dims, dtype):
    return jax.ShapeDtypeStruct(dims, dtype)


def call(body, outs, scratch=(), limit=4, **more):
    return pl.pallas_call(
        body,
        out_shape=outs,
        **more,
        scratch_shapes=list(scratch),
        compiler_params=pltpu.CompilerParams(vmem_limit_bytes=limit * 1024 * 1024),
    )


def along(axis, distance):
    size = lax.axis_size(axis)
    return [(i, (i + distance) % size) for i in range(size)]


def swap(to_higher, to_lower, axis):
    from_lower = lax.ppermute(to_higher, axis, along(axis, 1))
    from_higher = lax.ppermute(to_lower, axis, along(axis, -1))
    return from_lower, from_higher


def mm(a, b):
    return jnp.dot(a, b, preferred_element_type=f32)


def mm_nt(a, b):
    return lax.dot_general(a, b, NT, preferred_element_type=f32)


def split_nt(a, b):
    high = a.astype(bf16)
    low = (a - high.astype(f32)).astype(bf16)
    return mm_nt(b, high) + mm_nt(b, low)


def columns(row):
    return jnp.broadcast_to(row, (128, row.shape[1])).T


def padded(ids):
    return jnp.where(ids >= UNPADDED, ids + PAD, ids)


def picker(lists, extent):
    ids = jnp.concatenate([columns(lists[n : n + 1, :].astype(f32)) for n in range(2)], axis=0)
    parts = []
    for start in range(0, extent, 128):
        lane = (lax.broadcasted_iota(i32, ids.shape, 1) + start).astype(f32)
        parts.append(jnp.where(ids == lane, 1.0, 0.0).astype(bf16))
    return jnp.concatenate(parts, axis=1) if len(parts) > 1 else parts[0]


def place_into(out, lists):
    n = lists.shape[1]
    sub = lax.broadcasted_iota(i32, (out.shape[0], n), 0)
    for side in range(2):
        out[:, side * n : (side + 1) * n] = jnp.where(
            sub == lists[side : side + 1, :], 1.0, 0.0
        ).astype(bf16)


def for_slots(count, body):
    held = count[0, 0]
    below = -1.0
    for n in TIERS:
        pl.when((held > below) & (held <= n))(lambda n=n: body(n))
        below = float(n)


def first_kernel(*refs):
    inputs, refs = refs[:LOADED], refs[LOADED:]
    kept, refs = refs[: LOADED - 3], refs[LOADED - 3 :]
    feat, proj, up, down, pick_x, place_x, rows, types, table, send_x, sems = refs
    weight = kept[0]
    pairs = [(inputs[3].at[0], weight.at[0])]
    pairs += zip(inputs[:3], (types, table, send_x))
    pairs += [(inputs[3].at[1:], weight.at[1:])]
    pairs += zip(inputs[4:], kept[1:])
    moves = [pltpu.make_async_copy(a, b, sems.at[i]) for i, (a, b) in enumerate(pairs)]
    for move in moves:
        move.start()
    rows[...] = jnp.zeros_like(rows)
    for move in moves[:4]:
        move.wait()
    rows[0:6, :] = table[...].astype(f32)
    kinds = columns(types[...].astype(f32))
    lane = lax.broadcasted_iota(i32, (ATOMS, 128), 1).astype(f32)
    onehot = jnp.where(kinds == lane, 1.0, 0.0).astype(bf16)
    per_type = rows[...].astype(bf16)
    projected = mm(per_type, weight[0]).astype(bf16)
    pick = picker(send_x[...], ATOMS)
    chosen = mm(mm(pick, onehot).astype(bf16), projected).astype(bf16)
    up[...] = chosen[0:GX]
    down[...] = chosen[GX:]
    proj[...] = mm(onehot, projected).astype(bf16)
    feat[...] = mm(onehot, per_type).astype(bf16)
    pick_x[...] = pick
    place_into(place_x, send_x[...])
    for move in moves[4:]:
        move.wait()


def lists_kernel(
    send_y, send_z, energy_proj, energy_out,
    pick_y, pick_z, place_y, place_z, turned_proj, energy_columns,
):
    turned_proj[...] = turned(energy_proj[...])
    energy_columns[...] = columns(energy_out[...])
    ids_y, ids_z = send_y[...], padded(send_z[...])
    pick_y[...] = picker(ids_y, OFF_Y)
    pick_z[...] = picker(ids_z, OFF_Z)
    place_into(place_y, ids_y)
    place_into(place_z, ids_z)


def order_kernel(index, count, delta, ids_out, alive_out, delta_out, most):
    slot = lax.broadcasted_iota(i32, (SLOTS, ATOMS), 0)
    ids = padded(index[...])
    alive = slot < count[...]
    first = jnp.where(alive & (ids >= OFF_Z), 1.0, 0.0)
    rows = lax.broadcasted_iota(i32, (SLOTS, SLOTS), 0)
    columns_ = lax.broadcasted_iota(i32, (SLOTS, SLOTS), 1)
    earlier = jnp.where(columns_ < rows, 1.0, 0.0).astype(bf16)
    before = mm(earlier, first.astype(bf16))
    number = jnp.sum(first, axis=0, keepdims=True)
    place = jnp.where(first > 0.0, before, number + slot.astype(f32) - before)
    most[...] = jnp.broadcast_to(jnp.max(number, axis=1, keepdims=True), most.shape)
    coded = jnp.where(alive, ids, ids + 2 * ROWS).astype(f32)
    held = [coded, delta[0], delta[1], delta[2]]
    sorted_rows = [[], [], [], []]
    for k in range(SLOTS):
        here = place == float(k)
        for n in range(4):
            sorted_rows[n].append(jnp.sum(jnp.where(here, held[n], 0.0), axis=0, keepdims=True))
    coded, *moved = [jnp.concatenate(r, axis=0) for r in sorted_rows]
    live = coded < float(2 * ROWS)
    alive_out[...] = jnp.where(live, 1.0, 0.0)
    ids_out[...] = jnp.where(live, coded, coded - float(2 * ROWS)).astype(i32)
    for n in range(3):
        delta_out[n] = moved[n]


def onehot_kernel(index, onehot, *, start):
    ids = index[...]
    sub = lax.broadcasted_iota(i32, (OFF_Y, ATOMS), 0) + start
    for k in range(SLOTS):
        here = slice(k * ATOMS, (k + 1) * ATOMS)
        onehot[:, here] = jnp.where(sub == ids[k : k + 1, :], 1.0, 0.0).astype(bf16)


def weights_into(out, radius, base, decay_row):
    rate = columns(-decay_row)
    for k in range(SLOTS):
        here = slice(k * ATOMS, (k + 1) * ATOMS)
        out[:, here] = (base[k : k + 1, :] * jnp.exp(rate * radius[k : k + 1, :])).astype(bf16)


def radial_kernel(alive, delta, decay, w, slope, unit, radius_out, base_out):
    d = [delta[n] for n in range(3)]
    radius = jnp.sqrt(d[0] * d[0] + d[1] * d[1] + d[2] * d[2])
    half = (math.pi / (2.0 * cutoff)) * radius
    cosine, sine = jnp.cos(half), jnp.sin(half)
    base = alive[...] * (cosine * cosine) * (1.0 / math.sqrt(SLOTS)) / radius
    slope[...] = -(math.pi / cutoff) * sine / cosine - 1.0 / radius
    for n in range(3):
        unit[n] = d[n] / radius
    radius_out[...] = radius
    base_out[...] = base
    weights_into(w, radius, base, decay[0:1, :])


def later_weights_kernel(radius, base, decay, w, *, layer):
    weights_into(w, radius[...], base[...], decay[layer : layer + 1, :])


def pick_y_kernel(proj, lower, higher, pick, *refs):
    up, down, table = refs[-3:]
    table[0:ATOMS] = proj[...]
    table[OFF_X : OFF_X + GX] = lower[...]
    table[OFF_X + GX : OFF_X + 2 * GX] = higher[...]
    table[OFF_X + 2 * GX : OFF_Y] = jnp.zeros((PAD, C), bf16)
    chosen = mm(pick[...], table[...]).astype(bf16)
    up[...] = chosen[0:GY]
    down[...] = chosen[GY:]


def pick_z_kernel(proj, x_lower, x_higher, y_lower, y_higher, pick, *refs):
    up, down, table = refs[-3:]
    table[0:ATOMS] = proj[...]
    table[OFF_X : OFF_X + GX] = x_lower[...]
    table[OFF_X + GX : OFF_X + 2 * GX] = x_higher[...]
    table[OFF_X + 2 * GX : OFF_Y] = jnp.zeros((PAD, C), bf16)
    table[OFF_Y : OFF_Y + GY] = y_lower[...]
    table[OFF_Y + GY : OFF_Z] = y_higher[...]
    chosen = mm(pick[...], table[...]).astype(bf16)
    up[...] = chosen[0:GZ]
    down[...] = chosen[GZ:]


def turned(rows):
    return rows.astype(f32).T.astype(bf16)


def low_gather_kernel(
    proj, x_lower, x_higher, y_lower, y_higher, near, far, w, feat, self_weight,
    prod, total_out, turned_feat, table, *, layer,
):
    table[0:ATOMS] = proj[...]
    table[OFF_X : OFF_X + GX] = x_lower[...]
    table[OFF_X + GX : OFF_X + 2 * GX] = x_higher[...]
    table[OFF_X + 2 * GX : OFF_Y] = jnp.zeros((PAD, C), bf16)
    table[OFF_Y : OFF_Y + GY] = y_lower[...]
    table[OFF_Y + GY : OFF_Z] = y_higher[...]
    rows = turned(table[...])
    turned_feat[...] = feat[...].astype(f32).T
    total = mm(feat[...], self_weight[layer]).T
    for start in range(0, PAIRS, CHUNK):
        here = slice(start, start + CHUNK)
        gathered = mm(rows[:, 0:OFF_Y], near[:, here])
        gathered = gathered + mm(rows[:, OFF_Y:OFF_Z], far[0 : OFF_Z - OFF_Y, here])
        m = gathered.astype(bf16) * w[:, here]
        prod[:, here] = m
        total = total + (m[:, 0:ATOMS] + m[:, ATOMS:]).astype(f32)
    total_out[...] = total


def forward_kernel(z_lower, z_higher, low_prod, low_total, most, far, w, prod, total_out):
    rows = turned(jnp.concatenate([z_lower[...], z_higher[...]], axis=0))

    def add(n):
        total = low_total[...]
        for start in range(0, n * ATOMS, CHUNK):
            here = slice(start, start + CHUNK)
            m = mm(rows, far[OFF_Z - OFF_Y :, here]).astype(bf16) * w[:, here]
            prod[:, here] = low_prod[:, here] + m
            total = total + (m[:, 0:ATOMS] + m[:, ATOMS:]).astype(f32)
        total_out[...] = total

    for_slots(most, add)


def layer_kernel(
    total, feat, next_weight, pick_x,
    new_feat, tanh_out, new_proj, up, down, *, layer,
):
    t = jnp.tanh(total[...])
    tanh_out[...] = t
    features = (feat[...] + t).T.astype(bf16)
    new_feat[...] = features
    projected = mm(features, next_weight[layer + 1]).astype(bf16)
    new_proj[...] = projected
    chosen = mm(pick_x[...], projected).astype(bf16)
    up[...] = chosen[0:GX]
    down[...] = chosen[GX:]


def sum_rows(decay_row):
    high = decay_row.astype(bf16).astype(f32)
    rows = [jnp.ones_like(decay_row), high, decay_row - high, jnp.zeros((13, C), f32)]
    return jnp.concatenate(rows, axis=0).astype(bf16)


def backward_sums(prod, start, wide, rows, slope):
    s = mm(rows, prod[:, start : start + CHUNK] * wide)
    out = []
    for inner in range(0, CHUNK, ATOMS):
        k = (start + inner) // ATOMS
        here = slice(inner, inner + ATOMS)
        out.append(slope[k : k + 1, :] * s[0:1, here] - (s[1:2, here] + s[2:3, here]))
    return out


def wide_rows(x):
    return jnp.concatenate([x] * (CHUNK // ATOMS), axis=1)


def ghost_rows(rows, z_lower, z_higher):
    z_lower[...] = rows[0:GZ].astype(bf16)
    z_higher[...] = rows[GZ:].astype(bf16)


def mm_split(a, b):
    high = b.astype(bf16)
    low = (b - high.astype(f32)).astype(bf16)
    return mm(a, high) + mm(a, low)


def terms_into(terms, pg, w, n):
    wide = wide_rows(pg.astype(bf16))
    for start in range(0, n * ATOMS, CHUNK):
        here = slice(start, start + CHUNK)
        terms[:, here] = w[:, here] * wide


def terms_part(pg, w, most, far, terms, z_lower, z_higher):
    def add(n):
        terms_into(terms, pg, w, n)
        here = slice(0, n * ATOMS)
        ghost_rows(mm_nt(far[OFF_Z - OFF_Y :, here], terms[:, here]), z_lower, z_higher)

    for_slots(most, add)


def rest_kernel(pg, w, near, far, gradient, self_weight, kept, base, terms, *, layer):
    base[...] = gradient[...] + mm_split(self_weight[layer], pg[...])
    terms_into(terms, pg[...], w, SLOTS)
    kept[0:OFF_Y, :] = mm_nt(near[...], terms[...])
    kept[OFF_Y:OFF_Z, :] = mm_nt(far[0 : OFF_Z - OFF_Y, :], terms[...])


def force_rest_kernel(terms, near, far, kept):
    kept[...] = jnp.zeros_like(kept)
    n = terms.shape[0]
    kept[0:OFF_Y, 0:n] = mm_nt(near[...], terms[...])
    kept[OFF_Y:OFF_Z, 0:n] = mm_nt(far[0 : OFF_Z - OFF_Y, :], terms[...])


def sums_kernel(prod, pg, decay, slope, *refs, layer):
    wide, rows = wide_rows(pg[...].astype(bf16)), sum_rows(decay[layer : layer + 1, :])
    parts = []
    for start in range(0, PAIRS, CHUNK):
        parts += backward_sums(prod, start, wide, rows, slope)
    total = jnp.concatenate(parts, axis=0)
    if layer == 2:
        readout, energy_columns, radius_grad, energy = refs
        energy[...] = jnp.sum(readout[...] * energy_columns[...], axis=0, keepdims=True)
        radius_grad[...] = total
    else:
        before, radius_grad = refs
        radius_grad[...] = before[...] + total


def top_kernel(
    total, feat, most, far, w, turned_proj, energy_proj, energy_columns,
    readout_out, gradient_out, pg_out, z_lower, z_higher, terms,
):
    t = jnp.tanh(total[...])
    features = feat[...] + t
    readout = jnp.tanh(mm(turned_proj[...], features.astype(bf16)))
    readout_out[...] = readout
    upstream = (1.0 - readout * readout) * energy_columns[...]
    gradient = mm_split(energy_proj[...], upstream)
    pg = gradient * (1.0 - t * t)
    gradient_out[...] = gradient
    pg_out[...] = pg
    terms_part(pg, w, most, far, terms, z_lower, z_higher)


def return_z_kernel(kept, plus, minus, place, rest, y_lower, y_higher):
    pieces = jnp.concatenate([minus[...], plus[...]], axis=0)
    total = kept[...] + mm(place[...], pieces)
    rest[...] = total[0:UNPADDED]
    y_lower[...] = total[OFF_Y : OFF_Y + GY].astype(bf16)
    y_higher[...] = total[OFF_Y + GY : OFF_Z].astype(bf16)


def return_y_kernel(kept, plus, minus, place, *refs):
    own, x_lower, x_higher = refs[-3:]
    pieces = jnp.concatenate([minus[...], plus[...]], axis=0)
    total = kept[...] + mm(place[...], pieces)
    own[...] = total[0:ATOMS]
    x_lower[...] = total[OFF_X : OFF_X + GX].astype(bf16)
    x_higher[...] = total[OFF_X + GX :].astype(bf16)


def down_step(own, plus, minus, place, base, message_weight, layer):
    pieces = jnp.concatenate([minus[...], plus[...]], axis=0)
    row_sum = own[...] + mm(place[...], pieces)
    return base[...] + split_nt(row_sum, message_weight[layer])


def middle_kernel(
    own, plus, minus, place, base, message_weight, t, w, most, far,
    gradient_out, pg_out, z_lower, z_higher, terms,
):
    gradient = down_step(own, plus, minus, place, base, message_weight, 2)
    activation = t[...]
    pg = gradient * (1.0 - activation * activation)
    gradient_out[...] = gradient
    pg_out[...] = pg
    terms_part(pg, w, most, far, terms, z_lower, z_higher)


def bottom_kernel(
    own, plus, minus, place, base, message_weight,
    t, prod, decay, slope, far, radius_in, unit,
    own_force, terms, z_lower, z_higher, rows,
):
    gradient = down_step(own, plus, minus, place, base, message_weight, 1)
    activation = t[...]
    pg = gradient * (1.0 - activation * activation)
    wide, weighted = wide_rows(pg.astype(bf16)), sum_rows(decay[0:1, :])
    rows[...] = jnp.zeros_like(rows)
    sums = [jnp.zeros((1, ATOMS), f32)] * 3
    for start in range(0, PAIRS, CHUNK):
        for i, part in enumerate(backward_sums(prod, start, wide, weighted, slope)):
            k = start // ATOMS + i
            total = radius_in[k : k + 1, :] + part
            for n in range(3):
                pushed = total * unit[n, k : k + 1, :]
                sums[n] = sums[n] + pushed
                rows[n : n + 1, k * ATOMS : (k + 1) * ATOMS] = pushed
    terms[...] = rows[...].astype(bf16)
    ghosts = mm_nt(far[OFF_Z - OFF_Y :, :], terms[...])
    padding = jnp.zeros((2 * GZ, C - ghosts.shape[1]), f32)
    ghost_rows(jnp.concatenate([ghosts, padding], axis=1), z_lower, z_higher)
    for n in range(3):
        own_force[n : n + 1, :] = sums[n]


def final_kernel(own, plus, minus, place, own_force, forces):
    pieces = jnp.concatenate([minus[...], plus[...]], axis=0)
    row_sum = own[...] + mm(place[...], pieces)
    forces[...] = own_force[...] - row_sum.T[0:3, :]


def spread(proj, up, down, feat, pick_y, pick_z, near, far, w, self_weight, ready, layer):
    x = swap(up, down, "gx")
    sends = call(
        pick_y_kernel,
        [shape((GY, C), bf16)] * 2,
        [pltpu.VMEM((OFF_Y, C), bf16)],
    )(proj, *x, pick_y, *ready[0])
    y = swap(*sends, "gy")
    sends = call(
        pick_z_kernel,
        [shape((GZ, C), bf16)] * 2,
        [pltpu.VMEM((OFF_Z, C), bf16)],
    )(proj, *x, *y, pick_z, *ready[1])
    z = swap(*sends, "gz")
    low = call(
        lambda *refs: low_gather_kernel(*refs, layer=layer),
        [shape((C, PAIRS), bf16), shape((C, ATOMS), f32), shape((C, ATOMS), f32)],
        [pltpu.VMEM((OFF_Z, C), bf16)],
    )(proj, *x, *y, near, far, w, feat, self_weight)
    return (*z, *low)


def retract(kept, z_lower, z_higher, place_y, place_z, ready=()):
    arrived = swap(z_higher, z_lower, "gz")
    kept, y_lower, y_higher = call(
        return_z_kernel,
        [shape((UNPADDED, C), f32), shape((GY, C), bf16), shape((GY, C), bf16)],
    )(kept, *arrived, place_z)
    arrived = swap(y_higher, y_lower, "gy")
    own, x_lower, x_higher = call(
        return_y_kernel,
        [shape((ATOMS, C), f32), shape((GX, C), bf16), shape((GX, C), bf16)],
    )(kept, *arrived, place_y, *ready)
    arrived = swap(x_higher, x_lower, "gx")
    return (own, *arrived)


def local(
    atom_types,
    type_table,
    neighbor_index,
    neighbor_count,
    displacement,
    send_x,
    send_y,
    send_z,
    message_weight,
    self_weight,
    decay,
    energy_proj,
    energy_out,
):
    inputs = (
        atom_types.reshape(1, ATOMS),
        type_table,
        send_x,
        message_weight,
        send_y,
        send_z,
        neighbor_index.T,
        neighbor_count.reshape(1, ATOMS),
        jnp.swapaxes(displacement, 1, 2),
        decay,
        self_weight,
        energy_proj,
        energy_out.reshape(1, C),
    )
    inputs = [pltpu.with_memory_space_constraint(a, pltpu.HBM) for a in inputs]
    *loaded, features, proj, up, down, pick_x, place_x = call(
        first_kernel,
        [
            *[shape(a.shape, a.dtype) for a in inputs[3:]],
            shape((ATOMS, C), bf16),
            shape((ATOMS, C), bf16),
            shape((GX, C), bf16),
            shape((GX, C), bf16),
            shape((2 * GX, ATOMS), bf16),
            shape((ATOMS, 2 * GX), bf16),
        ],
        [
            pltpu.VMEM((128, C), f32),
            *[pltpu.VMEM(a.shape, a.dtype) for a in inputs[:3]],
            pltpu.SemaphoreType.DMA((LOADED + 1,)),
        ],
        in_specs=[pl.BlockSpec(memory_space=pltpu.HBM)] * LOADED,
    )(*inputs)
    message_weight, send_y, send_z, index, count, delta = loaded[:6]
    decay, self_weight, energy_proj, energy_row = loaded[6:]
    pick_y, pick_z, place_y, place_z, turned_proj, energy_columns = call(
        lists_kernel,
        [
            shape((2 * GY, OFF_Y), bf16),
            shape((2 * GZ, OFF_Z), bf16),
            shape((UNPADDED, 2 * GY), bf16),
            shape((OFF_Z, 2 * GZ), bf16),
            shape((C, C), bf16),
            shape((C, 128), f32),
        ],
    )(send_y, send_z, energy_proj, energy_row)
    ids, alive, delta, most = call(
        order_kernel,
        [
            shape((SLOTS, ATOMS), i32),
            shape((SLOTS, ATOMS), f32),
            shape((3, SLOTS, ATOMS), f32),
            shape((1, ATOMS), f32),
        ],
    )(index, count, delta)
    near, far = [
        call(lambda *refs, start=start: onehot_kernel(*refs, start=start), shape((OFF_Y, PAIRS), bf16))(
            ids
        )
        for start in (0, OFF_Y)
    ]
    w0, slope, unit, radius, base = call(
        radial_kernel,
        [
            shape((C, PAIRS), bf16),
            shape((SLOTS, ATOMS), f32),
            shape((3, SLOTS, ATOMS), f32),
            shape((SLOTS, ATOMS), f32),
            shape((SLOTS, ATOMS), f32),
        ],
    )(alive, delta, decay)
    weights = [w0]
    for layer in (1, 2):
        body = lambda *refs, layer=layer: later_weights_kernel(*refs, layer=layer)
        weights.append(call(body, shape((C, PAIRS), bf16))(radius, base, decay))
    w0, w1, w2 = weights
    lists = (pick_y, pick_z, near, far)
    saved = []
    square, terms_shape = shape((C, ATOMS), f32), shape((C, PAIRS), bf16)

    def forward(ghosts, w):
        outs = [terms_shape, square]
        return call(forward_kernel, outs, input_output_aliases={2: 0})(*ghosts, most, far, w)

    ready = (((ids,), (w0, near)), ((), (w1,)), ((), (w2,)))
    for layer in range(2):
        sends = (proj, up, down, features)
        *ghosts, turned_feat = spread(
            *sends, *lists, weights[layer], self_weight, ready[layer], layer
        )
        body = lambda *refs, layer=layer: layer_kernel(*refs, layer=layer)
        prod, total = forward(ghosts, weights[layer])
        features, t, proj, up, down = call(
            body,
            [
                shape((ATOMS, C), bf16),
                square,
                shape((ATOMS, C), bf16),
                shape((GX, C), bf16),
                shape((GX, C), bf16),
            ],
        )(total, turned_feat, message_weight, pick_x)
        saved.append((t, prod))
    *ghosts, turned_feat = spread(
        proj, up, down, features, *lists, w2, self_weight, ready[2], 2
    )
    ghost_shapes = [shape((GZ, C), bf16), shape((GZ, C), bf16)]
    radius_shape, kept_shape = shape((SLOTS, ATOMS), f32), shape((OFF_Z, C), f32)
    room = [pltpu.VMEM((C, PAIRS), bf16)]
    places = (place_y, place_z)

    def rest(pg, w, gradient, layer):
        body = lambda *refs: rest_kernel(*refs, layer=layer)
        return call(body, [kept_shape, square], room)(pg, w, near, far, gradient, self_weight)

    prod, total = forward(ghosts, w2)
    readout, gradient, pg, *back = call(top_kernel, [square, square, square, *ghost_shapes], room)(
        total, turned_feat, most, far, w2, turned_proj, energy_proj, energy_columns
    )
    sums = lambda *refs: sums_kernel(*refs, layer=2)
    radius_grad, energy = call(sums, [radius_shape, shape((1, ATOMS), f32)])(
        prod, pg, decay, slope, readout, energy_columns
    )
    kept, base = rest(pg, w2, gradient, 2)
    returned = retract(kept, *back, *places, [radius_grad])
    t, prod = saved[1]
    gradient, pg, *back = call(middle_kernel, [square, square, *ghost_shapes], room)(
        *returned, place_x, base, message_weight, t, w1, most, far
    )
    sums = lambda *refs: sums_kernel(*refs, layer=1)
    radius_grad = call(sums, radius_shape)(prod, pg, decay, slope, radius_grad)
    kept, base = rest(pg, w1, gradient, 1)
    returned = retract(kept, *back, *places, [radius_grad])
    t, prod = saved[0]
    own_force, terms, *back = call(
        bottom_kernel,
        [shape((3, ATOMS), f32), shape((16, PAIRS), bf16), *ghost_shapes],
        [pltpu.VMEM((16, PAIRS), f32)],
    )(
        *returned, place_x, base, message_weight, t, prod, decay, slope,
        far, radius_grad, unit,
    )
    kept = call(force_rest_kernel, kept_shape)(terms, near, far)
    returned = retract(kept, *back, *places)
    forces = call(final_kernel, shape((3, ATOMS), f32))(*returned, place_x, own_force)
    return (energy.reshape(ATOMS), forces)


def solution(mesh):
    split = ("gx", "gy", "gz")
    return jax.shard_map(
        local,
        mesh=mesh,
        in_specs=(
            P(split),
            P(),
            P(split, None),
            P(split),
            P(None, split, None),
            P(None, split),
            P(None, split),
            P(None, split),
            P(),
            P(),
            P(),
            P(),
            P(),
        ),
        out_specs=(P(split), P(None, split)),
        check_vma=False,
    )
```

```python
import math

import jax
import jax.numpy as jnp
from jax import lax
from jax.experimental import pallas as pl
from jax.experimental.pallas import tpu as pltpu
from jax.sharding import PartitionSpec as P

cutoff = 4.0
ATOMS = 128
C = 128
SLOTS = 48
GX, GY, GZ = 32, 64, 64
LOADED = 13
OFF_X, OFF_Y, OFF_Z, ROWS = 128, 256, 384, 512
PAD = 64
UNPADDED = ATOMS + 2 * GX
PAIRS = ATOMS * SLOTS
CHUNK = 2 * ATOMS
TIERS = (20, 24, 28, SLOTS)
f32, bf16, i32 = jnp.float32, jnp.bfloat16, jnp.int32
NT = (((1,), (1,)), ((), ()))


def shape(dims, dtype):
    return jax.ShapeDtypeStruct(dims, dtype)


def call(body, outs, scratch=(), limit=4, **more):
    return pl.pallas_call(
        body,
        out_shape=outs,
        **more,
        scratch_shapes=list(scratch),
        compiler_params=pltpu.CompilerParams(vmem_limit_bytes=limit * 1024 * 1024),
    )


def along(axis, distance):
    size = lax.axis_size(axis)
    return [(i, (i + distance) % size) for i in range(size)]


def swap(to_higher, to_lower, axis):
    from_lower = lax.ppermute(to_higher, axis, along(axis, 1))
    from_higher = lax.ppermute(to_lower, axis, along(axis, -1))
    return from_lower, from_higher


def mm(a, b):
    return jnp.dot(a, b, preferred_element_type=f32)


def mm_nt(a, b):
    return lax.dot_general(a, b, NT, preferred_element_type=f32)


def split_nt(a, b):
    high = a.astype(bf16)
    low = (a - high.astype(f32)).astype(bf16)
    return mm_nt(b, high) + mm_nt(b, low)


def columns(row):
    return jnp.broadcast_to(row, (128, row.shape[1])).T


def padded(ids):
    return jnp.where(ids >= UNPADDED, ids + PAD, ids)


def picker(lists, extent):
    ids = jnp.concatenate([columns(lists[n : n + 1, :].astype(f32)) for n in range(2)], axis=0)
    parts = []
    for start in range(0, extent, 128):
        lane = (lax.broadcasted_iota(i32, ids.shape, 1) + start).astype(f32)
        parts.append(jnp.where(ids == lane, 1.0, 0.0).astype(bf16))
    return jnp.concatenate(parts, axis=1) if len(parts) > 1 else parts[0]


def place_into(out, lists):
    n = lists.shape[1]
    sub = lax.broadcasted_iota(i32, (out.shape[0], n), 0)
    for side in range(2):
        out[:, side * n : (side + 1) * n] = jnp.where(
            sub == lists[side : side + 1, :], 1.0, 0.0
        ).astype(bf16)


def for_slots(count, body):
    held = count[0, 0]
    below = -1.0
    for n in TIERS:
        pl.when((held > below) & (held <= n))(lambda n=n: body(n))
        below = float(n)


def first_kernel(*refs):
    inputs, refs = refs[:LOADED], refs[LOADED:]
    kept, refs = refs[: LOADED - 3], refs[LOADED - 3 :]
    feat, proj, up, down, pick_x, place_x, rows, types, table, send_x, sems = refs
    weight = kept[0]
    pairs = [(inputs[3].at[0], weight.at[0])]
    pairs += zip(inputs[:3], (types, table, send_x))
    pairs += [(inputs[3].at[1:], weight.at[1:])]
    pairs += zip(inputs[4:], kept[1:])
    moves = [pltpu.make_async_copy(a, b, sems.at[i]) for i, (a, b) in enumerate(pairs)]
    for move in moves:
        move.start()
    rows[...] = jnp.zeros_like(rows)
    for move in moves[:4]:
        move.wait()
    rows[0:6, :] = table[...].astype(f32)
    kinds = columns(types[...].astype(f32))
    lane = lax.broadcasted_iota(i32, (ATOMS, 128), 1).astype(f32)
    onehot = jnp.where(kinds == lane, 1.0, 0.0).astype(bf16)
    per_type = rows[...].astype(bf16)
    projected = mm(per_type, weight[0]).astype(bf16)
    pick = picker(send_x[...], ATOMS)
    chosen = mm(mm(pick, onehot).astype(bf16), projected).astype(bf16)
    up[...] = chosen[0:GX]
    down[...] = chosen[GX:]
    proj[...] = mm(onehot, projected).astype(bf16)
    feat[...] = mm(onehot, per_type).astype(bf16)
    pick_x[...] = pick
    place_into(place_x, send_x[...])
    for move in moves[4:]:
        move.wait()


def lists_kernel(
    send_y, send_z, energy_proj, energy_out,
    pick_y, pick_z, place_y, place_z, turned_proj, energy_columns,
):
    turned_proj[...] = turned(energy_proj[...])
    energy_columns[...] = columns(energy_out[...])
    ids_y, ids_z = send_y[...], padded(send_z[...])
    pick_y[...] = picker(ids_y, OFF_Y)
    pick_z[...] = picker(ids_z, OFF_Z)
    place_into(place_y, ids_y)
    place_into(place_z, ids_z)


def order_kernel(index, count, delta, ids_out, alive_out, delta_out, most):
    slot = lax.broadcasted_iota(i32, (SLOTS, ATOMS), 0)
    ids = padded(index[...])
    alive = slot < count[...]
    first = jnp.where(alive & (ids >= OFF_Z), 1.0, 0.0)
    rows = lax.broadcasted_iota(i32, (SLOTS, SLOTS), 0)
    columns_ = lax.broadcasted_iota(i32, (SLOTS, SLOTS), 1)
    earlier = jnp.where(columns_ < rows, 1.0, 0.0).astype(bf16)
    before = mm(earlier, first.astype(bf16))
    number = jnp.sum(first, axis=0, keepdims=True)
    place = jnp.where(first > 0.0, before, number + slot.astype(f32) - before)
    most[...] = jnp.broadcast_to(jnp.max(number, axis=1, keepdims=True), most.shape)
    coded = jnp.where(alive, ids, ids + 2 * ROWS).astype(f32)
    held = [coded, delta[0], delta[1], delta[2]]
    sorted_rows = [[], [], [], []]
    for k in range(SLOTS):
        here = place == float(k)
        for n in range(4):
            sorted_rows[n].append(jnp.sum(jnp.where(here, held[n], 0.0), axis=0, keepdims=True))
    coded, *moved = [jnp.concatenate(r, axis=0) for r in sorted_rows]
    live = coded < float(2 * ROWS)
    alive_out[...] = jnp.where(live, 1.0, 0.0)
    ids_out[...] = jnp.where(live, coded, coded - float(2 * ROWS)).astype(i32)
    for n in range(3):
        delta_out[n] = moved[n]


def onehot_kernel(index, onehot, *, start):
    ids = index[...]
    sub = lax.broadcasted_iota(i32, (OFF_Y, ATOMS), 0) + start
    for k in range(SLOTS):
        here = slice(k * ATOMS, (k + 1) * ATOMS)
        onehot[:, here] = jnp.where(sub == ids[k : k + 1, :], 1.0, 0.0).astype(bf16)


def weights_into(out, radius, base, decay_row):
    rate = columns(-decay_row)
    for k in range(SLOTS):
        here = slice(k * ATOMS, (k + 1) * ATOMS)
        out[:, here] = (base[k : k + 1, :] * jnp.exp(rate * radius[k : k + 1, :])).astype(bf16)


def radial_kernel(alive, delta, decay, w, slope, unit, radius_out, base_out):
    d = [delta[n] for n in range(3)]
    radius = jnp.sqrt(d[0] * d[0] + d[1] * d[1] + d[2] * d[2])
    half = (math.pi / (2.0 * cutoff)) * radius
    cosine, sine = jnp.cos(half), jnp.sin(half)
    base = alive[...] * (cosine * cosine) * (1.0 / math.sqrt(SLOTS)) / radius
    slope[...] = -(math.pi / cutoff) * sine / cosine - 1.0 / radius
    for n in range(3):
        unit[n] = d[n] / radius
    radius_out[...] = radius
    base_out[...] = base
    weights_into(w, radius, base, decay[0:1, :])


def later_weights_kernel(radius, base, decay, w, *, layer):
    weights_into(w, radius[...], base[...], decay[layer : layer + 1, :])


def pick_y_kernel(proj, lower, higher, pick, *refs):
    up, down, table = refs[-3:]
    table[0:ATOMS] = proj[...]
    table[OFF_X : OFF_X + GX] = lower[...]
    table[OFF_X + GX : OFF_X + 2 * GX] = higher[...]
    table[OFF_X + 2 * GX : OFF_Y] = jnp.zeros((PAD, C), bf16)
    chosen = mm(pick[...], table[...]).astype(bf16)
    up[...] = chosen[0:GY]
    down[...] = chosen[GY:]


def pick_z_kernel(proj, x_lower, x_higher, y_lower, y_higher, pick, *refs):
    up, down, table = refs[-3:]
    table[0:ATOMS] = proj[...]
    table[OFF_X : OFF_X + GX] = x_lower[...]
    table[OFF_X + GX : OFF_X + 2 * GX] = x_higher[...]
    table[OFF_X + 2 * GX : OFF_Y] = jnp.zeros((PAD, C), bf16)
    table[OFF_Y : OFF_Y + GY] = y_lower[...]
    table[OFF_Y + GY : OFF_Z] = y_higher[...]
    chosen = mm(pick[...], table[...]).astype(bf16)
    up[...] = chosen[0:GZ]
    down[...] = chosen[GZ:]


def turned(rows):
    return rows.astype(f32).T.astype(bf16)


def low_gather_kernel(
    proj, x_lower, x_higher, y_lower, y_higher, near, far, w, feat, self_weight,
    prod, total_out, turned_feat, table, *, layer,
):
    table[0:ATOMS] = proj[...]
    table[OFF_X : OFF_X + GX] = x_lower[...]
    table[OFF_X + GX : OFF_X + 2 * GX] = x_higher[...]
    table[OFF_X + 2 * GX : OFF_Y] = jnp.zeros((PAD, C), bf16)
    table[OFF_Y : OFF_Y + GY] = y_lower[...]
    table[OFF_Y + GY : OFF_Z] = y_higher[...]
    rows = turned(table[...])
    turned_feat[...] = feat[...].astype(f32).T
    total = mm(feat[...], self_weight[layer]).T
    for start in range(0, PAIRS, CHUNK):
        here = slice(start, start + CHUNK)
        gathered = mm(rows[:, 0:OFF_Y], near[:, here])
        gathered = gathered + mm(rows[:, OFF_Y:OFF_Z], far[0 : OFF_Z - OFF_Y, here])
        m = gathered.astype(bf16) * w[:, here]
        prod[:, here] = m
        total = total + (m[:, 0:ATOMS] + m[:, ATOMS:]).astype(f32)
    total_out[...] = total


def forward_kernel(z_lower, z_higher, low_prod, low_total, most, far, w, prod, total_out):
    rows = turned(jnp.concatenate([z_lower[...], z_higher[...]], axis=0))

    def add(n):
        total = low_total[...]
        for start in range(0, n * ATOMS, CHUNK):
            here = slice(start, start + CHUNK)
            m = mm(rows, far[OFF_Z - OFF_Y :, here]).astype(bf16) * w[:, here]
            prod[:, here] = low_prod[:, here] + m
            total = total + (m[:, 0:ATOMS] + m[:, ATOMS:]).astype(f32)
        total_out[...] = total

    for_slots(most, add)


def layer_kernel(
    total, feat, next_weight, pick_x,
    new_feat, tanh_out, new_proj, up, down, *, layer,
):
    t = jnp.tanh(total[...])
    tanh_out[...] = t
    features = (feat[...] + t).T.astype(bf16)
    new_feat[...] = features
    projected = mm(features, next_weight[layer + 1]).astype(bf16)
    new_proj[...] = projected
    chosen = mm(pick_x[...], projected).astype(bf16)
    up[...] = chosen[0:GX]
    down[...] = chosen[GX:]


def sum_rows(decay_row):
    high = decay_row.astype(bf16).astype(f32)
    rows = [jnp.ones_like(decay_row), high, decay_row - high, jnp.zeros((13, C), f32)]
    return jnp.concatenate(rows, axis=0).astype(bf16)


def backward_sums(prod, start, wide, rows, slope):
    s = mm(rows, prod[:, start : start + CHUNK] * wide)
    out = []
    for inner in range(0, CHUNK, ATOMS):
        k = (start + inner) // ATOMS
        here = slice(inner, inner + ATOMS)
        out.append(slope[k : k + 1, :] * s[0:1, here] - (s[1:2, here] + s[2:3, here]))
    return out


def wide_rows(x):
    return jnp.concatenate([x] * (CHUNK // ATOMS), axis=1)


def ghost_rows(rows, z_lower, z_higher):
    z_lower[...] = rows[0:GZ].astype(bf16)
    z_higher[...] = rows[GZ:].astype(bf16)


def mm_split(a, b):
    high = b.astype(bf16)
    low = (b - high.astype(f32)).astype(bf16)
    return mm(a, high) + mm(a, low)


def terms_into(terms, pg, w, n):
    wide = wide_rows(pg.astype(bf16))
    for start in range(0, n * ATOMS, CHUNK):
        here = slice(start, start + CHUNK)
        terms[:, here] = w[:, here] * wide


def terms_part(pg, w, most, far, terms, z_lower, z_higher):
    def add(n):
        terms_into(terms, pg, w, n)
        here = slice(0, n * ATOMS)
        ghost_rows(mm_nt(far[OFF_Z - OFF_Y :, here], terms[:, here]), z_lower, z_higher)

    for_slots(most, add)


def rest_kernel(pg, w, near, far, gradient, self_weight, kept, base, terms, *, layer):
    base[...] = gradient[...] + mm_split(self_weight[layer], pg[...])
    terms_into(terms, pg[...], w, SLOTS)
    kept[0:OFF_Y, :] = mm_nt(near[...], terms[...])
    kept[OFF_Y:OFF_Z, :] = mm_nt(far[0 : OFF_Z - OFF_Y, :], terms[...])


def pushes_into(rows, n, pg, prod, decay, slope, radius_in, unit):
    wide, weighted = wide_rows(pg.astype(bf16)), sum_rows(decay[0:1, :])
    rows[...] = jnp.zeros_like(rows)
    sums = [jnp.zeros((1, ATOMS), f32)] * 3
    for start in range(0, n * ATOMS, CHUNK):
        for i, part in enumerate(backward_sums(prod, start, wide, weighted, slope)):
            k = start // ATOMS + i
            total = radius_in[k : k + 1, :] + part
            for axis in range(3):
                pushed = total * unit[axis, k : k + 1, :]
                sums[axis] = sums[axis] + pushed
                rows[axis : axis + 1, k * ATOMS : (k + 1) * ATOMS] = pushed
    return sums


def force_rest_kernel(pg, prod, decay, slope, radius_in, unit, near, far, kept, own_force, rows):
    sums = pushes_into(rows, SLOTS, pg[...], prod, decay, slope, radius_in, unit)
    for axis in range(3):
        own_force[axis : axis + 1, :] = sums[axis]
    terms = rows[...].astype(bf16)
    kept[...] = jnp.zeros_like(kept)
    n = terms.shape[0]
    kept[0:OFF_Y, 0:n] = mm_nt(near[...], terms)
    kept[OFF_Y:OFF_Z, 0:n] = mm_nt(far[0 : OFF_Z - OFF_Y, :], terms)


def sums_kernel(prod, pg, decay, slope, *refs, layer):
    wide, rows = wide_rows(pg[...].astype(bf16)), sum_rows(decay[layer : layer + 1, :])
    parts = []
    for start in range(0, PAIRS, CHUNK):
        parts += backward_sums(prod, start, wide, rows, slope)
    total = jnp.concatenate(parts, axis=0)
    if layer == 2:
        readout, energy_columns, radius_grad, energy = refs
        energy[...] = jnp.sum(readout[...] * energy_columns[...], axis=0, keepdims=True)
        radius_grad[...] = total
    else:
        before, radius_grad = refs
        radius_grad[...] = before[...] + total


def top_kernel(
    total, feat, most, far, w, turned_proj, energy_proj, energy_columns,
    readout_out, gradient_out, pg_out, z_lower, z_higher, terms,
):
    t = jnp.tanh(total[...])
    features = feat[...] + t
    readout = jnp.tanh(mm(turned_proj[...], features.astype(bf16)))
    readout_out[...] = readout
    upstream = (1.0 - readout * readout) * energy_columns[...]
    gradient = mm_split(energy_proj[...], upstream)
    pg = gradient * (1.0 - t * t)
    gradient_out[...] = gradient
    pg_out[...] = pg
    terms_part(pg, w, most, far, terms, z_lower, z_higher)


def return_z_kernel(kept, plus, minus, place, rest, y_lower, y_higher):
    pieces = jnp.concatenate([minus[...], plus[...]], axis=0)
    total = kept[...] + mm(place[...], pieces)
    rest[...] = total[0:UNPADDED]
    y_lower[...] = total[OFF_Y : OFF_Y + GY].astype(bf16)
    y_higher[...] = total[OFF_Y + GY : OFF_Z].astype(bf16)


def return_y_kernel(kept, plus, minus, place, *refs):
    own, x_lower, x_higher = refs[-3:]
    pieces = jnp.concatenate([minus[...], plus[...]], axis=0)
    total = kept[...] + mm(place[...], pieces)
    own[...] = total[0:ATOMS]
    x_lower[...] = total[OFF_X : OFF_X + GX].astype(bf16)
    x_higher[...] = total[OFF_X + GX :].astype(bf16)


def down_step(own, plus, minus, place, base, message_weight, layer):
    pieces = jnp.concatenate([minus[...], plus[...]], axis=0)
    row_sum = own[...] + mm(place[...], pieces)
    return base[...] + split_nt(row_sum, message_weight[layer])


def middle_kernel(
    own, plus, minus, place, base, message_weight, t, w, most, far,
    gradient_out, pg_out, z_lower, z_higher, terms,
):
    gradient = down_step(own, plus, minus, place, base, message_weight, 2)
    activation = t[...]
    pg = gradient * (1.0 - activation * activation)
    gradient_out[...] = gradient
    pg_out[...] = pg
    terms_part(pg, w, most, far, terms, z_lower, z_higher)


def bottom_kernel(
    own, plus, minus, place, base, message_weight,
    t, prod, decay, slope, most, far, radius_in, unit,
    pg_out, z_lower, z_higher, rows,
):
    gradient = down_step(own, plus, minus, place, base, message_weight, 1)
    activation = t[...]
    pg = gradient * (1.0 - activation * activation)
    pg_out[...] = pg
    z_lower[...] = jnp.zeros_like(z_lower)
    z_higher[...] = jnp.zeros_like(z_higher)

    def add(n):
        pushes_into(rows, n, pg, prod, decay, slope, radius_in, unit)
        here = slice(0, n * ATOMS)
        ghosts = mm_nt(far[OFF_Z - OFF_Y :, here], rows[:, here].astype(bf16)).astype(bf16)
        z_lower[:, 0 : rows.shape[0]] = ghosts[0:GZ]
        z_higher[:, 0 : rows.shape[0]] = ghosts[GZ:]

    for_slots(most, add)


def final_kernel(own, plus, minus, place, own_force, forces):
    pieces = jnp.concatenate([minus[...], plus[...]], axis=0)
    row_sum = own[...] + mm(place[...], pieces)
    forces[...] = own_force[...] - row_sum.T[0:3, :]


def spread(proj, up, down, feat, pick_y, pick_z, near, far, w, self_weight, ready, layer):
    x = swap(up, down, "gx")
    sends = call(
        pick_y_kernel,
        [shape((GY, C), bf16)] * 2,
        [pltpu.VMEM((OFF_Y, C), bf16)],
    )(proj, *x, pick_y, *ready[0])
    y = swap(*sends, "gy")
    sends = call(
        pick_z_kernel,
        [shape((GZ, C), bf16)] * 2,
        [pltpu.VMEM((OFF_Z, C), bf16)],
    )(proj, *x, *y, pick_z, *ready[1])
    z = swap(*sends, "gz")
    low = call(
        lambda *refs: low_gather_kernel(*refs, layer=layer),
        [shape((C, PAIRS), bf16), shape((C, ATOMS), f32), shape((C, ATOMS), f32)],
        [pltpu.VMEM((OFF_Z, C), bf16)],
    )(proj, *x, *y, near, far, w, feat, self_weight)
    return (*z, *low)


def retract(kept, z_lower, z_higher, place_y, place_z, ready=()):
    arrived = swap(z_higher, z_lower, "gz")
    kept, y_lower, y_higher = call(
        return_z_kernel,
        [shape((UNPADDED, C), f32), shape((GY, C), bf16), shape((GY, C), bf16)],
    )(kept, *arrived, place_z)
    arrived = swap(y_higher, y_lower, "gy")
    own, x_lower, x_higher = call(
        return_y_kernel,
        [shape((ATOMS, C), f32), shape((GX, C), bf16), shape((GX, C), bf16)],
    )(kept, *arrived, place_y, *ready)
    arrived = swap(x_higher, x_lower, "gx")
    return (own, *arrived)


def local(
    atom_types,
    type_table,
    neighbor_index,
    neighbor_count,
    displacement,
    send_x,
    send_y,
    send_z,
    message_weight,
    self_weight,
    decay,
    energy_proj,
    energy_out,
):
    inputs = (
        atom_types.reshape(1, ATOMS),
        type_table,
        send_x,
        message_weight,
        send_y,
        send_z,
        neighbor_index.T,
        neighbor_count.reshape(1, ATOMS),
        jnp.swapaxes(displacement, 1, 2),
        decay,
        self_weight,
        energy_proj,
        energy_out.reshape(1, C),
    )
    inputs = [pltpu.with_memory_space_constraint(a, pltpu.HBM) for a in inputs]
    *loaded, features, proj, up, down, pick_x, place_x = call(
        first_kernel,
        [
            *[shape(a.shape, a.dtype) for a in inputs[3:]],
            shape((ATOMS, C), bf16),
            shape((ATOMS, C), bf16),
            shape((GX, C), bf16),
            shape((GX, C), bf16),
            shape((2 * GX, ATOMS), bf16),
            shape((ATOMS, 2 * GX), bf16),
        ],
        [
            pltpu.VMEM((128, C), f32),
            *[pltpu.VMEM(a.shape, a.dtype) for a in inputs[:3]],
            pltpu.SemaphoreType.DMA((LOADED + 1,)),
        ],
        in_specs=[pl.BlockSpec(memory_space=pltpu.HBM)] * LOADED,
    )(*inputs)
    message_weight, send_y, send_z, index, count, delta = loaded[:6]
    decay, self_weight, energy_proj, energy_row = loaded[6:]
    pick_y, pick_z, place_y, place_z, turned_proj, energy_columns = call(
        lists_kernel,
        [
            shape((2 * GY, OFF_Y), bf16),
            shape((2 * GZ, OFF_Z), bf16),
            shape((UNPADDED, 2 * GY), bf16),
            shape((OFF_Z, 2 * GZ), bf16),
            shape((C, C), bf16),
            shape((C, 128), f32),
        ],
    )(send_y, send_z, energy_proj, energy_row)
    ids, alive, delta, most = call(
        order_kernel,
        [
            shape((SLOTS, ATOMS), i32),
            shape((SLOTS, ATOMS), f32),
            shape((3, SLOTS, ATOMS), f32),
            shape((1, ATOMS), f32),
        ],
    )(index, count, delta)
    near, far = [
        call(lambda *refs, start=start: onehot_kernel(*refs, start=start), shape((OFF_Y, PAIRS), bf16))(
            ids
        )
        for start in (0, OFF_Y)
    ]
    w0, slope, unit, radius, base = call(
        radial_kernel,
        [
            shape((C, PAIRS), bf16),
            shape((SLOTS, ATOMS), f32),
            shape((3, SLOTS, ATOMS), f32),
            shape((SLOTS, ATOMS), f32),
            shape((SLOTS, ATOMS), f32),
        ],
    )(alive, delta, decay)
    weights = [w0]
    for layer in (1, 2):
        body = lambda *refs, layer=layer: later_weights_kernel(*refs, layer=layer)
        weights.append(call(body, shape((C, PAIRS), bf16))(radius, base, decay))
    w0, w1, w2 = weights
    lists = (pick_y, pick_z, near, far)
    saved = []
    square, terms_shape = shape((C, ATOMS), f32), shape((C, PAIRS), bf16)

    def forward(ghosts, w):
        outs = [terms_shape, square]
        return call(forward_kernel, outs, input_output_aliases={2: 0})(*ghosts, most, far, w)

    ready = (((ids,), (w0, near)), ((), (w1,)), ((), (w2,)))
    for layer in range(2):
        sends = (proj, up, down, features)
        *ghosts, turned_feat = spread(
            *sends, *lists, weights[layer], self_weight, ready[layer], layer
        )
        body = lambda *refs, layer=layer: layer_kernel(*refs, layer=layer)
        prod, total = forward(ghosts, weights[layer])
        features, t, proj, up, down = call(
            body,
            [
                shape((ATOMS, C), bf16),
                square,
                shape((ATOMS, C), bf16),
                shape((GX, C), bf16),
                shape((GX, C), bf16),
            ],
        )(total, turned_feat, message_weight, pick_x)
        saved.append((t, prod))
    *ghosts, turned_feat = spread(
        proj, up, down, features, *lists, w2, self_weight, ready[2], 2
    )
    ghost_shapes = [shape((GZ, C), bf16), shape((GZ, C), bf16)]
    radius_shape, kept_shape = shape((SLOTS, ATOMS), f32), shape((OFF_Z, C), f32)
    room = [pltpu.VMEM((C, PAIRS), bf16)]
    places = (place_y, place_z)

    def rest(pg, w, gradient, layer):
        body = lambda *refs: rest_kernel(*refs, layer=layer)
        return call(body, [kept_shape, square], room)(pg, w, near, far, gradient, self_weight)

    prod, total = forward(ghosts, w2)
    readout, gradient, pg, *back = call(top_kernel, [square, square, square, *ghost_shapes], room)(
        total, turned_feat, most, far, w2, turned_proj, energy_proj, energy_columns
    )
    sums = lambda *refs: sums_kernel(*refs, layer=2)
    radius_grad, energy = call(sums, [radius_shape, shape((1, ATOMS), f32)])(
        prod, pg, decay, slope, readout, energy_columns
    )
    kept, base = rest(pg, w2, gradient, 2)
    returned = retract(kept, *back, *places, [radius_grad])
    t, prod = saved[1]
    gradient, pg, *back = call(middle_kernel, [square, square, *ghost_shapes], room)(
        *returned, place_x, base, message_weight, t, w1, most, far
    )
    sums = lambda *refs: sums_kernel(*refs, layer=1)
    radius_grad = call(sums, radius_shape)(prod, pg, decay, slope, radius_grad)
    kept, base = rest(pg, w1, gradient, 1)
    returned = retract(kept, *back, *places, [radius_grad])
    t, prod = saved[0]
    room = [pltpu.VMEM((16, PAIRS), f32)]
    pg, *back = call(bottom_kernel, [square, *ghost_shapes], room)(
        *returned, place_x, base, message_weight, t, prod, decay, slope, most, far, radius_grad, unit
    )
    kept, own_force = call(force_rest_kernel, [kept_shape, shape((3, ATOMS), f32)], room)(
        pg, prod, decay, slope, radius_grad, unit, near, far
    )
    returned = retract(kept, *back, *places)
    forces = call(final_kernel, shape((3, ATOMS), f32))(*returned, place_x, own_force)
    return (energy.reshape(ATOMS), forces)


def solution(mesh):
    split = ("gx", "gy", "gz")
    return jax.shard_map(
        local,
        mesh=mesh,
        in_specs=(
            P(split),
            P(),
            P(split, None),
            P(split),
            P(None, split, None),
            P(None, split),
            P(None, split),
            P(None, split),
            P(),
            P(),
            P(),
            P(),
            P(),
        ),
        out_specs=(P(split), P(None, split)),
        check_vma=False,
    )
```
